32 devices in a mesh: ctx: 8 (over z, y), section: 2 (over core), tp: 2 (over x).
Axes of the slice: x: 2, y: 2, z: 4, core: 2. Of those that a mesh axis runs over, the one named last changes fastest.
Arguments:
- residual: bfloat16 [2048, 3584], P('ctx', 'tp'), may hold values from -6 to 6
- queries: bfloat16 [2, 2048, 2048], P('section', 'ctx', 'tp'), may hold values from -5 to 5
- keys: bfloat16 [2, 2048, 512], P('section', 'ctx', 'tp'), may hold values from -5 to 5
- window_values: bfloat16 [2048, 512], P('ctx', 'tp'), may hold values from -6 to 6
- mixing: bfloat16 [2, 2048, 3584], P('section', 'tp'), may hold values from -0.125 to 0.125
- norm_gain: bfloat16 [3584], replicated, may hold values from 0.5 to 1.5
- log_decay: float32 [2048, 16], P('ctx', 'tp'), may hold values from -1 to 0
- spike_counts: int32 [2048, 2048], P('ctx', 'tp'), may hold values from 0 to 3
- thresholds: float32 [2048], P('tp'), may hold values from 0.5 to 2
- lengths: int32 [8], replicated, may hold values from 128 to 256, as said below
Outputs:
- head_outputs: bfloat16 [2, 2048, 2048], P('section', 'ctx', 'tp')
- hidden: bfloat16 [2048, 3584], P('ctx', 'tp')
The draws below stay inside these ranges and needn't reach their ends.
Inputs may be any that keep to these rules, and one draw needn't show every extreme that they name: `lengths`: the valid tokens of a shard come first; some shard is full in every draw.
All inputs are finite; a program needn't handle non-finite values.
Results may differ from the reference program's by a relative error of at most 0.015.
Values may be sent and summed in bfloat16 or wider, within the bound.
A program may use at most 128 MiB of HBM per device.

```python
import math
import jax
import jax.numpy as jnp
from jax import lax

D = 3584
KV_HEADS = 4
PROBE_BANDS = 16
HEAD = 128
WINDOW = 4096
TOK_DEV = 256
CONTEXT_EXTENT = 2048
SHARDS = 8
SECTIONS = 2
N_TP = 2


def draw_queries(key, part):
    shape = (SECTIONS, CONTEXT_EXTENT, PROBE_BANDS * HEAD)
    entries = jnp.clip(jax.random.normal(jax.random.fold_in(key, 1), shape, jnp.float32), -5.0, 5.0)
    return entries.astype(jnp.bfloat16)


def draw_keys(key, part):
    shape = (SECTIONS, CONTEXT_EXTENT, KV_HEADS * HEAD)
    entries = jnp.clip(jax.random.normal(jax.random.fold_in(key, 2), shape, jnp.float32), -5.0, 5.0)
    return entries.astype(jnp.bfloat16)


def draw_log_decay(key, part):
    slow_rate = -math.log(10.0) / CONTEXT_EXTENT * jax.random.uniform(jax.random.fold_in(key, 21), (PROBE_BANDS,), jnp.float32, 0.3, 1.0)
    fast_rate = -1.0 / jax.random.uniform(jax.random.fold_in(key, 22), (PROBE_BANDS,), jnp.float32, 30.0, 50.0)
    fast_share = 0.5
    picked = jax.random.uniform(jax.random.fold_in(key, 23), (PROBE_BANDS,)) < fast_share
    threshold_mark = jnp.where(picked, fast_rate, slow_rate)
    jitter_bias = jnp.exp(jax.random.uniform(jax.random.fold_in(key, 24), (CONTEXT_EXTENT, PROBE_BANDS), jnp.float32, -0.7, 0.7))
    pulse_train = jax.random.uniform(jax.random.fold_in(key, 25), (CONTEXT_EXTENT, PROBE_BANDS)) < 4.0 / CONTEXT_EXTENT
    pulse_train_height = jnp.log(jax.random.uniform(jax.random.fold_in(key, 26), (CONTEXT_EXTENT, PROBE_BANDS), jnp.float32, 0.5, 0.8))
    return jnp.where(pulse_train, pulse_train_height, threshold_mark[None, :] * jitter_bias).astype(jnp.float32)


def draw_lengths(key, part):
    drawn = jax.random.randint(jax.random.fold_in(key, 3), (SHARDS,), TOK_DEV // 2, TOK_DEV + 1)
    chosen = jax.random.randint(jax.random.fold_in(key, 4), (), 0, SHARDS)
    return jnp.where(jnp.arange(SHARDS) == chosen, TOK_DEV, drawn).astype(jnp.int32)


def place_ends(array, stream_key, least, top_value):
    extent = array.shape
    spot = [jax.random.randint(jax.random.fold_in(stream_key, axis), (), 0, extent[axis]) for axis in range(len(extent))]
    array = array.at[tuple(spot)].set(least)
    longest = extent.index(max(extent))
    spot[longest] = (spot[longest] + 1) % extent[longest]
    return array.at[tuple(spot)].set(top_value)


def levels(rng, extent, shards, least, top_value):
    def one(dim, shards_of):
        steps = jax.random.uniform(jax.random.fold_in(jax.random.fold_in(rng, 6), dim), (shards_of,), jnp.float32, least / len(shards), top_value / len(shards))
        return jnp.repeat(jnp.exp(steps), extent[dim] // shards_of).reshape((-1,) + (1,) * (len(extent) - dim - 1))

    gain = one(*shards[0])
    for cut in shards[1:]:
        gain = gain * one(*cut)
    return gain


def noise(key, shape, scale, most, shards=(), kind=jnp.bfloat16):
    factor_of = levels(key, shape, shards, -0.22, 0.18) if shards else 1.0
    values = jax.random.normal(key, shape, jnp.float32) * scale * factor_of
    return jnp.minimum(jnp.maximum(values, -most), most).astype(kind)


def setup_inputs(seed: int = 0) -> dict:
    seeds = jax.random.split(jax.random.key(seed), 11)
    return {
        "residual": noise(seeds[0], (CONTEXT_EXTENT, D), 1.0, 6.0, ((0, 8), (1, 2))),
        "queries": draw_queries(jax.random.fold_in(seeds[10], 71), 0),
        "keys": draw_keys(jax.random.fold_in(seeds[10], 71), 0),
        "window_values": noise(seeds[3], (CONTEXT_EXTENT, KV_HEADS * HEAD), 1.0, 6.0, ((0, 8), (1, 2))),
        "mixing": noise(seeds[4], (SECTIONS, PROBE_BANDS * HEAD, D), (PROBE_BANDS * HEAD) ** -0.5, 0.125, ((0, 2), (1, 2))),
        "norm_gain": jnp.clip(1.0 + 0.1 * jax.random.normal(seeds[5], (D,), jnp.float32), 0.5, 1.5).astype(jnp.bfloat16),
        "log_decay": draw_log_decay(jax.random.fold_in(seeds[10], 71), 0),
        "spike_counts": place_ends(jax.random.randint(seeds[7], (CONTEXT_EXTENT, PROBE_BANDS * HEAD), 0, 4), jax.random.fold_in(seeds[7], 1), 0, 3).astype(jnp.int32),
        "thresholds": jnp.clip(jnp.exp(math.log(2.0) - 1.3862944 * jax.random.uniform(seeds[8], (PROBE_BANDS * HEAD,), jnp.float32) ** levels(seeds[8], (PROBE_BANDS * HEAD,), ((0, 2),), -0.2, 0.2)), 0.5, 2.0),
        "lengths": draw_lengths(jax.random.fold_in(seeds[10], 71), 0),
    }


def reference(residual, queries, keys, window_values, mixing, norm_gain, log_decay, spike_counts, thresholds, lengths):
    group_size = PROBE_BANDS // KV_HEADS
    key_width = KV_HEADS * HEAD
    positions = jnp.arange(CONTEXT_EXTENT, dtype=jnp.int32)
    valid_rows = positions % TOK_DEV < lengths[positions // TOK_DEV]
    scale = 1.0 / math.sqrt(HEAD)
    padded_keys = jnp.concatenate([jnp.zeros((WINDOW, key_width), jnp.bfloat16), keys[0]], 0)
    padded_values = jnp.concatenate([jnp.zeros((WINDOW, key_width), jnp.bfloat16), window_values], 0)
    padded_valid = jnp.concatenate([jnp.arange(WINDOW, dtype=jnp.int32) < 0, valid_rows], 0)

    def window_block(block_index):
        start = (block_index * TOK_DEV).astype(jnp.int32)
        query_rows = lax.dynamic_slice_in_dim(queries[0], start, TOK_DEV, 0).astype(jnp.float32).reshape(TOK_DEV, KV_HEADS, group_size, HEAD)
        key_rows = lax.dynamic_slice_in_dim(padded_keys, start, WINDOW + TOK_DEV, 0).astype(jnp.float32).reshape(WINDOW + TOK_DEV, KV_HEADS, HEAD)
        value_rows = lax.dynamic_slice_in_dim(padded_values, start, WINDOW + TOK_DEV, 0).astype(jnp.float32).reshape(WINDOW + TOK_DEV, KV_HEADS, HEAD)
        key_valid = lax.dynamic_slice_in_dim(padded_valid, start, WINDOW + TOK_DEV, 0)
        scores = jnp.einsum('rgjd,kgd->gjrk', query_rows, key_rows) * scale
        distance = jnp.arange(TOK_DEV, dtype=jnp.int32)[:, None] + WINDOW - jnp.arange(WINDOW + TOK_DEV, dtype=jnp.int32)[None, :]
        allowed = key_valid[None, :] & (distance >= 0) & (distance < WINDOW)
        masked = jnp.where(allowed, scores, -1e+30)
        highest = lax.optimization_barrier(jnp.max(masked, axis=-1, keepdims=True))
        weights = jnp.where(allowed, jnp.exp(masked - highest), 0.0)
        totals = jnp.maximum(lax.optimization_barrier(jnp.sum(weights, axis=-1)), 1.0)
        rounded = lax.optimization_barrier(weights.astype(jnp.bfloat16)).astype(jnp.float32)
        blended = jnp.einsum('gjrk,kgd->gjrd', rounded, value_rows) / totals[..., None]
        blended = blended.transpose(2, 0, 1, 3).reshape(TOK_DEV, PROBE_BANDS * HEAD)
        row_valid = lax.dynamic_slice_in_dim(valid_rows, start, TOK_DEV, 0)
        return jnp.where(row_valid[:, None], blended, 0.0).astype(jnp.bfloat16)
    attention = lax.map(window_block, jnp.arange(SHARDS, dtype=jnp.int32)).reshape(CONTEXT_EXTENT, PROBE_BANDS * HEAD)
    width = PROBE_BANDS * HEAD // N_TP
    summed = residual.astype(jnp.float32)
    for member in range(N_TP):
        term = jnp.dot(attention[:, member * width:(member + 1) * width], mixing[0, member * width:(member + 1) * width], preferred_element_type=jnp.float32)
        summed = summed + lax.optimization_barrier(term.astype(jnp.bfloat16)).astype(jnp.float32)
    hidden = summed.astype(jnp.bfloat16)
    wide = hidden.astype(jnp.float32)
    normed = (wide * lax.rsqrt(lax.optimization_barrier(jnp.mean(wide * wide, axis=-1, keepdims=True)) + 1e-05) * norm_gain.astype(jnp.float32)).astype(jnp.bfloat16)
    payload_vectors = lax.dot_general(normed, mixing[1], (((1,), (1,)), ((), ())), preferred_element_type=jnp.float32).astype(jnp.bfloat16)
    decay_all = log_decay * valid_rows[:, None].astype(jnp.float32)
    masked_keys = jnp.where(valid_rows[:, None], keys[1], jnp.zeros_like(keys[1]))
    triangle = jnp.arange(TOK_DEV, dtype=jnp.int32)[:, None] >= jnp.arange(TOK_DEV, dtype=jnp.int32)[None, :]

    def linear_block(state, block_index):
        start = (block_index * TOK_DEV).astype(jnp.int32)
        query_rows = lax.dynamic_slice_in_dim(queries[1], start, TOK_DEV, 0).astype(jnp.float32).reshape(TOK_DEV, KV_HEADS, group_size, HEAD)
        key_rows = lax.dynamic_slice_in_dim(masked_keys, start, TOK_DEV, 0).astype(jnp.float32).reshape(TOK_DEV, KV_HEADS, HEAD)
        value_rows = lax.dynamic_slice_in_dim(payload_vectors, start, TOK_DEV, 0).astype(jnp.float32).reshape(TOK_DEV, KV_HEADS, group_size, HEAD)
        decays = lax.dynamic_slice_in_dim(decay_all, start, TOK_DEV, 0).reshape(TOK_DEV, KV_HEADS, group_size)
        cumulated = jnp.cumsum(decays, axis=0)
        block_total = cumulated[-1]
        inter = jnp.einsum('rgjd,gdje->rgje', query_rows, state, precision=lax.Precision.HIGHEST) * jnp.exp(cumulated)[..., None]
        products = jnp.einsum('rgjd,sgd->gjrs', query_rows, key_rows)
        ordered = cumulated.transpose(1, 2, 0)
        spread = ordered[..., :, None] - ordered[..., None, :]
        damping = jnp.where(triangle, jnp.exp(jnp.minimum(spread, 0.0)), 0.0)
        intra = jnp.einsum('gjrs,sgje->rgje', products * damping, value_rows, precision=lax.Precision.HIGHEST)
        fresh_state = jnp.einsum('sgd,sgje->gdje', key_rows, value_rows * jnp.exp(block_total - cumulated)[..., None], precision=lax.Precision.HIGHEST)
        state = state * jnp.exp(block_total)[:, None, :, None] + fresh_state
        return (state, inter + intra)
    start_state = jnp.zeros((KV_HEADS, HEAD, group_size, HEAD), jnp.float32)
    unused_state, linear_rows = lax.scan(linear_block, start_state, jnp.arange(SHARDS, dtype=jnp.int32))
    mixed = linear_rows.reshape(CONTEXT_EXTENT, PROBE_BANDS, HEAD)
    scaled = mixed * lax.rsqrt(lax.optimization_barrier(jnp.mean(mixed * mixed, axis=-1, keepdims=True)) + 1e-05)
    gating = spike_counts.astype(jnp.float32).reshape(CONTEXT_EXTENT, PROBE_BANDS, HEAD) * thresholds.reshape(PROBE_BANDS, HEAD)
    gated = jnp.where(valid_rows[:, None], (scaled * gating).reshape(CONTEXT_EXTENT, PROBE_BANDS * HEAD), 0.0).astype(jnp.bfloat16)
    return (jnp.stack([attention, gated], 0), hidden)
```

```python
import functools
import math

import jax
import jax.numpy as jnp
from jax import lax
from jax.experimental import pallas as pl
from jax.experimental.pallas import tpu as pltpu
from jax.sharding import PartitionSpec as P

HEAD = 128
WINDOW = 4096


def passed_along(x, axis, by):
    devices = lax.axis_size(axis)
    pairs = [(i, i + by) for i in range(devices) if 0 <= i + by < devices]
    return lax.ppermute(x, axis, pairs)


def entering(x, axis, join, neutral):
    place = lax.axis_index(axis)
    gathered = jax.tree.map(
        lambda a, kind: lax.all_gather(a.astype(kind), axis), x, (jnp.bfloat16, jnp.bfloat16)
    )
    state = jax.tree.map(lambda a, e: jnp.zeros_like(a) + jnp.asarray(e, a.dtype), x, neutral)

    def one(step, state):
        return join(
            state,
            jax.tree.map(
                lambda a, own: lax.dynamic_index_in_dim(a, step, 0, False).astype(own.dtype),
                gathered,
                x,
            ),
        )

    return lax.fori_loop(0, place, one, state)


def body(
    residual,
    queries,
    keys,
    window_values,
    mixing,
    norm_gain,
    log_decay,
    spike_counts,
    thresholds,
    lengths,
):
    section_index = lax.axis_index("section")
    shard_index = lax.axis_index("ctx")
    row_count = keys.shape[1]
    head_size = HEAD
    key_heads = keys.shape[2] // head_size
    query_head_rows = queries.shape[2] // head_size
    group_size = query_head_rows // key_heads
    span_blocks = WINDOW // row_count
    feature_count = mixing.shape[2]
    scale = 1.0 / math.sqrt(head_size)
    positions = jnp.arange(row_count, dtype=jnp.int32)
    valid_rows = positions < lengths[shard_index]
    own_keys = keys[0]
    earlier = [
        passed_along((own_keys, window_values), "ctx", distance + 1)
        for distance in range(span_blocks)
    ]
    key_blocks = jnp.stack([pair[0] for pair in earlier[::-1]] + [own_keys], 0)
    value_blocks = jnp.stack([pair[1] for pair in earlier[::-1]] + [window_values], 0)

    def window_layer(dummy_arg):
        query_rows = queries[0].reshape(row_count, key_heads, group_size, head_size)
        sources = shard_index - span_blocks + jnp.arange(span_blocks + 1, dtype=jnp.int32)
        block_valid = (sources[:, None] >= 0) & (
            positions[None, :] < lengths[jnp.clip(sources, 0, None)][:, None]
        )
        offsets = (span_blocks - jnp.arange(span_blocks + 1, dtype=jnp.int32)) * row_count
        base_distance = positions[:, None] - positions[None, :]

        def weight_step(carry, items):
            running, totals, best = carry
            scores = (
                jnp.einsum(
                    "rgjd,kgd->gjrk",
                    query_rows,
                    items[0].reshape(row_count, key_heads, head_size),
                    preferred_element_type=jnp.float32,
                )
                * scale
            )
            distance = base_distance + items[3]
            allowed = items[2][None, :] & (distance >= 0) & (distance < WINDOW)
            scores = jnp.where(allowed, scores, -1e30)
            new_best = jnp.maximum(best, jnp.max(scores, axis=-1))
            factor = jnp.exp(best - new_best)
            weights = jnp.where(allowed, jnp.exp(scores - new_best[..., None]), 0.0)
            blended = jnp.einsum(
                "gjrk,kgd->gjrd",
                weights.astype(jnp.bfloat16),
                items[1].reshape(row_count, key_heads, head_size),
                preferred_element_type=jnp.float32,
            )
            return (
                (
                    running * factor[..., None] + blended,
                    totals * factor + jnp.sum(weights, axis=-1),
                    new_best,
                ),
                None,
            )

        start_sums = (
            jnp.zeros((key_heads, group_size, row_count, head_size), jnp.float32),
            jnp.zeros((key_heads, group_size, row_count), jnp.float32),
            jnp.full((key_heads, group_size, row_count), -1e30, jnp.float32),
        )
        (blended, totals, unused_best), unused_sum = lax.scan(
            weight_step, start_sums, (key_blocks, value_blocks, block_valid, offsets)
        )
        attention = blended / jnp.maximum(totals, 1.0)[..., None]
        attention = attention.transpose(2, 0, 1, 3).reshape(row_count, query_head_rows * head_size)
        attention = jnp.where(valid_rows[:, None], attention, 0.0).astype(jnp.bfloat16)
        projected = jnp.dot(attention, mixing[0], preferred_element_type=jnp.float32)
        return (attention, projected)

    def window_skip(dummy_arg):
        return (
            jnp.zeros((row_count, query_head_rows * head_size), jnp.bfloat16),
            jnp.zeros((row_count, feature_count), jnp.float32),
        )

    attention, projected = lax.cond(section_index == 0, window_layer, window_skip, 0)
    share = lax.psum_scatter(
        projected.astype(jnp.bfloat16), "tp", scatter_dimension=1, tiled=True
    ).astype(jnp.float32)
    own_hidden = (share + residual.astype(jnp.float32)).astype(jnp.bfloat16)
    moved_share = passed_along(own_hidden, "section", 1)
    local_activations = jnp.where(section_index == 0, own_hidden, moved_share)
    complete_hidden_matrix = lax.all_gather(local_activations, "tp", axis=1, tiled=True)
    masked_keys = jnp.where(valid_rows[:, None], own_keys, jnp.zeros_like(own_keys)).reshape(
        row_count, key_heads, head_size
    )
    wide_keys = masked_keys.astype(jnp.float32)
    decays = log_decay * valid_rows[:, None].astype(jnp.float32)

    def linear_prepare(dummy_arg):
        wide = complete_hidden_matrix.astype(jnp.float32)
        normed = (
            wide
            * lax.rsqrt(jnp.mean(wide * wide, axis=-1, keepdims=True) + 1e-05)
            * norm_gain.astype(jnp.float32)
        ).astype(jnp.bfloat16)
        payload_vectors = lax.dot_general(
            normed, mixing[0], (((1,), (1,)), ((), ())), preferred_element_type=jnp.float32
        ).astype(jnp.bfloat16)
        cumulated = jnp.cumsum(decays, axis=0).reshape(row_count, key_heads, group_size)
        value_rows = payload_vectors.astype(jnp.float32).reshape(
            row_count, key_heads, group_size, head_size
        )
        fresh_state = jnp.einsum(
            "sgd,sgje->gdje",
            wide_keys,
            value_rows * jnp.exp(cumulated[-1] - cumulated)[..., None],
            precision=lax.Precision.HIGHEST,
        )
        return (payload_vectors, cumulated, fresh_state)

    def linear_skip(dummy_arg):
        return (
            jnp.zeros((row_count, query_head_rows * head_size), jnp.bfloat16),
            jnp.zeros((row_count, key_heads, group_size), jnp.float32),
            jnp.zeros((key_heads, head_size, group_size, head_size), jnp.float32),
        )

    payload_vectors, cumulated, fresh_state = lax.cond(
        section_index == 1, linear_prepare, linear_skip, 0
    )

    def chain(previous_entry, latter):
        return (
            previous_entry[0] + latter[0],
            previous_entry[1] * jnp.exp(latter[0])[:, None, :, None] + latter[1],
        )

    identity = (jnp.zeros((key_heads, group_size), jnp.float32), jnp.zeros_like(fresh_state))
    unused_total, incoming = entering((cumulated[-1], fresh_state), "ctx", chain, identity)

    def linear_finish(dummy_arg):
        query_narrow = queries[0].reshape(row_count, key_heads, group_size, head_size)
        query_rows = query_narrow.astype(jnp.float32)
        value_rows = payload_vectors.astype(jnp.float32).reshape(
            row_count, key_heads, group_size, head_size
        )
        inter = (
            jnp.einsum("rgjd,gdje->rgje", query_rows, incoming, precision=lax.Precision.HIGHEST)
            * jnp.exp(cumulated)[..., None]
        )
        products = jnp.einsum(
            "rgjd,sgd->gjrs", query_narrow, masked_keys, preferred_element_type=jnp.float32
        )
        ordered = cumulated.transpose(1, 2, 0)
        spread = ordered[..., :, None] - ordered[..., None, :]
        triangle = positions[:, None] >= positions[None, :]
        damping = jnp.where(triangle, jnp.exp(jnp.minimum(spread, 0.0)), 0.0)
        intra = jnp.einsum(
            "gjrs,sgje->rgje", products * damping, value_rows, precision=lax.Precision.HIGHEST
        )
        mixed = (inter + intra).reshape(row_count, query_head_rows, head_size)
        scaled = mixed * lax.rsqrt(jnp.mean(mixed * mixed, axis=-1, keepdims=True) + 1e-05)
        gating = spike_counts.astype(jnp.float32).reshape(
            row_count, query_head_rows, head_size
        ) * thresholds.reshape(query_head_rows, head_size)
        return jnp.where(
            valid_rows[:, None],
            (scaled * gating).reshape(row_count, query_head_rows * head_size),
            0.0,
        ).astype(jnp.bfloat16)

    def finish_skip(dummy_arg):
        return jnp.zeros((row_count, query_head_rows * head_size), jnp.bfloat16)

    gated = lax.cond(section_index == 1, linear_finish, finish_skip, 0)
    head_outputs = jnp.where(section_index == 0, attention, gated)[None]
    return (head_outputs, local_activations)


MESH = pl.DeviceIdType.MESH
F32 = jnp.float32
BF16 = jnp.bfloat16
CHUNK = 256
PAD = 16


def nt(a, b):
    return lax.dot_general(a, b, (((1,), (1,)), ((), ())), preferred_element_type=F32)


def nn(a, b):
    return jnp.dot(a, b, preferred_element_type=F32)


def turned(x):
    return jnp.transpose(x.astype(F32)).astype(BF16)


def kernel(
    n,
    residual,
    queries,
    keys,
    window_values,
    mixing,
    gain,
    decay,
    decay_t,
    spikes,
    thresholds,
    lengths,
    head_out,
    hidden_out,
    weights,
    spike_buf,
    kv,
    moved_queries,
    stacked,
    top,
    total,
    blend,
    attention,
    terms,
    own_terms,
    far_terms,
    residuals,
    hidden_buf,
    values_sum,
    square_sum,
    damped,
    faded,
    rest,
    keys_t,
    values,
    states,
    incoming,
    passed,
    mixed,
    weights_sem,
    spike_sem,
    res_sem,
    first_sem,
    first_recv,
    kv_send,
    kv_recv,
    kv_forward,
    att_sem,
    term_own_send,
    term_far_send,
    term_own_recv,
    term_far_recv,
    hid_send,
    hid_recv,
    state_send,
    state_recv,
    state_forward,
):
    c = lax.axis_index("ctx")
    s = lax.axis_index("section")
    p = lax.axis_index("tp")
    odd = c % 2
    step_to = 1 - 2 * odd
    partner = c + step_to
    rows = keys.shape[0]
    half = residual.shape[1]
    chunks_half = half // CHUNK
    chunks = 2 * chunks_half
    group = 4
    wide = group * HEAD
    factor = math.log2(math.e) / math.sqrt(HEAD)

    barrier = pltpu.get_barrier_semaphore()
    pl.semaphore_signal(barrier, inc=1, device_id={"section": 1 - s}, device_id_type=MESH)
    pl.semaphore_signal(barrier, inc=1, device_id={"tp": 1 - p}, device_id_type=MESH)
    pl.semaphore_signal(
        barrier, inc=1, device_id={"section": 1 - s, "tp": 1 - p}, device_id_type=MESH
    )
    pl.semaphore_signal(barrier, inc=1, device_id={"ctx": partner}, device_id_type=MESH)
    for k in range(1, n // 2):
        pl.semaphore_signal(
            barrier, inc=1, device_id={"ctx": (c + 2 * k) % n}, device_id_type=MESH
        )

    weights_copy = pltpu.make_async_copy(mixing, weights, weights_sem)
    weights_copy.start()

    own_len = lengths[c]

    @pl.when(s == 0)
    def _():
        kv[0, 0:rows] = keys[:, 0:HEAD]
        value_t = turned(window_values[:, 0:HEAD])
        kv[0, rows : rows + HEAD] = value_t[:, 0:HEAD]
        kv[0, rows + HEAD : rows + 2 * HEAD] = value_t[:, HEAD : 2 * HEAD]
        for h in range(group):
            stacked[h * rows : (h + 1) * rows, :] = queries[:, h * HEAD : (h + 1) * HEAD]

    @pl.when(s == 1)
    def _():
        value_t = turned(window_values[:, HEAD : 2 * HEAD])
        kv[0, rows : rows + HEAD] = value_t[:, 0:HEAD]
        kv[0, rows + HEAD : rows + 2 * HEAD] = value_t[:, HEAD : 2 * HEAD]

    pl.semaphore_wait(barrier, 3 + n // 2)

    key_copy = pltpu.make_async_remote_copy(
        src_ref=keys.at[:, HEAD : 2 * HEAD],
        dst_ref=kv.at[0, 0:rows],
        send_sem=first_sem.at[0],
        recv_sem=first_recv.at[0],
        device_id={"section": 1 - s},
        device_id_type=MESH,
    )
    query_copy = pltpu.make_async_remote_copy(
        src_ref=queries.at[:, wide : 2 * wide],
        dst_ref=moved_queries,
        send_sem=first_sem.at[1],
        recv_sem=first_recv.at[1],
        device_id={"section": 1 - s},
        device_id_type=MESH,
    )
    residual_send = pltpu.make_async_remote_copy(
        src_ref=residual,
        dst_ref=residuals.at[p],
        send_sem=res_sem.at[0],
        recv_sem=res_sem.at[1],
        device_id={"tp": 1 - p},
        device_id_type=MESH,
    )
    residual_recv = pltpu.make_async_remote_copy(
        src_ref=residual,
        dst_ref=residuals.at[1 - p],
        send_sem=res_sem.at[0],
        recv_sem=res_sem.at[1],
        device_id={"tp": 1 - p},
        device_id_type=MESH,
    )
    residual_copy = pltpu.make_async_copy(residual, residuals.at[p], res_sem.at[2])
    spike_copy = pltpu.make_async_copy(spikes, spike_buf, spike_sem)

    @pl.when(s == 0)
    def _():
        key_copy.start()
        query_copy.start()

    @pl.when(s == 1)
    def _():
        residual_send.start()
        residual_copy.start()
        spike_copy.start()
        key_copy.wait_recv()

    def direct(buf, send, recv, k):
        return pltpu.make_async_remote_copy(
            src_ref=buf.at[0],
            dst_ref=buf.at[2 * k],
            send_sem=send.at[k],
            recv_sem=recv.at[2 * k],
            device_id={"ctx": lax.rem(c + 2 * k, n)},
            device_id_type=MESH,
        )

    def forward(buf, send, recv, k):
        return pltpu.make_async_remote_copy(
            src_ref=buf.at[2 * k],
            dst_ref=buf.at[2 * k + step_to],
            send_sem=send.at[k],
            recv_sem=recv.at[2 * k + step_to],
            device_id={"ctx": partner},
            device_id_type=MESH,
        )

    def arrival(buf, send, recv, slot):
        return pltpu.make_async_remote_copy(
            src_ref=buf.at[slot],
            dst_ref=buf.at[slot],
            send_sem=send.at[0],
            recv_sem=recv.at[slot],
            device_id={"ctx": partner},
            device_id_type=MESH,
        )

    later = (n - 1 - c) // 2
    before = c // 2

    def send_own(buf, send, forward_sem, recv):
        @pl.when(odd == 0)
        def _():
            forward(buf, forward_sem, recv, 0).start()

        def one(k, carry):
            direct(buf, send, recv, k).start()
            return carry

        lax.fori_loop(1, later + 1, one, 0)

    def sent_own(buf, send, forward_sem, recv):
        @pl.when(odd == 0)
        def _():
            forward(buf, forward_sem, recv, 0).wait_send()

        def one(k, carry):
            direct(buf, send, recv, k).wait_send()
            return carry

        lax.fori_loop(1, later + 1, one, 0)

        def two(k, carry):
            forward(buf, forward_sem, recv, k).wait_send()
            return carry

        lax.fori_loop(1, before + 1, two, 0)

    send_own(kv, kv_send, kv_forward, kv_recv)

    @pl.when(s == 1)
    def _():
        query_copy.wait_recv()
        for h in range(group):
            stacked[h * rows : (h + 1) * rows, :] = moved_queries[:, h * HEAD : (h + 1) * HEAD]

    def attend(slot, first):
        key_rows = kv[slot, 0:rows]
        value_t = jnp.concatenate(
            [kv[slot, rows : rows + HEAD], kv[slot, rows + HEAD : rows + 2 * HEAD]], axis=1
        )
        key_index = lax.broadcasted_iota(jnp.int32, (rows, rows), 0)
        allowed = key_index < lengths[c - slot]
        if first:
            allowed = allowed & (key_index <= lax.broadcasted_iota(jnp.int32, (rows, rows), 1))
        for h in range(group):
            at = slice(h * rows, (h + 1) * rows)
            scores = jnp.where(allowed, nt(key_rows, stacked[at, :]), -1e30)
            best = jnp.max(scores, axis=0, keepdims=True)
            if not first:
                best = jnp.maximum(best, top[:, at])
            part = jnp.exp2((scores - best) * factor)
            part_sum = jnp.sum(part, axis=0, keepdims=True)
            blended = nn(value_t, part.astype(BF16))
            if first:
                total[:, at] = part_sum
                blend[:, at] = blended
            else:
                shrink = jnp.exp2((top[:, at] - best) * factor)
                total[:, at] = total[:, at] * shrink + part_sum
                blend[:, at] = blend[:, at] * shrink + blended
            top[:, at] = best

    attend(0, True)

    def attend_pair(k, carry):
        arrival(kv, kv_send, kv_recv, 2 * k).wait_recv()
        forward(kv, kv_forward, kv_recv, k).start()
        attend(2 * k, False)
        arrival(kv, kv_send, kv_recv, 2 * k - 1).wait_recv()
        attend(2 * k - 1, False)
        return carry

    lax.fori_loop(1, before + 1, attend_pair, 0)

    @pl.when(odd == 1)
    def _():
        arrival(kv, kv_send, kv_recv, c).wait_recv()
        attend(c, False)

    row_lane = lax.broadcasted_iota(jnp.int32, (1, rows), 1)
    for h in range(group):
        at = slice(h * rows, (h + 1) * rows)
        scaled = blend[:, at] / jnp.maximum(total[:, at], 1.0)
        scaled = jnp.where(row_lane < own_len, scaled, 0.0)
        attention[s, :, h * HEAD : (h + 1) * HEAD] = jnp.transpose(scaled).astype(BF16)

    att_copy = pltpu.make_async_remote_copy(
        src_ref=attention.at[1],
        dst_ref=attention.at[1],
        send_sem=att_sem.at[0],
        recv_sem=att_sem.at[1],
        device_id={"section": 1 - s},
        device_id_type=MESH,
    )

    def term_own(j):
        return pltpu.make_async_remote_copy(
            src_ref=terms.at[j],
            dst_ref=own_terms.at[j],
            send_sem=term_own_send.at[j],
            recv_sem=term_own_recv.at[j],
            device_id={"section": 1 - s},
            device_id_type=MESH,
        )

    def term_far(j):
        return pltpu.make_async_remote_copy(
            src_ref=terms.at[j],
            dst_ref=far_terms.at[j],
            send_sem=term_far_send.at[j],
            recv_sem=term_far_recv.at[j],
            device_id={"section": 1 - s, "tp": 1 - p},
            device_id_type=MESH,
        )

    def hid(j):
        return pltpu.make_async_remote_copy(
            src_ref=hidden_buf.at[j],
            dst_ref=hidden_out.at[:, pl.ds(pl.multiple_of(j * CHUNK, CHUNK), CHUNK)],
            send_sem=hid_send.at[j],
            recv_sem=hid_recv.at[j],
            device_id={"section": 1 - s},
            device_id_type=MESH,
        )

    def each(count, act):
        def one(j, carry):
            act(j)
            return carry

        lax.fori_loop(0, count, one, 0)

    @pl.when(s == 0)
    def _():
        weights_copy.wait()
        att_copy.wait_recv()

        def project(j, carry):
            at = pl.ds(pl.multiple_of(j * CHUNK, CHUNK), CHUNK)
            both = jnp.concatenate([attention[0], attention[1]], axis=1)
            terms[j] = nn(both, weights[:, at]).astype(BF16)
            term_far(j).start()
            term_own(j).start()
            return carry

        lax.fori_loop(0, chunks, project, 0)
        head_out[:, 0:wide] = attention[0]
        head_out[:, wide : 2 * wide] = attention[1]
        each(chunks, lambda j: term_far(j).wait_send())
        each(chunks, lambda j: term_own(j).wait_send())
        key_copy.wait_send()
        query_copy.wait_send()
        each(chunks_half, lambda j: hid(j).wait_recv())

    @pl.when(s == 1)
    def _():
        att_copy.start()
        heads = 2 * group
        row_col = lax.broadcasted_iota(jnp.int32, (rows, 1), 0)
        valid_col = row_col < own_len
        r = lax.broadcasted_iota(jnp.int32, (rows, rows), 0)
        t = lax.broadcasted_iota(jnp.int32, (rows, rows), 1)
        lower = jnp.where(r >= t, 1.0, 0.0)
        upper = jnp.where(r <= t, 1.0, 0.0)
        cum = jnp.dot(
            lower,
            jnp.where(valid_col, decay[...], 0.0),
            precision=lax.Precision.HIGHEST,
            preferred_element_type=F32,
        )
        cum_t = jnp.dot(
            jnp.where(row_lane < own_len, decay_t[...], 0.0),
            upper,
            precision=lax.Precision.HIGHEST,
            preferred_element_type=F32,
        )
        last = cum[rows - 1 : rows, :]
        rest[...] = jnp.exp(last - cum)
        for g in range(2):
            masked = jnp.where(valid_col, keys[:, g * HEAD : (g + 1) * HEAD].astype(F32), 0.0)
            keys_t[g] = jnp.transpose(masked).astype(BF16)
        for h in range(heads):
            at = slice(h * HEAD, (h + 1) * HEAD)
            col = cum[:, h : h + 1]
            row = cum_t[h : h + 1, :]
            query = queries[:, at]
            damping = jnp.where(r >= t, jnp.exp(jnp.minimum(col - row, 0.0)), 0.0)
            damped[h] = (nn(query, keys_t[h // group]) * damping).astype(BF16)
            faded[:, at] = (query.astype(F32) * jnp.exp(col)).astype(BF16)
            sum_row = jnp.broadcast_to(last[:, h : h + 1], (PAD, HEAD))
            high = sum_row.astype(BF16)
            low = (sum_row - high.astype(F32)).astype(BF16)
            states[0, HEAD : HEAD + PAD, at] = high
            states[0, HEAD + PAD : HEAD + 2 * PAD, at] = low
        values_sum[...] = jnp.zeros_like(values_sum)
        square_sum[...] = jnp.zeros_like(square_sum)
        weights_copy.wait()
        residual_copy.wait()
        residual_recv.wait_recv()

        def collect(j, carry):
            side = j // chunks_half
            col = j - side * chunks_half
            here = pl.ds(pl.multiple_of(col * CHUNK, CHUNK), CHUNK)
            at = pl.ds(pl.multiple_of(j * CHUNK, CHUNK), CHUNK)
            term_own(j).wait_recv()
            term_far(j).wait_recv()
            summed = residuals[side, :, here].astype(F32) + (
                own_terms[j].astype(F32) + far_terms[j].astype(F32)
            )
            narrow = summed.astype(BF16)

            @pl.when(side == p)
            def _():
                hidden_buf[col] = narrow
                hidden_out[:, here] = narrow
                hid(col).start()

            rounded = narrow.astype(F32)
            square_sum[...] += jnp.sum(rounded * rounded, axis=1, keepdims=True)
            ready = (rounded * gain[:, at].astype(F32)).astype(BF16)
            values_sum[...] += nt(ready, weights[:, at])
            return carry

        lax.fori_loop(0, chunks, collect, 0)
        scale = lax.rsqrt(square_sum[...] * (1.0 / (2 * half)) + 1e-05)
        values[...] = (values_sum[...] * scale).astype(BF16)
        for h in range(heads):
            at = slice(h * HEAD, (h + 1) * HEAD)
            weighted = (values[:, at].astype(F32) * rest[:, h : h + 1]).astype(BF16)
            states[0, 0:HEAD, at] = nn(keys_t[h // group], weighted).astype(BF16)
        send_own(states, state_send, state_forward, state_recv)
        for h in range(heads):
            at = slice(h * HEAD, (h + 1) * HEAD)
            mixed[:, at] = nn(damped[h], values[:, at])
        incoming[...] = jnp.zeros_like(incoming)
        passed[...] = jnp.zeros_like(passed)

        def join(slot):
            incoming[...] += states[slot, 0:HEAD, :].astype(F32) * jnp.exp(passed[0:1, :])
            passed[...] += states[slot, HEAD : HEAD + PAD, :].astype(F32) + states[
                slot, HEAD + PAD : HEAD + 2 * PAD, :
            ].astype(F32)

        def join_pair(k, carry):
            arrival(states, state_send, state_recv, 2 * k).wait_recv()
            forward(states, state_forward, state_recv, k).start()
            arrival(states, state_send, state_recv, 2 * k - 1).wait_recv()
            join(2 * k - 1)
            join(2 * k)
            return carry

        lax.fori_loop(1, before + 1, join_pair, 0)

        @pl.when(odd == 1)
        def _():
            arrival(states, state_send, state_recv, c).wait_recv()
            join(c)

        spike_copy.wait()
        for h in range(heads):
            at = slice(h * HEAD, (h + 1) * HEAD)
            both = mixed[:, at] + nn(faded[:, at], incoming[:, at].astype(BF16))
            scaled = both * lax.rsqrt(jnp.mean(both * both, axis=1, keepdims=True) + 1e-05)
            gated = scaled * (spike_buf[:, at].astype(F32) * thresholds[:, at])
            head_out[:, at] = jnp.where(valid_col, gated, 0.0).astype(BF16)
        sent_own(states, state_send, state_forward, state_recv)
        each(chunks_half, lambda j: hid(j).wait_send())
        residual_send.wait_send()
        att_copy.wait_send()

    sent_own(kv, kv_send, kv_forward, kv_recv)


def fused(
    residual,
    queries,
    keys,
    window_values,
    mixing,
    norm_gain,
    log_decay,
    spike_counts,
    thresholds,
    lengths,
):
    n = lax.axis_size("ctx")
    rows, half = residual.shape
    width = queries.shape[2]
    heads = width // HEAD
    chunks = 2 * half // CHUNK
    dma = pltpu.SemaphoreType.DMA
    whole = pl.BlockSpec(memory_space=pltpu.VMEM)
    away = pl.BlockSpec(memory_space=pl.ANY)
    head_outputs, hidden = pl.pallas_call(
        functools.partial(kernel, n),
        out_shape=(
            jax.ShapeDtypeStruct((rows, width), BF16),
            jax.ShapeDtypeStruct((rows, half), BF16),
        ),
        in_specs=[
            away,
            whole,
            whole,
            whole,
            away,
            whole,
            whole,
            whole,
            away,
            whole,
            pl.BlockSpec(memory_space=pltpu.SMEM),
        ],
        out_specs=(whole, whole),
        scratch_shapes=[
            pltpu.VMEM(mixing.shape[1:], BF16),
            pltpu.VMEM((rows, width), jnp.int32),
            pltpu.VMEM((n, 2 * rows, HEAD), BF16),
            pltpu.VMEM((rows, width // 2), BF16),
            pltpu.VMEM((4 * rows, HEAD), BF16),
            pltpu.VMEM((1, 4 * rows), F32),
            pltpu.VMEM((1, 4 * rows), F32),
            pltpu.VMEM((HEAD, 4 * rows), F32),
            pltpu.VMEM((2, rows, width // 2), BF16),
            pltpu.VMEM((chunks, rows, CHUNK), BF16),
            pltpu.VMEM((chunks, rows, CHUNK), BF16),
            pltpu.VMEM((chunks, rows, CHUNK), BF16),
            pltpu.VMEM((2, rows, half), BF16),
            pltpu.VMEM((chunks // 2, rows, CHUNK), BF16),
            pltpu.VMEM((rows, width), F32),
            pltpu.VMEM((rows, 1), F32),
            pltpu.VMEM((heads, rows, rows), BF16),
            pltpu.VMEM((rows, width), BF16),
            pltpu.VMEM((rows, heads), F32),
            pltpu.VMEM((2, HEAD, rows), BF16),
            pltpu.VMEM((rows, width), BF16),
            pltpu.VMEM((n, HEAD + 2 * PAD, width), BF16),
            pltpu.VMEM((HEAD, width), F32),
            pltpu.VMEM((PAD, width), F32),
            pltpu.VMEM((rows, width), F32),
            dma,
            dma,
            dma((3,)),
            dma((2,)),
            dma((2,)),
            dma((n // 2,)),
            dma((n,)),
            dma((n // 2,)),
            dma((2,)),
            dma((chunks,)),
            dma((chunks,)),
            dma((chunks,)),
            dma((chunks,)),
            dma((chunks // 2,)),
            dma((chunks // 2,)),
            dma((n // 2,)),
            dma((n,)),
            dma((n // 2,)),
        ],
        compiler_params=pltpu.CompilerParams(
            collective_id=0, has_side_effects=True, vmem_limit_bytes=56 * 1024 * 1024
        ),
    )(
        residual,
        queries[0],
        keys[0],
        window_values,
        mixing[0],
        norm_gain.reshape(1, -1),
        log_decay,
        log_decay.T,
        spike_counts,
        thresholds.reshape(1, -1),
        lengths,
    )
    return (head_outputs[None], hidden)


def chosen(*arrays):
    residual, queries, keys = arrays[:3]
    shards = lax.axis_size("ctx")
    rows = residual.shape[0]
    fits = (
        lax.axis_size("tp") == 2
        and lax.axis_size("section") == 2
        and keys.shape[2] == 2 * HEAD
        and queries.shape[2] == 8 * HEAD
        and rows == 2 * HEAD
        and residual.shape[1] % CHUNK == 0
        and shards % 2 == 0
        and shards * rows <= WINDOW
    )
    return fused(*arrays) if fits else body(*arrays)


def solution(mesh):
    return jax.shard_map(
        chosen,
        mesh=mesh,
        in_specs=(
            P("ctx", "tp"),
            P("section", "ctx", "tp"),
            P("section", "ctx", "tp"),
            P("ctx", "tp"),
            P("section", "tp", None),
            P(),
            P("ctx", "tp"),
            P("ctx", "tp"),
            P("tp"),
            P(),
        ),
        out_specs=(P("section", "ctx", "tp"), P("ctx", "tp")),
        check_vma=False,
    )
```

```python
import functools
import math

import jax
import jax.numpy as jnp
from jax import lax
from jax.experimental import pallas as pl
from jax.experimental.pallas import tpu as pltpu
from jax.sharding import PartitionSpec as P

HEAD = 128
WINDOW = 4096


def passed_along(x, axis, by):
    devices = lax.axis_size(axis)
    pairs = [(i, i + by) for i in range(devices) if 0 <= i + by < devices]
    return lax.ppermute(x, axis, pairs)


def entering(x, axis, join, neutral):
    place = lax.axis_index(axis)
    gathered = jax.tree.map(
        lambda a, kind: lax.all_gather(a.astype(kind), axis), x, (jnp.bfloat16, jnp.bfloat16)
    )
    state = jax.tree.map(lambda a, e: jnp.zeros_like(a) + jnp.asarray(e, a.dtype), x, neutral)

    def one(step, state):
        return join(
            state,
            jax.tree.map(
                lambda a, own: lax.dynamic_index_in_dim(a, step, 0, False).astype(own.dtype),
                gathered,
                x,
            ),
        )

    return lax.fori_loop(0, place, one, state)


def body(
    residual,
    queries,
    keys,
    window_values,
    mixing,
    norm_gain,
    log_decay,
    spike_counts,
    thresholds,
    lengths,
):
    section_index = lax.axis_index("section")
    shard_index = lax.axis_index("ctx")
    row_count = keys.shape[1]
    head_size = HEAD
    key_heads = keys.shape[2] // head_size
    query_head_rows = queries.shape[2] // head_size
    group_size = query_head_rows // key_heads
    span_blocks = WINDOW // row_count
    feature_count = mixing.shape[2]
    scale = 1.0 / math.sqrt(head_size)
    positions = jnp.arange(row_count, dtype=jnp.int32)
    valid_rows = positions < lengths[shard_index]
    own_keys = keys[0]
    earlier = [
        passed_along((own_keys, window_values), "ctx", distance + 1)
        for distance in range(span_blocks)
    ]
    key_blocks = jnp.stack([pair[0] for pair in earlier[::-1]] + [own_keys], 0)
    value_blocks = jnp.stack([pair[1] for pair in earlier[::-1]] + [window_values], 0)

    def window_layer(dummy_arg):
        query_rows = queries[0].reshape(row_count, key_heads, group_size, head_size)
        sources = shard_index - span_blocks + jnp.arange(span_blocks + 1, dtype=jnp.int32)
        block_valid = (sources[:, None] >= 0) & (
            positions[None, :] < lengths[jnp.clip(sources, 0, None)][:, None]
        )
        offsets = (span_blocks - jnp.arange(span_blocks + 1, dtype=jnp.int32)) * row_count
        base_distance = positions[:, None] - positions[None, :]

        def weight_step(carry, items):
            running, totals, best = carry
            scores = (
                jnp.einsum(
                    "rgjd,kgd->gjrk",
                    query_rows,
                    items[0].reshape(row_count, key_heads, head_size),
                    preferred_element_type=jnp.float32,
                )
                * scale
            )
            distance = base_distance + items[3]
            allowed = items[2][None, :] & (distance >= 0) & (distance < WINDOW)
            scores = jnp.where(allowed, scores, -1e30)
            new_best = jnp.maximum(best, jnp.max(scores, axis=-1))
            factor = jnp.exp(best - new_best)
            weights = jnp.where(allowed, jnp.exp(scores - new_best[..., None]), 0.0)
            blended = jnp.einsum(
                "gjrk,kgd->gjrd",
                weights.astype(jnp.bfloat16),
                items[1].reshape(row_count, key_heads, head_size),
                preferred_element_type=jnp.float32,
            )
            return (
                (
                    running * factor[..., None] + blended,
                    totals * factor + jnp.sum(weights, axis=-1),
                    new_best,
                ),
                None,
            )

        start_sums = (
            jnp.zeros((key_heads, group_size, row_count, head_size), jnp.float32),
            jnp.zeros((key_heads, group_size, row_count), jnp.float32),
            jnp.full((key_heads, group_size, row_count), -1e30, jnp.float32),
        )
        (blended, totals, unused_best), unused_sum = lax.scan(
            weight_step, start_sums, (key_blocks, value_blocks, block_valid, offsets)
        )
        attention = blended / jnp.maximum(totals, 1.0)[..., None]
        attention = attention.transpose(2, 0, 1, 3).reshape(row_count, query_head_rows * head_size)
        attention = jnp.where(valid_rows[:, None], attention, 0.0).astype(jnp.bfloat16)
        projected = jnp.dot(attention, mixing[0], preferred_element_type=jnp.float32)
        return (attention, projected)

    def window_skip(dummy_arg):
        return (
            jnp.zeros((row_count, query_head_rows * head_size), jnp.bfloat16),
            jnp.zeros((row_count, feature_count), jnp.float32),
        )

    attention, projected = lax.cond(section_index == 0, window_layer, window_skip, 0)
    share = lax.psum_scatter(
        projected.astype(jnp.bfloat16), "tp", scatter_dimension=1, tiled=True
    ).astype(jnp.float32)
    own_hidden = (share + residual.astype(jnp.float32)).astype(jnp.bfloat16)
    moved_share = passed_along(own_hidden, "section", 1)
    local_activations = jnp.where(section_index == 0, own_hidden, moved_share)
    complete_hidden_matrix = lax.all_gather(local_activations, "tp", axis=1, tiled=True)
    masked_keys = jnp.where(valid_rows[:, None], own_keys, jnp.zeros_like(own_keys)).reshape(
        row_count, key_heads, head_size
    )
    wide_keys = masked_keys.astype(jnp.float32)
    decays = log_decay * valid_rows[:, None].astype(jnp.float32)

    def linear_prepare(dummy_arg):
        wide = complete_hidden_matrix.astype(jnp.float32)
        normed = (
            wide
            * lax.rsqrt(jnp.mean(wide * wide, axis=-1, keepdims=True) + 1e-05)
            * norm_gain.astype(jnp.float32)
        ).astype(jnp.bfloat16)
        payload_vectors = lax.dot_general(
            normed, mixing[0], (((1,), (1,)), ((), ())), preferred_element_type=jnp.float32
        ).astype(jnp.bfloat16)
        cumulated = jnp.cumsum(decays, axis=0).reshape(row_count, key_heads, group_size)
        value_rows = payload_vectors.astype(jnp.float32).reshape(
            row_count, key_heads, group_size, head_size
        )
        fresh_state = jnp.einsum(
            "sgd,sgje->gdje",
            wide_keys,
            value_rows * jnp.exp(cumulated[-1] - cumulated)[..., None],
            precision=lax.Precision.HIGHEST,
        )
        return (payload_vectors, cumulated, fresh_state)

    def linear_skip(dummy_arg):
        return (
            jnp.zeros((row_count, query_head_rows * head_size), jnp.bfloat16),
            jnp.zeros((row_count, key_heads, group_size), jnp.float32),
            jnp.zeros((key_heads, head_size, group_size, head_size), jnp.float32),
        )

    payload_vectors, cumulated, fresh_state = lax.cond(
        section_index == 1, linear_prepare, linear_skip, 0
    )

    def chain(previous_entry, latter):
        return (
            previous_entry[0] + latter[0],
            previous_entry[1] * jnp.exp(latter[0])[:, None, :, None] + latter[1],
        )

    identity = (jnp.zeros((key_heads, group_size), jnp.float32), jnp.zeros_like(fresh_state))
    unused_total, incoming = entering((cumulated[-1], fresh_state), "ctx", chain, identity)

    def linear_finish(dummy_arg):
        query_narrow = queries[0].reshape(row_count, key_heads, group_size, head_size)
        query_rows = query_narrow.astype(jnp.float32)
        value_rows = payload_vectors.astype(jnp.float32).reshape(
            row_count, key_heads, group_size, head_size
        )
        inter = (
            jnp.einsum("rgjd,gdje->rgje", query_rows, incoming, precision=lax.Precision.HIGHEST)
            * jnp.exp(cumulated)[..., None]
        )
        products = jnp.einsum(
            "rgjd,sgd->gjrs", query_narrow, masked_keys, preferred_element_type=jnp.float32
        )
        ordered = cumulated.transpose(1, 2, 0)
        spread = ordered[..., :, None] - ordered[..., None, :]
        triangle = positions[:, None] >= positions[None, :]
        damping = jnp.where(triangle, jnp.exp(jnp.minimum(spread, 0.0)), 0.0)
        intra = jnp.einsum(
            "gjrs,sgje->rgje", products * damping, value_rows, precision=lax.Precision.HIGHEST
        )
        mixed = (inter + intra).reshape(row_count, query_head_rows, head_size)
        scaled = mixed * lax.rsqrt(jnp.mean(mixed * mixed, axis=-1, keepdims=True) + 1e-05)
        gating = spike_counts.astype(jnp.float32).reshape(
            row_count, query_head_rows, head_size
        ) * thresholds.reshape(query_head_rows, head_size)
        return jnp.where(
            valid_rows[:, None],
            (scaled * gating).reshape(row_count, query_head_rows * head_size),
            0.0,
        ).astype(jnp.bfloat16)

    def finish_skip(dummy_arg):
        return jnp.zeros((row_count, query_head_rows * head_size), jnp.bfloat16)

    gated = lax.cond(section_index == 1, linear_finish, finish_skip, 0)
    head_outputs = jnp.where(section_index == 0, attention, gated)[None]
    return (head_outputs, local_activations)


MESH = pl.DeviceIdType.MESH
F32 = jnp.float32
BF16 = jnp.bfloat16
CHUNK = 256
PAD = 16


def nt(a, b):
    return lax.dot_general(a, b, (((1,), (1,)), ((), ())), preferred_element_type=F32)


def nn(a, b):
    return jnp.dot(a, b, preferred_element_type=F32)


def turned(x):
    return jnp.transpose(x.astype(F32)).astype(BF16)


def kernel(
    n,
    residual,
    queries,
    keys,
    window_values,
    mixing,
    gain,
    decay_t,
    spikes,
    thresholds,
    lengths,
    head_out,
    hidden_out,
    weights,
    spike_buf,
    kv,
    moved_queries,
    stacked,
    top,
    total,
    blend,
    attention,
    terms,
    own_terms,
    far_terms,
    residuals,
    hidden_buf,
    values_sum,
    square_sum,
    damped,
    faded,
    rest,
    keys_t,
    values,
    states,
    fresh,
    incoming,
    passed,
    mixed,
    gain_row,
    decay_wide,
    weights_sem,
    spike_sem,
    res_sem,
    first_sem,
    first_recv,
    kv_send,
    kv_recv,
    kv_forward,
    att_sem,
    term_own_send,
    term_far_send,
    term_own_recv,
    term_far_recv,
    hid_send,
    hid_recv,
    swap_send,
    swap_recv,
    state_send,
    state_recv,
):
    c = lax.axis_index("ctx")
    s = lax.axis_index("section")
    p = lax.axis_index("tp")
    odd = c % 2
    step_to = 1 - 2 * odd
    partner = c + step_to
    rows = keys.shape[0]
    half = residual.shape[1]
    chunks_half = half // CHUNK
    chunks = 2 * chunks_half
    group = 4
    wide = group * HEAD
    factor = math.log2(math.e) / math.sqrt(HEAD)

    barrier = pltpu.get_barrier_semaphore()
    pl.semaphore_signal(barrier, inc=1, device_id={"section": 1 - s}, device_id_type=MESH)
    pl.semaphore_signal(barrier, inc=1, device_id={"tp": 1 - p}, device_id_type=MESH)
    pl.semaphore_signal(
        barrier, inc=1, device_id={"section": 1 - s, "tp": 1 - p}, device_id_type=MESH
    )
    pl.semaphore_signal(barrier, inc=1, device_id={"ctx": partner}, device_id_type=MESH)
    for k in range(1, n // 2):
        pl.semaphore_signal(
            barrier, inc=1, device_id={"ctx": (c + 2 * k) % n}, device_id_type=MESH
        )

    weights_copy = pltpu.make_async_copy(mixing, weights, weights_sem)
    weights_copy.start()

    own_len = lengths[c]

    @pl.when(s == 0)
    def _():
        kv[0, 0:rows] = keys[:, 0:HEAD]
        value_t = turned(window_values[:, 0:HEAD])
        kv[0, rows : rows + HEAD] = value_t[:, 0:HEAD]
        kv[0, rows + HEAD : rows + 2 * HEAD] = value_t[:, HEAD : 2 * HEAD]
        for h in range(group):
            stacked[h * rows : (h + 1) * rows, :] = queries[:, h * HEAD : (h + 1) * HEAD]

    @pl.when(s == 1)
    def _():
        value_t = turned(window_values[:, HEAD : 2 * HEAD])
        kv[0, rows : rows + HEAD] = value_t[:, 0:HEAD]
        kv[0, rows + HEAD : rows + 2 * HEAD] = value_t[:, HEAD : 2 * HEAD]

    pl.semaphore_wait(barrier, 3 + n // 2)

    key_copy = pltpu.make_async_remote_copy(
        src_ref=keys.at[:, HEAD : 2 * HEAD],
        dst_ref=kv.at[0, 0:rows],
        send_sem=first_sem.at[0],
        recv_sem=first_recv.at[0],
        device_id={"section": 1 - s},
        device_id_type=MESH,
    )
    query_copy = pltpu.make_async_remote_copy(
        src_ref=queries.at[:, wide : 2 * wide],
        dst_ref=moved_queries,
        send_sem=first_sem.at[1],
        recv_sem=first_recv.at[1],
        device_id={"section": 1 - s},
        device_id_type=MESH,
    )
    residual_send = pltpu.make_async_remote_copy(
        src_ref=residual,
        dst_ref=residuals.at[p],
        send_sem=res_sem.at[0],
        recv_sem=res_sem.at[1],
        device_id={"tp": 1 - p},
        device_id_type=MESH,
    )
    residual_recv = pltpu.make_async_remote_copy(
        src_ref=residual,
        dst_ref=residuals.at[1 - p],
        send_sem=res_sem.at[0],
        recv_sem=res_sem.at[1],
        device_id={"tp": 1 - p},
        device_id_type=MESH,
    )
    residual_copy = pltpu.make_async_copy(residual, residuals.at[p], res_sem.at[2])
    spike_copy = pltpu.make_async_copy(spikes, spike_buf, spike_sem)

    @pl.when(s == 0)
    def _():
        key_copy.start()
        query_copy.start()

    @pl.when(s == 1)
    def _():
        residual_send.start()
        residual_copy.start()
        spike_copy.start()
        key_copy.wait_recv()

    def along(k):
        return pltpu.make_async_remote_copy(
            src_ref=kv.at[2 * k],
            dst_ref=kv.at[2 * k + 2],
            send_sem=kv_send.at[k],
            recv_sem=kv_recv.at[2 * k + 2],
            device_id={"ctx": lax.rem(c + 2, n)},
            device_id_type=MESH,
        )

    def across(k):
        return pltpu.make_async_remote_copy(
            src_ref=kv.at[2 * k],
            dst_ref=kv.at[2 * k + step_to],
            send_sem=kv_forward.at[k],
            recv_sem=kv_recv.at[2 * k + step_to],
            device_id={"ctx": partner},
            device_id_type=MESH,
        )

    def arrival(slot):
        return pltpu.make_async_remote_copy(
            src_ref=kv.at[slot],
            dst_ref=kv.at[slot],
            send_sem=kv_send.at[0],
            recv_sem=kv_recv.at[slot],
            device_id={"ctx": partner},
            device_id_type=MESH,
        )

    before = c // 2
    pairs = n // 2

    @pl.when(c + 2 < n)
    def _():
        along(0).start()

    @pl.when(odd == 0)
    def _():
        across(0).start()

    @pl.when(s == 1)
    def _():
        query_copy.wait_recv()
        for h in range(group):
            stacked[h * rows : (h + 1) * rows, :] = moved_queries[:, h * HEAD : (h + 1) * HEAD]

    def attend(slot, first):
        key_rows = kv[slot, 0:rows]
        value_t = jnp.concatenate(
            [kv[slot, rows : rows + HEAD], kv[slot, rows + HEAD : rows + 2 * HEAD]], axis=1
        )
        key_index = lax.broadcasted_iota(jnp.int32, (rows, rows), 0)
        allowed = key_index < lengths[c - slot]
        if first:
            allowed = allowed & (key_index <= lax.broadcasted_iota(jnp.int32, (rows, rows), 1))
        for h in range(group):
            at = slice(h * rows, (h + 1) * rows)
            scores = jnp.where(allowed, nt(key_rows, stacked[at, :]), -1e30)
            best = jnp.max(scores, axis=0, keepdims=True)
            if not first:
                best = jnp.maximum(best, top[:, at])
            part = jnp.exp2((scores - best) * factor)
            part_sum = jnp.sum(part, axis=0, keepdims=True)
            blended = nn(value_t, part.astype(BF16))
            if first:
                total[:, at] = part_sum
                blend[:, at] = blended
            else:
                shrink = jnp.exp2((top[:, at] - best) * factor)
                total[:, at] = total[:, at] * shrink + part_sum
                blend[:, at] = blend[:, at] * shrink + blended
            top[:, at] = best

    attend(0, True)

    def attend_pair(k, carry):
        arrival(2 * k).wait_recv()

        @pl.when(c + 2 < n)
        def _():
            along(k).start()

        across(k).start()
        arrival(2 * k - 1).wait_recv()
        attend(2 * k - 1, False)
        attend(2 * k, False)
        return carry

    lax.fori_loop(1, before + 1, attend_pair, 0)

    @pl.when(odd == 1)
    def _():
        arrival(c).wait_recv()
        attend(c, False)

    row_lane = lax.broadcasted_iota(jnp.int32, (1, rows), 1)
    for h in range(group):
        at = slice(h * rows, (h + 1) * rows)
        scaled = blend[:, at] / jnp.maximum(total[:, at], 1.0)
        scaled = jnp.where(row_lane < own_len, scaled, 0.0)
        attention[s, :, h * HEAD : (h + 1) * HEAD] = jnp.transpose(scaled).astype(BF16)

    att_copy = pltpu.make_async_remote_copy(
        src_ref=attention.at[1],
        dst_ref=attention.at[1],
        send_sem=att_sem.at[0],
        recv_sem=att_sem.at[1],
        device_id={"section": 1 - s},
        device_id_type=MESH,
    )

    def term_own(j):
        return pltpu.make_async_remote_copy(
            src_ref=terms.at[j],
            dst_ref=own_terms.at[j],
            send_sem=term_own_send.at[j],
            recv_sem=term_own_recv.at[j],
            device_id={"section": 1 - s},
            device_id_type=MESH,
        )

    def term_far(j):
        return pltpu.make_async_remote_copy(
            src_ref=terms.at[j],
            dst_ref=far_terms.at[j],
            send_sem=term_far_send.at[j],
            recv_sem=term_far_recv.at[j],
            device_id={"section": 1 - s, "tp": 1 - p},
            device_id_type=MESH,
        )

    def hid(j):
        return pltpu.make_async_remote_copy(
            src_ref=hidden_buf.at[j],
            dst_ref=hidden_out.at[:, pl.ds(pl.multiple_of(j * CHUNK, CHUNK), CHUNK)],
            send_sem=hid_send.at[j],
            recv_sem=hid_recv.at[j],
            device_id={"section": 1 - s},
            device_id_type=MESH,
        )

    def each(count, act):
        def one(j, carry):
            act(j)
            return carry

        lax.fori_loop(0, count, one, 0)

    @pl.when(s == 0)
    def _():
        weights_copy.wait()
        att_copy.wait_recv()

        def project(j, carry):
            at = pl.ds(pl.multiple_of(j * CHUNK, CHUNK), CHUNK)
            both = jnp.concatenate([attention[0], attention[1]], axis=1)
            terms[j] = nn(both, weights[:, at]).astype(BF16)
            term_far(j).start()
            term_own(j).start()
            return carry

        lax.fori_loop(0, chunks, project, 0)
        head_out[:, 0:wide] = attention[0]
        head_out[:, wide : 2 * wide] = attention[1]
        each(chunks, lambda j: term_far(j).wait_send())
        each(chunks, lambda j: term_own(j).wait_send())
        key_copy.wait_send()
        query_copy.wait_send()
        each(chunks_half, lambda j: hid(j).wait_recv())

    @pl.when(s == 1)
    def _():
        att_copy.start()
        heads = 2 * group
        row_col = lax.broadcasted_iota(jnp.int32, (rows, 1), 0)
        valid_col = row_col < own_len
        r = lax.broadcasted_iota(jnp.int32, (rows, rows), 0)
        t = lax.broadcasted_iota(jnp.int32, (rows, rows), 1)
        upper = jnp.where(r <= t, 1.0, 0.0)
        decay_wide[...] = jnp.zeros_like(decay_wide)
        decay_wide[0:heads, :] = jnp.where(row_lane < own_len, decay_t[...], 0.0)
        cum_t = jnp.dot(
            decay_wide[...], upper, precision=lax.Precision.HIGHEST, preferred_element_type=F32
        )
        cum = jnp.transpose(cum_t)
        gain_row[...] = gain[...].astype(F32).reshape(1, 2 * half)
        last = cum[rows - 1 : rows, :]
        rest[...] = jnp.exp(last - cum)
        for g in range(2):
            masked = jnp.where(valid_col, keys[:, g * HEAD : (g + 1) * HEAD].astype(F32), 0.0)
            keys_t[g] = jnp.transpose(masked).astype(BF16)
        for h in range(heads):
            at = slice(h * HEAD, (h + 1) * HEAD)
            col = cum[:, h : h + 1]
            row = cum_t[h : h + 1, :]
            query = queries[:, at]
            damping = jnp.where(r >= t, jnp.exp(jnp.minimum(col - row, 0.0)), 0.0)
            damped[h] = (nn(query, keys_t[h // group]) * damping).astype(BF16)
            faded[:, at] = (query.astype(F32) * jnp.exp(col)).astype(BF16)
            sum_row = jnp.broadcast_to(last[:, h : h + 1], (PAD, HEAD))
            high = sum_row.astype(BF16)
            low = sum_row - high.astype(F32)
            in_group = slice((h % group) * HEAD, (h % group + 1) * HEAD)
            states[0, h // group, HEAD : HEAD + PAD, in_group] = jnp.where(
                lax.broadcasted_iota(jnp.int32, (PAD, HEAD), 0) < PAD // 2,
                high.astype(F32),
                low,
            ).astype(BF16)
        values_sum[...] = jnp.zeros_like(values_sum)
        square_sum[...] = jnp.zeros_like(square_sum)
        weights_copy.wait()
        residual_copy.wait()
        residual_recv.wait_recv()

        def collect(j, carry):
            side = j // chunks_half
            col = j - side * chunks_half
            here = pl.ds(pl.multiple_of(col * CHUNK, CHUNK), CHUNK)
            at = pl.ds(pl.multiple_of(j * CHUNK, CHUNK), CHUNK)
            term_own(j).wait_recv()
            term_far(j).wait_recv()
            summed = residuals[side, :, here].astype(F32) + (
                own_terms[j].astype(F32) + far_terms[j].astype(F32)
            )
            narrow = summed.astype(BF16)

            @pl.when(side == p)
            def _():
                hidden_buf[col] = narrow
                hidden_out[:, here] = narrow
                hid(col).start()

            rounded = narrow.astype(F32)
            square_sum[...] += jnp.sum(rounded * rounded, axis=1, keepdims=True)
            ready = (rounded * gain_row[:, at]).astype(BF16)
            values_sum[...] += nt(ready, weights[:, at])
            return carry

        lax.fori_loop(0, chunks, collect, 0)
        scale = lax.rsqrt(square_sum[...] * (1.0 / (2 * half)) + 1e-05)
        values[...] = (values_sum[...] * scale).astype(BF16)
        def swap(g):
            return pltpu.make_async_remote_copy(
                src_ref=states.at[0, g],
                dst_ref=states.at[1, g],
                send_sem=swap_send.at[g],
                recv_sem=swap_recv.at[g],
                device_id={"ctx": partner},
                device_id_type=MESH,
            )

        def onward(k, g):
            return pltpu.make_async_remote_copy(
                src_ref=states.at[2, g],
                dst_ref=states.at[2 + k, g],
                send_sem=state_send.at[k, g],
                recv_sem=state_recv.at[k, g],
                device_id={"ctx": lax.rem(c + 2 * k, n)},
                device_id_type=MESH,
            )

        def sum_of(slot, g):
            rows_of = states[slot, g, HEAD : HEAD + PAD, :].astype(F32)
            return rows_of[0:1, :] + rows_of[PAD // 2 : PAD // 2 + 1, :]

        here_later = pairs - 1 - before
        swap_out = (odd == 0) | (here_later > 0)
        swap_in = (odd == 1) | (here_later > 0)
        for g in range(2):
            for h in range(g * group, (g + 1) * group):
                at = slice(h * HEAD, (h + 1) * HEAD)
                weighted = (values[:, at].astype(F32) * rest[:, h : h + 1]).astype(BF16)
                fresh[:, at] = nn(keys_t[g], weighted)
                in_group = slice((h % group) * HEAD, (h % group + 1) * HEAD)
                states[0, g, 0:HEAD, in_group] = fresh[:, at].astype(BF16)

            @pl.when(swap_out)
            def _():
                swap(g).start()

        for h in range(heads):
            at = slice(h * HEAD, (h + 1) * HEAD)
            mixed[:, at] = nn(damped[h], values[:, at])

        for g in range(2):
            at = slice(g * wide, (g + 1) * wide)

            @pl.when(swap_in)
            def _():
                swap(g).wait_recv()

            @pl.when(here_later > 0)
            def _():
                own_sum = sum_of(0, g)
                other_sum = sum_of(1, g)
                second = jnp.where(odd == 1, own_sum, other_sum)
                own = fresh[:, at]
                other = states[1, g, 0:HEAD, :].astype(F32)
                first_part = jnp.where(odd == 1, other, own)
                second_part = jnp.where(odd == 1, own, other)
                states[2, g, 0:HEAD, :] = (first_part * jnp.exp(second) + second_part).astype(BF16)
                both_sum = jnp.broadcast_to(own_sum + other_sum, (PAD, wide))
                high = both_sum.astype(BF16).astype(F32)
                states[2, g, HEAD : HEAD + PAD, :] = jnp.where(
                    lax.broadcasted_iota(jnp.int32, (PAD, wide), 0) < PAD // 2,
                    high,
                    both_sum - high,
                ).astype(BF16)

                def send_on(k, carry):
                    onward(k, g).start()
                    return carry

                lax.fori_loop(1, here_later + 1, send_on, 0)

        spike_copy.wait()
        for g in range(2):
            at = slice(g * wide, (g + 1) * wide)

            @pl.when(odd == 1)
            def _():
                incoming[:, at] = states[1, g, 0:HEAD, :].astype(F32)
                passed[:, at] = sum_of(1, g)

            @pl.when(odd == 0)
            def _():
                incoming[:, at] = jnp.zeros((HEAD, wide), F32)
                passed[:, at] = jnp.zeros((1, wide), F32)

            def join(k, carry):
                onward(k, g).wait_recv()
                incoming[:, at] += states[2 + k, g, 0:HEAD, :].astype(F32) * jnp.exp(passed[:, at])
                passed[:, at] += sum_of(2 + k, g)
                return carry

            lax.fori_loop(1, before + 1, join, 0)
            for h in range(g * group, (g + 1) * group):
                at = slice(h * HEAD, (h + 1) * HEAD)
                both = mixed[:, at] + nn(faded[:, at], incoming[:, at].astype(BF16))
                scaled = both * lax.rsqrt(jnp.mean(both * both, axis=1, keepdims=True) + 1e-05)
                gated = scaled * (spike_buf[:, at].astype(F32) * thresholds[:, at])
                head_out[:, at] = jnp.where(valid_col, gated, 0.0).astype(BF16)

        for g in range(2):

            @pl.when(swap_out)
            def _():
                swap(g).wait_send()

            def sent_on(k, carry):
                onward(k, g).wait_send()
                return carry

            lax.fori_loop(1, here_later + 1, sent_on, 0)
        each(chunks_half, lambda j: hid(j).wait_send())
        residual_send.wait_send()
        att_copy.wait_send()

    def along_done(k, carry):
        along(k).wait_send()
        return carry

    @pl.when(c + 2 < n)
    def _():
        lax.fori_loop(0, before + 1, along_done, 0)

    @pl.when(odd == 0)
    def _():
        across(0).wait_send()

    def across_done(k, carry):
        across(k).wait_send()
        return carry

    lax.fori_loop(1, before + 1, across_done, 0)


def handed_on(a, b, a_out, b_out, a_sem, b_sem):
    one = pltpu.make_async_copy(a, a_out, a_sem)
    two = pltpu.make_async_copy(b, b_out, b_sem)
    one.start()
    two.start()
    one.wait()
    two.wait()


def fused(
    residual,
    queries,
    keys,
    window_values,
    mixing,
    norm_gain,
    log_decay,
    spike_counts,
    thresholds,
    lengths,
):
    n = lax.axis_size("ctx")
    rows, half = residual.shape
    width = queries.shape[2]
    heads = width // HEAD
    chunks = 2 * half // CHUNK
    dma = pltpu.SemaphoreType.DMA
    whole = pl.BlockSpec(memory_space=pltpu.VMEM)
    away = pl.BlockSpec(memory_space=pl.ANY)
    head_outputs, hidden = pl.pallas_call(
        functools.partial(kernel, n),
        out_shape=(
            jax.ShapeDtypeStruct((rows, width), BF16),
            jax.ShapeDtypeStruct((rows, half), BF16),
        ),
        in_specs=[
            away,
            whole,
            whole,
            whole,
            away,
            whole,
            whole,
            away,
            whole,
            pl.BlockSpec(memory_space=pltpu.SMEM),
        ],
        out_specs=(whole, whole),
        scratch_shapes=[
            pltpu.VMEM(mixing.shape[1:], BF16),
            pltpu.VMEM((rows, width), jnp.int32),
            pltpu.VMEM((n, 2 * rows, HEAD), BF16),
            pltpu.VMEM((rows, width // 2), BF16),
            pltpu.VMEM((4 * rows, HEAD), BF16),
            pltpu.VMEM((1, 4 * rows), F32),
            pltpu.VMEM((1, 4 * rows), F32),
            pltpu.VMEM((HEAD, 4 * rows), F32),
            pltpu.VMEM((2, rows, width // 2), BF16),
            pltpu.VMEM((chunks, rows, CHUNK), BF16),
            pltpu.VMEM((chunks, rows, CHUNK), BF16),
            pltpu.VMEM((chunks, rows, CHUNK), BF16),
            pltpu.VMEM((2, rows, half), BF16),
            pltpu.VMEM((chunks // 2, rows, CHUNK), BF16),
            pltpu.VMEM((rows, width), F32),
            pltpu.VMEM((rows, 1), F32),
            pltpu.VMEM((heads, rows, rows), BF16),
            pltpu.VMEM((rows, width), BF16),
            pltpu.VMEM((rows, HEAD), F32),
            pltpu.VMEM((2, HEAD, rows), BF16),
            pltpu.VMEM((rows, width), BF16),
            pltpu.VMEM((n // 2 + 2, 2, HEAD + PAD, width // 2), BF16),
            pltpu.VMEM((HEAD, width), F32),
            pltpu.VMEM((HEAD, width), F32),
            pltpu.VMEM((1, width), F32),
            pltpu.VMEM((rows, width), F32),
            pltpu.VMEM((1, 2 * half), F32),
            pltpu.VMEM((HEAD, rows), F32),
            dma,
            dma,
            dma((3,)),
            dma((2,)),
            dma((2,)),
            dma((n // 2,)),
            dma((n,)),
            dma((n // 2,)),
            dma((2,)),
            dma((chunks,)),
            dma((chunks,)),
            dma((chunks,)),
            dma((chunks,)),
            dma((chunks // 2,)),
            dma((chunks // 2,)),
            dma((2,)),
            dma((2,)),
            dma((n // 2, 2)),
            dma((n // 2, 2)),
        ],
        compiler_params=pltpu.CompilerParams(
            collective_id=0, has_side_effects=True, vmem_limit_bytes=56 * 1024 * 1024
        ),
    )(
        residual,
        queries[0],
        keys[0],
        window_values,
        mixing[0],
        norm_gain,
        log_decay.T,
        spike_counts,
        thresholds.reshape(1, -1),
        lengths,
    )
    head_outputs, hidden = pl.pallas_call(
        handed_on,
        out_shape=(
            jax.ShapeDtypeStruct((rows, width), BF16),
            jax.ShapeDtypeStruct((rows, half), BF16),
        ),
        in_specs=[away, away],
        out_specs=(away, away),
        scratch_shapes=[dma, dma],
        compiler_params=pltpu.CompilerParams(vmem_limit_bytes=60 * 1024 * 1024),
    )(head_outputs, hidden)
    return (head_outputs[None], hidden)


def chosen(*arrays):
    residual, queries, keys = arrays[:3]
    shards = lax.axis_size("ctx")
    rows = residual.shape[0]
    fits = (
        lax.axis_size("tp") == 2
        and lax.axis_size("section") == 2
        and keys.shape[2] == 2 * HEAD
        and queries.shape[2] == 8 * HEAD
        and rows == 2 * HEAD
        and residual.shape[1] % CHUNK == 0
        and shards % 2 == 0
        and shards * rows <= WINDOW
    )
    return fused(*arrays) if fits else body(*arrays)


def solution(mesh):
    return jax.shard_map(
        chosen,
        mesh=mesh,
        in_specs=(
            P("ctx", "tp"),
            P("section", "ctx", "tp"),
            P("section", "ctx", "tp"),
            P("ctx", "tp"),
            P("section", "tp", None),
            P(),
            P("ctx", "tp"),
            P("ctx", "tp"),
            P("tp"),
            P(),
        ),
        out_specs=(P("section", "ctx", "tp"), P("ctx", "tp")),
        check_vma=False,
    )
```

```python
import functools
import math

import jax
import jax.numpy as jnp
from jax import lax
from jax.experimental import pallas as pl
from jax.experimental.pallas import tpu as pltpu
from jax.sharding import PartitionSpec as P

HEAD = 128
WINDOW = 4096


def passed_along(x, axis, by):
    devices = lax.axis_size(axis)
    pairs = [(i, i + by) for i in range(devices) if 0 <= i + by < devices]
    return lax.ppermute(x, axis, pairs)


def entering(x, axis, join, neutral):
    place = lax.axis_index(axis)
    gathered = jax.tree.map(
        lambda a, kind: lax.all_gather(a.astype(kind), axis), x, (jnp.bfloat16, jnp.bfloat16)
    )
    state = jax.tree.map(lambda a, e: jnp.zeros_like(a) + jnp.asarray(e, a.dtype), x, neutral)

    def one(step, state):
        return join(
            state,
            jax.tree.map(
                lambda a, own: lax.dynamic_index_in_dim(a, step, 0, False).astype(own.dtype),
                gathered,
                x,
            ),
        )

    return lax.fori_loop(0, place, one, state)


def body(
    residual,
    queries,
    keys,
    window_values,
    mixing,
    norm_gain,
    log_decay,
    spike_counts,
    thresholds,
    lengths,
):
    section_index = lax.axis_index("section")
    shard_index = lax.axis_index("ctx")
    row_count = keys.shape[1]
    head_size = HEAD
    key_heads = keys.shape[2] // head_size
    query_head_rows = queries.shape[2] // head_size
    group_size = query_head_rows // key_heads
    span_blocks = WINDOW // row_count
    feature_count = mixing.shape[2]
    scale = 1.0 / math.sqrt(head_size)
    positions = jnp.arange(row_count, dtype=jnp.int32)
    valid_rows = positions < lengths[shard_index]
    own_keys = keys[0]
    earlier = [
        passed_along((own_keys, window_values), "ctx", distance + 1)
        for distance in range(span_blocks)
    ]
    key_blocks = jnp.stack([pair[0] for pair in earlier[::-1]] + [own_keys], 0)
    value_blocks = jnp.stack([pair[1] for pair in earlier[::-1]] + [window_values], 0)

    def window_layer(dummy_arg):
        query_rows = queries[0].reshape(row_count, key_heads, group_size, head_size)
        sources = shard_index - span_blocks + jnp.arange(span_blocks + 1, dtype=jnp.int32)
        block_valid = (sources[:, None] >= 0) & (
            positions[None, :] < lengths[jnp.clip(sources, 0, None)][:, None]
        )
        offsets = (span_blocks - jnp.arange(span_blocks + 1, dtype=jnp.int32)) * row_count
        base_distance = positions[:, None] - positions[None, :]

        def weight_step(carry, items):
            running, totals, best = carry
            scores = (
                jnp.einsum(
                    "rgjd,kgd->gjrk",
                    query_rows,
                    items[0].reshape(row_count, key_heads, head_size),
                    preferred_element_type=jnp.float32,
                )
                * scale
            )
            distance = base_distance + items[3]
            allowed = items[2][None, :] & (distance >= 0) & (distance < WINDOW)
            scores = jnp.where(allowed, scores, -1e30)
            new_best = jnp.maximum(best, jnp.max(scores, axis=-1))
            factor = jnp.exp(best - new_best)
            weights = jnp.where(allowed, jnp.exp(scores - new_best[..., None]), 0.0)
            blended = jnp.einsum(
                "gjrk,kgd->gjrd",
                weights.astype(jnp.bfloat16),
                items[1].reshape(row_count, key_heads, head_size),
                preferred_element_type=jnp.float32,
            )
            return (
                (
                    running * factor[..., None] + blended,
                    totals * factor + jnp.sum(weights, axis=-1),
                    new_best,
                ),
                None,
            )

        start_sums = (
            jnp.zeros((key_heads, group_size, row_count, head_size), jnp.float32),
            jnp.zeros((key_heads, group_size, row_count), jnp.float32),
            jnp.full((key_heads, group_size, row_count), -1e30, jnp.float32),
        )
        (blended, totals, unused_best), unused_sum = lax.scan(
            weight_step, start_sums, (key_blocks, value_blocks, block_valid, offsets)
        )
        attention = blended / jnp.maximum(totals, 1.0)[..., None]
        attention = attention.transpose(2, 0, 1, 3).reshape(row_count, query_head_rows * head_size)
        attention = jnp.where(valid_rows[:, None], attention, 0.0).astype(jnp.bfloat16)
        projected = jnp.dot(attention, mixing[0], preferred_element_type=jnp.float32)
        return (attention, projected)

    def window_skip(dummy_arg):
        return (
            jnp.zeros((row_count, query_head_rows * head_size), jnp.bfloat16),
            jnp.zeros((row_count, feature_count), jnp.float32),
        )

    attention, projected = lax.cond(section_index == 0, window_layer, window_skip, 0)
    share = lax.psum_scatter(
        projected.astype(jnp.bfloat16), "tp", scatter_dimension=1, tiled=True
    ).astype(jnp.float32)
    own_hidden = (share + residual.astype(jnp.float32)).astype(jnp.bfloat16)
    moved_share = passed_along(own_hidden, "section", 1)
    local_activations = jnp.where(section_index == 0, own_hidden, moved_share)
    complete_hidden_matrix = lax.all_gather(local_activations, "tp", axis=1, tiled=True)
    masked_keys = jnp.where(valid_rows[:, None], own_keys, jnp.zeros_like(own_keys)).reshape(
        row_count, key_heads, head_size
    )
    wide_keys = masked_keys.astype(jnp.float32)
    decays = log_decay * valid_rows[:, None].astype(jnp.float32)

    def linear_prepare(dummy_arg):
        wide = complete_hidden_matrix.astype(jnp.float32)
        normed = (
            wide
            * lax.rsqrt(jnp.mean(wide * wide, axis=-1, keepdims=True) + 1e-05)
            * norm_gain.astype(jnp.float32)
        ).astype(jnp.bfloat16)
        payload_vectors = lax.dot_general(
            normed, mixing[0], (((1,), (1,)), ((), ())), preferred_element_type=jnp.float32
        ).astype(jnp.bfloat16)
        cumulated = jnp.cumsum(decays, axis=0).reshape(row_count, key_heads, group_size)
        value_rows = payload_vectors.astype(jnp.float32).reshape(
            row_count, key_heads, group_size, head_size
        )
        fresh_state = jnp.einsum(
            "sgd,sgje->gdje",
            wide_keys,
            value_rows * jnp.exp(cumulated[-1] - cumulated)[..., None],
            precision=lax.Precision.HIGHEST,
        )
        return (payload_vectors, cumulated, fresh_state)

    def linear_skip(dummy_arg):
        return (
            jnp.zeros((row_count, query_head_rows * head_size), jnp.bfloat16),
            jnp.zeros((row_count, key_heads, group_size), jnp.float32),
            jnp.zeros((key_heads, head_size, group_size, head_size), jnp.float32),
        )

    payload_vectors, cumulated, fresh_state = lax.cond(
        section_index == 1, linear_prepare, linear_skip, 0
    )

    def chain(previous_entry, latter):
        return (
            previous_entry[0] + latter[0],
            previous_entry[1] * jnp.exp(latter[0])[:, None, :, None] + latter[1],
        )

    identity = (jnp.zeros((key_heads, group_size), jnp.float32), jnp.zeros_like(fresh_state))
    unused_total, incoming = entering((cumulated[-1], fresh_state), "ctx", chain, identity)

    def linear_finish(dummy_arg):
        query_narrow = queries[0].reshape(row_count, key_heads, group_size, head_size)
        query_rows = query_narrow.astype(jnp.float32)
        value_rows = payload_vectors.astype(jnp.float32).reshape(
            row_count, key_heads, group_size, head_size
        )
        inter = (
            jnp.einsum("rgjd,gdje->rgje", query_rows, incoming, precision=lax.Precision.HIGHEST)
            * jnp.exp(cumulated)[..., None]
        )
        products = jnp.einsum(
            "rgjd,sgd->gjrs", query_narrow, masked_keys, preferred_element_type=jnp.float32
        )
        ordered = cumulated.transpose(1, 2, 0)
        spread = ordered[..., :, None] - ordered[..., None, :]
        triangle = positions[:, None] >= positions[None, :]
        damping = jnp.where(triangle, jnp.exp(jnp.minimum(spread, 0.0)), 0.0)
        intra = jnp.einsum(
            "gjrs,sgje->rgje", products * damping, value_rows, precision=lax.Precision.HIGHEST
        )
        mixed = (inter + intra).reshape(row_count, query_head_rows, head_size)
        scaled = mixed * lax.rsqrt(jnp.mean(mixed * mixed, axis=-1, keepdims=True) + 1e-05)
        gating = spike_counts.astype(jnp.float32).reshape(
            row_count, query_head_rows, head_size
        ) * thresholds.reshape(query_head_rows, head_size)
        return jnp.where(
            valid_rows[:, None],
            (scaled * gating).reshape(row_count, query_head_rows * head_size),
            0.0,
        ).astype(jnp.bfloat16)

    def finish_skip(dummy_arg):
        return jnp.zeros((row_count, query_head_rows * head_size), jnp.bfloat16)

    gated = lax.cond(section_index == 1, linear_finish, finish_skip, 0)
    head_outputs = jnp.where(section_index == 0, attention, gated)[None]
    return (head_outputs, local_activations)


MESH = pl.DeviceIdType.MESH
F32 = jnp.float32
BF16 = jnp.bfloat16
CHUNK = 256
PAD = 16
PIECES = 4


def nt(a, b):
    return lax.dot_general(a, b, (((1,), (1,)), ((), ())), preferred_element_type=F32)


def nn(a, b):
    return jnp.dot(a, b, preferred_element_type=F32)


def turned(x):
    return jnp.transpose(x.astype(F32)).astype(BF16)


def kernel(
    n,
    residual,
    queries,
    keys,
    window_values,
    mixing,
    gain,
    decay_t,
    spikes,
    thresholds,
    lengths,
    head_out,
    hidden_out,
    weights,
    spike_buf,
    kv,
    moved_queries,
    stacked,
    top,
    total,
    blend,
    attention,
    terms,
    own_terms,
    far_terms,
    residuals,
    hidden_buf,
    values_sum,
    square_sum,
    damped,
    faded,
    rest,
    keys_t,
    values,
    states,
    fresh,
    incoming,
    passed,
    mixed,
    gain_row,
    decay_wide,
    weights_sem,
    spike_sem,
    res_sem,
    first_sem,
    first_recv,
    kv_send,
    kv_recv,
    kv_forward,
    att_sem,
    term_own_send,
    term_far_send,
    term_own_recv,
    term_far_recv,
    hid_send,
    hid_recv,
    swap_send,
    swap_recv,
    state_send,
    state_recv,
):
    c = lax.axis_index("ctx")
    s = lax.axis_index("section")
    p = lax.axis_index("tp")
    odd = c % 2
    step_to = 1 - 2 * odd
    partner = c + step_to
    rows = keys.shape[0]
    half = residual.shape[1]
    chunks_half = half // CHUNK
    chunks = 2 * chunks_half
    group = 4
    wide = group * HEAD
    factor = math.log2(math.e) / math.sqrt(HEAD)

    barrier = pltpu.get_barrier_semaphore()
    pl.semaphore_signal(barrier, inc=1, device_id={"section": 1 - s}, device_id_type=MESH)
    pl.semaphore_signal(barrier, inc=1, device_id={"tp": 1 - p}, device_id_type=MESH)
    pl.semaphore_signal(
        barrier, inc=1, device_id={"section": 1 - s, "tp": 1 - p}, device_id_type=MESH
    )
    pl.semaphore_signal(barrier, inc=1, device_id={"ctx": partner}, device_id_type=MESH)
    for k in range(1, n // 2):
        pl.semaphore_signal(
            barrier, inc=1, device_id={"ctx": (c + 2 * k) % n}, device_id_type=MESH
        )

    weights_copy = pltpu.make_async_copy(mixing, weights, weights_sem)
    weights_copy.start()

    own_len = lengths[c]

    @pl.when(s == 0)
    def _():
        kv[0, 0:rows] = keys[:, 0:HEAD]
        value_t = turned(window_values[:, 0:HEAD])
        kv[0, rows : rows + HEAD] = value_t[:, 0:HEAD]
        kv[0, rows + HEAD : rows + 2 * HEAD] = value_t[:, HEAD : 2 * HEAD]
        for h in range(group):
            stacked[h * rows : (h + 1) * rows, :] = queries[:, h * HEAD : (h + 1) * HEAD]

    @pl.when(s == 1)
    def _():
        value_t = turned(window_values[:, HEAD : 2 * HEAD])
        kv[0, rows : rows + HEAD] = value_t[:, 0:HEAD]
        kv[0, rows + HEAD : rows + 2 * HEAD] = value_t[:, HEAD : 2 * HEAD]

    pl.semaphore_wait(barrier, 3 + n // 2)

    key_copy = pltpu.make_async_remote_copy(
        src_ref=keys.at[:, HEAD : 2 * HEAD],
        dst_ref=kv.at[0, 0:rows],
        send_sem=first_sem.at[0],
        recv_sem=first_recv.at[0],
        device_id={"section": 1 - s},
        device_id_type=MESH,
    )
    query_copy = pltpu.make_async_remote_copy(
        src_ref=queries.at[:, wide : 2 * wide],
        dst_ref=moved_queries,
        send_sem=first_sem.at[1],
        recv_sem=first_recv.at[1],
        device_id={"section": 1 - s},
        device_id_type=MESH,
    )
    residual_send = pltpu.make_async_remote_copy(
        src_ref=residual,
        dst_ref=residuals.at[p],
        send_sem=res_sem.at[0],
        recv_sem=res_sem.at[1],
        device_id={"tp": 1 - p},
        device_id_type=MESH,
    )
    residual_recv = pltpu.make_async_remote_copy(
        src_ref=residual,
        dst_ref=residuals.at[1 - p],
        send_sem=res_sem.at[0],
        recv_sem=res_sem.at[1],
        device_id={"tp": 1 - p},
        device_id_type=MESH,
    )
    residual_copy = pltpu.make_async_copy(residual, residuals.at[p], res_sem.at[2])
    spike_copy = pltpu.make_async_copy(spikes, spike_buf, spike_sem)

    @pl.when(s == 0)
    def _():
        key_copy.start()
        query_copy.start()

    @pl.when(s == 1)
    def _():
        residual_send.start()
        residual_copy.start()
        spike_copy.start()
        key_copy.wait_recv()

    def along(k):
        return pltpu.make_async_remote_copy(
            src_ref=kv.at[2 * k],
            dst_ref=kv.at[2 * k + 2],
            send_sem=kv_send.at[k],
            recv_sem=kv_recv.at[2 * k + 2],
            device_id={"ctx": lax.rem(c + 2, n)},
            device_id_type=MESH,
        )

    def across(k):
        return pltpu.make_async_remote_copy(
            src_ref=kv.at[2 * k],
            dst_ref=kv.at[2 * k + step_to],
            send_sem=kv_forward.at[k],
            recv_sem=kv_recv.at[2 * k + step_to],
            device_id={"ctx": partner},
            device_id_type=MESH,
        )

    def arrival(slot):
        return pltpu.make_async_remote_copy(
            src_ref=kv.at[slot],
            dst_ref=kv.at[slot],
            send_sem=kv_send.at[0],
            recv_sem=kv_recv.at[slot],
            device_id={"ctx": partner},
            device_id_type=MESH,
        )

    before = c // 2
    pairs = n // 2

    @pl.when(c + 2 < n)
    def _():
        along(0).start()

    @pl.when(odd == 0)
    def _():
        across(0).start()

    @pl.when(s == 1)
    def _():
        query_copy.wait_recv()
        for h in range(group):
            stacked[h * rows : (h + 1) * rows, :] = moved_queries[:, h * HEAD : (h + 1) * HEAD]

    def attend(slot, first):
        key_rows = kv[slot, 0:rows]
        value_t = jnp.concatenate(
            [kv[slot, rows : rows + HEAD], kv[slot, rows + HEAD : rows + 2 * HEAD]], axis=1
        )
        key_index = lax.broadcasted_iota(jnp.int32, (rows, rows), 0)
        allowed = key_index < lengths[c - slot]
        if first:
            allowed = allowed & (key_index <= lax.broadcasted_iota(jnp.int32, (rows, rows), 1))
        for h in range(group):
            at = slice(h * rows, (h + 1) * rows)
            scores = jnp.where(allowed, nt(key_rows, stacked[at, :]), -1e30)
            best = jnp.max(scores, axis=0, keepdims=True)
            if not first:
                best = jnp.maximum(best, top[:, at])
            part = jnp.exp2((scores - best) * factor)
            part_sum = jnp.sum(part, axis=0, keepdims=True)
            blended = nn(value_t, part.astype(BF16))
            if first:
                total[:, at] = part_sum
                blend[:, at] = blended
            else:
                shrink = jnp.exp2((top[:, at] - best) * factor)
                total[:, at] = total[:, at] * shrink + part_sum
                blend[:, at] = blend[:, at] * shrink + blended
            top[:, at] = best

    attend(0, True)

    def attend_pair(k, carry):
        arrival(2 * k).wait_recv()

        @pl.when(c + 2 < n)
        def _():
            along(k).start()

        across(k).start()
        arrival(2 * k - 1).wait_recv()
        attend(2 * k - 1, False)
        attend(2 * k, False)
        return carry

    lax.fori_loop(1, before + 1, attend_pair, 0)

    @pl.when(odd == 1)
    def _():
        arrival(c).wait_recv()
        attend(c, False)

    row_lane = lax.broadcasted_iota(jnp.int32, (1, rows), 1)
    for h in range(group):
        at = slice(h * rows, (h + 1) * rows)
        scaled = blend[:, at] / jnp.maximum(total[:, at], 1.0)
        scaled = jnp.where(row_lane < own_len, scaled, 0.0)
        attention[s, :, h * HEAD : (h + 1) * HEAD] = jnp.transpose(scaled).astype(BF16)

    att_copy = pltpu.make_async_remote_copy(
        src_ref=attention.at[1],
        dst_ref=attention.at[1],
        send_sem=att_sem.at[0],
        recv_sem=att_sem.at[1],
        device_id={"section": 1 - s},
        device_id_type=MESH,
    )

    def term_own(j):
        return pltpu.make_async_remote_copy(
            src_ref=terms.at[j],
            dst_ref=own_terms.at[j],
            send_sem=term_own_send.at[j],
            recv_sem=term_own_recv.at[j],
            device_id={"section": 1 - s},
            device_id_type=MESH,
        )

    def term_far(j):
        return pltpu.make_async_remote_copy(
            src_ref=terms.at[j],
            dst_ref=far_terms.at[j],
            send_sem=term_far_send.at[j],
            recv_sem=term_far_recv.at[j],
            device_id={"section": 1 - s, "tp": 1 - p},
            device_id_type=MESH,
        )

    def hid(j):
        return pltpu.make_async_remote_copy(
            src_ref=hidden_buf.at[j],
            dst_ref=hidden_out.at[:, pl.ds(pl.multiple_of(j * CHUNK, CHUNK), CHUNK)],
            send_sem=hid_send.at[j],
            recv_sem=hid_recv.at[j],
            device_id={"section": 1 - s},
            device_id_type=MESH,
        )

    def each(count, act):
        def one(j, carry):
            act(j)
            return carry

        lax.fori_loop(0, count, one, 0)

    @pl.when(s == 0)
    def _():
        weights_copy.wait()
        att_copy.wait_recv()

        def project(j, carry):
            at = pl.ds(pl.multiple_of(j * CHUNK, CHUNK), CHUNK)
            both = jnp.concatenate([attention[0], attention[1]], axis=1)
            terms[j] = nn(both, weights[:, at]).astype(BF16)
            term_own(j).start()

            @pl.when(j >= 2)
            def _():
                term_far(j - 2).wait_send()

            term_far(j).start()
            return carry

        lax.fori_loop(0, chunks, project, 0)
        head_out[:, 0:wide] = attention[0]
        head_out[:, wide : 2 * wide] = attention[1]
        term_far(chunks - 2).wait_send()
        term_far(chunks - 1).wait_send()
        each(chunks, lambda j: term_own(j).wait_send())
        key_copy.wait_send()
        query_copy.wait_send()
        each(chunks_half, lambda j: hid(j).wait_recv())

    @pl.when(s == 1)
    def _():
        att_copy.start()
        heads = 2 * group
        row_col = lax.broadcasted_iota(jnp.int32, (rows, 1), 0)
        valid_col = row_col < own_len
        r = lax.broadcasted_iota(jnp.int32, (rows, rows), 0)
        t = lax.broadcasted_iota(jnp.int32, (rows, rows), 1)
        upper = jnp.where(r <= t, 1.0, 0.0)
        decay_wide[...] = jnp.zeros_like(decay_wide)
        decay_wide[0:heads, :] = jnp.where(row_lane < own_len, decay_t[...], 0.0)
        cum_t = jnp.dot(
            decay_wide[...], upper, precision=lax.Precision.HIGHEST, preferred_element_type=F32
        )
        cum = jnp.transpose(cum_t)
        gain_row[...] = gain[...].astype(F32).reshape(1, 2 * half)
        last = cum[rows - 1 : rows, :]
        rest[...] = jnp.exp(last - cum)
        for g in range(2):
            masked = jnp.where(valid_col, keys[:, g * HEAD : (g + 1) * HEAD].astype(F32), 0.0)
            keys_t[g] = jnp.transpose(masked).astype(BF16)
        for h in range(heads):
            at = slice(h * HEAD, (h + 1) * HEAD)
            col = cum[:, h : h + 1]
            row = cum_t[h : h + 1, :]
            query = queries[:, at]
            damping = jnp.where(r >= t, jnp.exp(jnp.minimum(col - row, 0.0)), 0.0)
            damped[h] = (nn(query, keys_t[h // group]) * damping).astype(BF16)
            faded[:, at] = (query.astype(F32) * jnp.exp(col)).astype(BF16)
            sum_row = jnp.broadcast_to(last[:, h : h + 1], (PAD, HEAD))
            high = sum_row.astype(BF16)
            low = sum_row - high.astype(F32)
            in_group = slice((h % group) * HEAD, (h % group + 1) * HEAD)
            states[0, h // group, HEAD : HEAD + PAD, in_group] = jnp.where(
                lax.broadcasted_iota(jnp.int32, (PAD, HEAD), 0) < PAD // 2,
                high.astype(F32),
                low,
            ).astype(BF16)
        values_sum[...] = jnp.zeros_like(values_sum)
        square_sum[...] = jnp.zeros_like(square_sum)
        weights_copy.wait()
        residual_copy.wait()
        residual_recv.wait_recv()

        def collect(j, carry):
            side = j // chunks_half
            col = j - side * chunks_half
            here = pl.ds(pl.multiple_of(col * CHUNK, CHUNK), CHUNK)
            at = pl.ds(pl.multiple_of(j * CHUNK, CHUNK), CHUNK)
            term_own(j).wait_recv()
            term_far(j).wait_recv()
            summed = residuals[side, :, here].astype(F32) + (
                own_terms[j].astype(F32) + far_terms[j].astype(F32)
            )
            narrow = summed.astype(BF16)

            @pl.when(side == p)
            def _():
                hidden_buf[col] = narrow
                hidden_out[:, here] = narrow
                hid(col).start()

            rounded = narrow.astype(F32)
            square_sum[...] += jnp.sum(rounded * rounded, axis=1, keepdims=True)
            ready = (rounded * gain_row[:, at]).astype(BF16)
            values_sum[...] += nt(ready, weights[:, at])
            return carry

        lax.fori_loop(0, chunks, collect, 0)
        scale = lax.rsqrt(square_sum[...] * (1.0 / (2 * half)) + 1e-05)
        values[...] = (values_sum[...] * scale).astype(BF16)
        def swap(g):
            return pltpu.make_async_remote_copy(
                src_ref=states.at[0, g],
                dst_ref=states.at[1, g],
                send_sem=swap_send.at[g],
                recv_sem=swap_recv.at[g],
                device_id={"ctx": partner},
                device_id_type=MESH,
            )

        def onward(k, g):
            return pltpu.make_async_remote_copy(
                src_ref=states.at[2, g],
                dst_ref=states.at[2 + k, g],
                send_sem=state_send.at[k, g],
                recv_sem=state_recv.at[k, g],
                device_id={"ctx": lax.rem(c + 2 * k, n)},
                device_id_type=MESH,
            )

        def sum_of(slot, g):
            rows_of = states[slot, g, HEAD : HEAD + PAD, :].astype(F32)
            return rows_of[0:1, :] + rows_of[PAD // 2 : PAD // 2 + 1, :]

        here_later = pairs - 1 - before
        swap_out = (odd == 0) | (here_later > 0)
        swap_in = (odd == 1) | (here_later > 0)
        for g in range(2):
            for h in range(g * group, (g + 1) * group):
                at = slice(h * HEAD, (h + 1) * HEAD)
                weighted = (values[:, at].astype(F32) * rest[:, h : h + 1]).astype(BF16)
                fresh[:, at] = nn(keys_t[g], weighted)
                in_group = slice((h % group) * HEAD, (h % group + 1) * HEAD)
                states[0, g, 0:HEAD, in_group] = fresh[:, at].astype(BF16)

            @pl.when(swap_out)
            def _():
                swap(g).start()

        for h in range(heads):
            at = slice(h * HEAD, (h + 1) * HEAD)
            mixed[:, at] = nn(damped[h], values[:, at])

        for g in range(2):
            at = slice(g * wide, (g + 1) * wide)

            @pl.when(swap_in)
            def _():
                swap(g).wait_recv()

            @pl.when(here_later > 0)
            def _():
                own_sum = sum_of(0, g)
                other_sum = sum_of(1, g)
                second = jnp.where(odd == 1, own_sum, other_sum)
                own = fresh[:, at]
                other = states[1, g, 0:HEAD, :].astype(F32)
                first_part = jnp.where(odd == 1, other, own)
                second_part = jnp.where(odd == 1, own, other)
                states[2, g, 0:HEAD, :] = (first_part * jnp.exp(second) + second_part).astype(BF16)
                both_sum = jnp.broadcast_to(own_sum + other_sum, (PAD, wide))
                high = both_sum.astype(BF16).astype(F32)
                states[2, g, HEAD : HEAD + PAD, :] = jnp.where(
                    lax.broadcasted_iota(jnp.int32, (PAD, wide), 0) < PAD // 2,
                    high,
                    both_sum - high,
                ).astype(BF16)

                def send_on(k, carry):
                    onward(k, g).start()
                    return carry

                lax.fori_loop(1, here_later + 1, send_on, 0)

        spike_copy.wait()
        for g in range(2):
            at = slice(g * wide, (g + 1) * wide)

            @pl.when(odd == 1)
            def _():
                incoming[:, at] = states[1, g, 0:HEAD, :].astype(F32)
                passed[:, at] = sum_of(1, g)

            @pl.when(odd == 0)
            def _():
                incoming[:, at] = jnp.zeros((HEAD, wide), F32)
                passed[:, at] = jnp.zeros((1, wide), F32)

            def join(k, carry):
                onward(k, g).wait_recv()
                incoming[:, at] += states[2 + k, g, 0:HEAD, :].astype(F32) * jnp.exp(passed[:, at])
                passed[:, at] += sum_of(2 + k, g)
                return carry

            lax.fori_loop(1, before + 1, join, 0)
            for h in range(g * group, (g + 1) * group):
                at = slice(h * HEAD, (h + 1) * HEAD)
                both = mixed[:, at] + nn(faded[:, at], incoming[:, at].astype(BF16))
                scaled = both * lax.rsqrt(jnp.mean(both * both, axis=1, keepdims=True) + 1e-05)
                gated = scaled * (spike_buf[:, at].astype(F32) * thresholds[:, at])
                head_out[:, at] = jnp.where(valid_col, gated, 0.0).astype(BF16)

        for g in range(2):

            @pl.when(swap_out)
            def _():
                swap(g).wait_send()

            def sent_on(k, carry):
                onward(k, g).wait_send()
                return carry

            lax.fori_loop(1, here_later + 1, sent_on, 0)
        each(chunks_half, lambda j: hid(j).wait_send())
        residual_send.wait_send()
        att_copy.wait_send()

    def along_done(k, carry):
        along(k).wait_send()
        return carry

    @pl.when(c + 2 < n)
    def _():
        lax.fori_loop(0, before + 1, along_done, 0)

    @pl.when(odd == 0)
    def _():
        across(0).wait_send()

    def across_done(k, carry):
        across(k).wait_send()
        return carry

    lax.fori_loop(1, before + 1, across_done, 0)


def handed_on(a, b, a_out, b_out, a_buf, b_buf, in_sem, out_sem):
    step = a.shape[0] // PIECES

    def copies(i):
        at = slice(i * step, (i + 1) * step)
        return (
            pltpu.make_async_copy(b.at[at], b_buf.at[at], in_sem.at[0, i]),
            pltpu.make_async_copy(a.at[at], a_buf.at[at], in_sem.at[1, i]),
            pltpu.make_async_copy(b_buf.at[at], b_out.at[at], out_sem.at[0, i]),
            pltpu.make_async_copy(a_buf.at[at], a_out.at[at], out_sem.at[1, i]),
        )

    for i in range(PIECES):
        copies(i)[0].start()
        copies(i)[1].start()
    for i in range(PIECES):
        for k in range(2):
            copies(i)[k].wait()
            copies(i)[k + 2].start()
    for i in range(PIECES):
        copies(i)[2].wait()
        copies(i)[3].wait()


def fused(
    residual,
    queries,
    keys,
    window_values,
    mixing,
    norm_gain,
    log_decay,
    spike_counts,
    thresholds,
    lengths,
):
    n = lax.axis_size("ctx")
    rows, half = residual.shape
    width = queries.shape[2]
    heads = width // HEAD
    chunks = 2 * half // CHUNK
    dma = pltpu.SemaphoreType.DMA
    whole = pl.BlockSpec(memory_space=pltpu.VMEM)
    away = pl.BlockSpec(memory_space=pl.ANY)
    head_outputs, hidden = pl.pallas_call(
        functools.partial(kernel, n),
        out_shape=(
            jax.ShapeDtypeStruct((rows, width), BF16),
            jax.ShapeDtypeStruct((rows, half), BF16),
        ),
        in_specs=[
            away,
            whole,
            whole,
            whole,
            away,
            whole,
            whole,
            away,
            whole,
            pl.BlockSpec(memory_space=pltpu.SMEM),
        ],
        out_specs=(whole, whole),
        scratch_shapes=[
            pltpu.VMEM(mixing.shape[1:], BF16),
            pltpu.VMEM((rows, width), jnp.int32),
            pltpu.VMEM((n, 2 * rows, HEAD), BF16),
            pltpu.VMEM((rows, width // 2), BF16),
            pltpu.VMEM((4 * rows, HEAD), BF16),
            pltpu.VMEM((1, 4 * rows), F32),
            pltpu.VMEM((1, 4 * rows), F32),
            pltpu.VMEM((HEAD, 4 * rows), F32),
            pltpu.VMEM((2, rows, width // 2), BF16),
            pltpu.VMEM((chunks, rows, CHUNK), BF16),
            pltpu.VMEM((chunks, rows, CHUNK), BF16),
            pltpu.VMEM((chunks, rows, CHUNK), BF16),
            pltpu.VMEM((2, rows, half), BF16),
            pltpu.VMEM((chunks // 2, rows, CHUNK), BF16),
            pltpu.VMEM((rows, width), F32),
            pltpu.VMEM((rows, 1), F32),
            pltpu.VMEM((heads, rows, rows), BF16),
            pltpu.VMEM((rows, width), BF16),
            pltpu.VMEM((rows, HEAD), F32),
            pltpu.VMEM((2, HEAD, rows), BF16),
            pltpu.VMEM((rows, width), BF16),
            pltpu.VMEM((n // 2 + 2, 2, HEAD + PAD, width // 2), BF16),
            pltpu.VMEM((HEAD, width), F32),
            pltpu.VMEM((HEAD, width), F32),
            pltpu.VMEM((1, width), F32),
            pltpu.VMEM((rows, width), F32),
            pltpu.VMEM((1, 2 * half), F32),
            pltpu.VMEM((HEAD, rows), F32),
            dma,
            dma,
            dma((3,)),
            dma((2,)),
            dma((2,)),
            dma((n // 2,)),
            dma((n,)),
            dma((n // 2,)),
            dma((2,)),
            dma((chunks,)),
            dma((chunks,)),
            dma((chunks,)),
            dma((chunks,)),
            dma((chunks // 2,)),
            dma((chunks // 2,)),
            dma((2,)),
            dma((2,)),
            dma((n // 2, 2)),
            dma((n // 2, 2)),
        ],
        compiler_params=pltpu.CompilerParams(
            collective_id=0, has_side_effects=True, vmem_limit_bytes=56 * 1024 * 1024
        ),
    )(
        residual,
        queries[0],
        keys[0],
        window_values,
        mixing[0],
        norm_gain,
        log_decay.T,
        spike_counts,
        thresholds.reshape(1, -1),
        lengths,
    )
    head_outputs, hidden = pl.pallas_call(
        handed_on,
        out_shape=(
            jax.ShapeDtypeStruct((rows, width), BF16),
            jax.ShapeDtypeStruct((rows, half), BF16),
        ),
        in_specs=[away, away],
        out_specs=(away, away),
        scratch_shapes=[
            pltpu.VMEM((rows, width), BF16),
            pltpu.VMEM((rows, half), BF16),
            dma((2, PIECES)),
            dma((2, PIECES)),
        ],
        compiler_params=pltpu.CompilerParams(vmem_limit_bytes=60 * 1024 * 1024),
    )(head_outputs, hidden)
    return (head_outputs[None], hidden)


def chosen(*arrays):
    residual, queries, keys = arrays[:3]
    shards = lax.axis_size("ctx")
    rows = residual.shape[0]
    fits = (
        lax.axis_size("tp") == 2
        and lax.axis_size("section") == 2
        and keys.shape[2] == 2 * HEAD
        and queries.shape[2] == 8 * HEAD
        and rows == 2 * HEAD
        and residual.shape[1] % CHUNK == 0
        and shards % 2 == 0
        and shards * rows <= WINDOW
    )
    return fused(*arrays) if fits else body(*arrays)


def solution(mesh):
    return jax.shard_map(
        chosen,
        mesh=mesh,
        in_specs=(
            P("ctx", "tp"),
            P("section", "ctx", "tp"),
            P("section", "ctx", "tp"),
            P("ctx", "tp"),
            P("section", "tp", None),
            P(),
            P("ctx", "tp"),
            P("ctx", "tp"),
            P("tp"),
            P(),
        ),
        out_specs=(P("section", "ctx", "tp"), P("ctx", "tp")),
        check_vma=False,
    )
```

```python
import functools
import math

import jax
import jax.numpy as jnp
from jax import lax
from jax.experimental import pallas as pl
from jax.experimental.pallas import tpu as pltpu
from jax.sharding import PartitionSpec as P

HEAD = 128
WINDOW = 4096


def passed_along(x, axis, by):
    devices = lax.axis_size(axis)
    pairs = [(i, i + by) for i in range(devices) if 0 <= i + by < devices]
    return lax.ppermute(x, axis, pairs)


def entering(x, axis, join, neutral):
    place = lax.axis_index(axis)
    gathered = jax.tree.map(
        lambda a, kind: lax.all_gather(a.astype(kind), axis), x, (jnp.bfloat16, jnp.bfloat16)
    )
    state = jax.tree.map(lambda a, e: jnp.zeros_like(a) + jnp.asarray(e, a.dtype), x, neutral)

    def one(step, state):
        return join(
            state,
            jax.tree.map(
                lambda a, own: lax.dynamic_index_in_dim(a, step, 0, False).astype(own.dtype),
                gathered,
                x,
            ),
        )

    return lax.fori_loop(0, place, one, state)


def body(
    residual,
    queries,
    keys,
    window_values,
    mixing,
    norm_gain,
    log_decay,
    spike_counts,
    thresholds,
    lengths,
):
    section_index = lax.axis_index("section")
    shard_index = lax.axis_index("ctx")
    row_count = keys.shape[1]
    head_size = HEAD
    key_heads = keys.shape[2] // head_size
    query_head_rows = queries.shape[2] // head_size
    group_size = query_head_rows // key_heads
    span_blocks = WINDOW // row_count
    feature_count = mixing.shape[2]
    scale = 1.0 / math.sqrt(head_size)
    positions = jnp.arange(row_count, dtype=jnp.int32)
    valid_rows = positions < lengths[shard_index]
    own_keys = keys[0]
    earlier = [
        passed_along((own_keys, window_values), "ctx", distance + 1)
        for distance in range(span_blocks)
    ]
    key_blocks = jnp.stack([pair[0] for pair in earlier[::-1]] + [own_keys], 0)
    value_blocks = jnp.stack([pair[1] for pair in earlier[::-1]] + [window_values], 0)

    def window_layer(dummy_arg):
        query_rows = queries[0].reshape(row_count, key_heads, group_size, head_size)
        sources = shard_index - span_blocks + jnp.arange(span_blocks + 1, dtype=jnp.int32)
        block_valid = (sources[:, None] >= 0) & (
            positions[None, :] < lengths[jnp.clip(sources, 0, None)][:, None]
        )
        offsets = (span_blocks - jnp.arange(span_blocks + 1, dtype=jnp.int32)) * row_count
        base_distance = positions[:, None] - positions[None, :]

        def weight_step(carry, items):
            running, totals, best = carry
            scores = (
                jnp.einsum(
                    "rgjd,kgd->gjrk",
                    query_rows,
                    items[0].reshape(row_count, key_heads, head_size),
                    preferred_element_type=jnp.float32,
                )
                * scale
            )
            distance = base_distance + items[3]
            allowed = items[2][None, :] & (distance >= 0) & (distance < WINDOW)
            scores = jnp.where(allowed, scores, -1e30)
            new_best = jnp.maximum(best, jnp.max(scores, axis=-1))
            factor = jnp.exp(best - new_best)
            weights = jnp.where(allowed, jnp.exp(scores - new_best[..., None]), 0.0)
            blended = jnp.einsum(
                "gjrk,kgd->gjrd",
                weights.astype(jnp.bfloat16),
                items[1].reshape(row_count, key_heads, head_size),
                preferred_element_type=jnp.float32,
            )
            return (
                (
                    running * factor[..., None] + blended,
                    totals * factor + jnp.sum(weights, axis=-1),
                    new_best,
                ),
                None,
            )

        start_sums = (
            jnp.zeros((key_heads, group_size, row_count, head_size), jnp.float32),
            jnp.zeros((key_heads, group_size, row_count), jnp.float32),
            jnp.full((key_heads, group_size, row_count), -1e30, jnp.float32),
        )
        (blended, totals, unused_best), unused_sum = lax.scan(
            weight_step, start_sums, (key_blocks, value_blocks, block_valid, offsets)
        )
        attention = blended / jnp.maximum(totals, 1.0)[..., None]
        attention = attention.transpose(2, 0, 1, 3).reshape(row_count, query_head_rows * head_size)
        attention = jnp.where(valid_rows[:, None], attention, 0.0).astype(jnp.bfloat16)
        projected = jnp.dot(attention, mixing[0], preferred_element_type=jnp.float32)
        return (attention, projected)

    def window_skip(dummy_arg):
        return (
            jnp.zeros((row_count, query_head_rows * head_size), jnp.bfloat16),
            jnp.zeros((row_count, feature_count), jnp.float32),
        )

    attention, projected = lax.cond(section_index == 0, window_layer, window_skip, 0)
    share = lax.psum_scatter(
        projected.astype(jnp.bfloat16), "tp", scatter_dimension=1, tiled=True
    ).astype(jnp.float32)
    own_hidden = (share + residual.astype(jnp.float32)).astype(jnp.bfloat16)
    moved_share = passed_along(own_hidden, "section", 1)
    local_activations = jnp.where(section_index == 0, own_hidden, moved_share)
    complete_hidden_matrix = lax.all_gather(local_activations, "tp", axis=1, tiled=True)
    masked_keys = jnp.where(valid_rows[:, None], own_keys, jnp.zeros_like(own_keys)).reshape(
        row_count, key_heads, head_size
    )
    wide_keys = masked_keys.astype(jnp.float32)
    decays = log_decay * valid_rows[:, None].astype(jnp.float32)

    def linear_prepare(dummy_arg):
        wide = complete_hidden_matrix.astype(jnp.float32)
        normed = (
            wide
            * lax.rsqrt(jnp.mean(wide * wide, axis=-1, keepdims=True) + 1e-05)
            * norm_gain.astype(jnp.float32)
        ).astype(jnp.bfloat16)
        payload_vectors = lax.dot_general(
            normed, mixing[0], (((1,), (1,)), ((), ())), preferred_element_type=jnp.float32
        ).astype(jnp.bfloat16)
        cumulated = jnp.cumsum(decays, axis=0).reshape(row_count, key_heads, group_size)
        value_rows = payload_vectors.astype(jnp.float32).reshape(
            row_count, key_heads, group_size, head_size
        )
        fresh_state = jnp.einsum(
            "sgd,sgje->gdje",
            wide_keys,
            value_rows * jnp.exp(cumulated[-1] - cumulated)[..., None],
            precision=lax.Precision.HIGHEST,
        )
        return (payload_vectors, cumulated, fresh_state)

    def linear_skip(dummy_arg):
        return (
            jnp.zeros((row_count, query_head_rows * head_size), jnp.bfloat16),
            jnp.zeros((row_count, key_heads, group_size), jnp.float32),
            jnp.zeros((key_heads, head_size, group_size, head_size), jnp.float32),
        )

    payload_vectors, cumulated, fresh_state = lax.cond(
        section_index == 1, linear_prepare, linear_skip, 0
    )

    def chain(previous_entry, latter):
        return (
            previous_entry[0] + latter[0],
            previous_entry[1] * jnp.exp(latter[0])[:, None, :, None] + latter[1],
        )

    identity = (jnp.zeros((key_heads, group_size), jnp.float32), jnp.zeros_like(fresh_state))
    unused_total, incoming = entering((cumulated[-1], fresh_state), "ctx", chain, identity)

    def linear_finish(dummy_arg):
        query_narrow = queries[0].reshape(row_count, key_heads, group_size, head_size)
        query_rows = query_narrow.astype(jnp.float32)
        value_rows = payload_vectors.astype(jnp.float32).reshape(
            row_count, key_heads, group_size, head_size
        )
        inter = (
            jnp.einsum("rgjd,gdje->rgje", query_rows, incoming, precision=lax.Precision.HIGHEST)
            * jnp.exp(cumulated)[..., None]
        )
        products = jnp.einsum(
            "rgjd,sgd->gjrs", query_narrow, masked_keys, preferred_element_type=jnp.float32
        )
        ordered = cumulated.transpose(1, 2, 0)
        spread = ordered[..., :, None] - ordered[..., None, :]
        triangle = positions[:, None] >= positions[None, :]
        damping = jnp.where(triangle, jnp.exp(jnp.minimum(spread, 0.0)), 0.0)
        intra = jnp.einsum(
            "gjrs,sgje->rgje", products * damping, value_rows, precision=lax.Precision.HIGHEST
        )
        mixed = (inter + intra).reshape(row_count, query_head_rows, head_size)
        scaled = mixed * lax.rsqrt(jnp.mean(mixed * mixed, axis=-1, keepdims=True) + 1e-05)
        gating = spike_counts.astype(jnp.float32).reshape(
            row_count, query_head_rows, head_size
        ) * thresholds.reshape(query_head_rows, head_size)
        return jnp.where(
            valid_rows[:, None],
            (scaled * gating).reshape(row_count, query_head_rows * head_size),
            0.0,
        ).astype(jnp.bfloat16)

    def finish_skip(dummy_arg):
        return jnp.zeros((row_count, query_head_rows * head_size), jnp.bfloat16)

    gated = lax.cond(section_index == 1, linear_finish, finish_skip, 0)
    head_outputs = jnp.where(section_index == 0, attention, gated)[None]
    return (head_outputs, local_activations)


MESH = pl.DeviceIdType.MESH
F32 = jnp.float32
BF16 = jnp.bfloat16
CHUNK = 256
PAD = 16
PIECES = 4


def nt(a, b):
    return lax.dot_general(a, b, (((1,), (1,)), ((), ())), preferred_element_type=F32)


def nn(a, b):
    return jnp.dot(a, b, preferred_element_type=F32)


def turned(x):
    return jnp.transpose(x.astype(F32)).astype(BF16)


def kernel(
    n,
    residual,
    queries,
    keys,
    window_values,
    mixing,
    gain,
    decay_t,
    spikes,
    thresholds,
    lengths,
    head_out,
    hidden_out,
    weights,
    spike_buf,
    kv,
    moved_queries,
    stacked,
    top,
    total,
    blend,
    attention,
    terms,
    own_terms,
    far_terms,
    residuals,
    hidden_buf,
    values_sum,
    square_sum,
    damped,
    faded,
    rest,
    keys_t,
    values,
    states,
    fresh,
    incoming,
    passed,
    mixed,
    gain_row,
    decay_wide,
    weights_sem,
    spike_sem,
    res_sem,
    first_sem,
    first_recv,
    kv_send,
    kv_recv,
    kv_forward,
    att_sem,
    term_own_send,
    term_far_send,
    term_own_recv,
    term_far_recv,
    hid_send,
    hid_recv,
    swap_send,
    swap_recv,
    state_send,
    state_recv,
):
    c = lax.axis_index("ctx")
    s = lax.axis_index("section")
    p = lax.axis_index("tp")
    odd = c % 2
    step_to = 1 - 2 * odd
    partner = c + step_to
    rows = keys.shape[0]
    half = residual.shape[1]
    chunks_half = half // CHUNK
    chunks = 2 * chunks_half
    group = 4
    wide = group * HEAD
    factor = math.log2(math.e) / math.sqrt(HEAD)

    barrier = pltpu.get_barrier_semaphore()
    pl.semaphore_signal(barrier, inc=1, device_id={"section": 1 - s}, device_id_type=MESH)
    pl.semaphore_signal(barrier, inc=1, device_id={"tp": 1 - p}, device_id_type=MESH)
    pl.semaphore_signal(
        barrier, inc=1, device_id={"section": 1 - s, "tp": 1 - p}, device_id_type=MESH
    )
    pl.semaphore_signal(barrier, inc=1, device_id={"ctx": partner}, device_id_type=MESH)
    for k in range(1, n // 2):
        pl.semaphore_signal(
            barrier, inc=1, device_id={"ctx": (c + 2 * k) % n}, device_id_type=MESH
        )

    weights_copy = pltpu.make_async_copy(mixing, weights, weights_sem)
    weights_copy.start()

    own_len = lengths[c]

    @pl.when(s == 0)
    def _():
        kv[0, 0:rows] = keys[:, 0:HEAD]
        value_t = turned(window_values[:, 0:HEAD])
        kv[0, rows : rows + HEAD] = value_t[:, 0:HEAD]
        kv[0, rows + HEAD : rows + 2 * HEAD] = value_t[:, HEAD : 2 * HEAD]
        for h in range(group):
            stacked[h * rows : (h + 1) * rows, :] = queries[:, h * HEAD : (h + 1) * HEAD]

    @pl.when(s == 1)
    def _():
        value_t = turned(window_values[:, HEAD : 2 * HEAD])
        kv[0, rows : rows + HEAD] = value_t[:, 0:HEAD]
        kv[0, rows + HEAD : rows + 2 * HEAD] = value_t[:, HEAD : 2 * HEAD]

    pl.semaphore_wait(barrier, 3 + n // 2)

    key_copy = pltpu.make_async_remote_copy(
        src_ref=keys.at[:, HEAD : 2 * HEAD],
        dst_ref=kv.at[0, 0:rows],
        send_sem=first_sem.at[0],
        recv_sem=first_recv.at[0],
        device_id={"section": 1 - s},
        device_id_type=MESH,
    )
    query_copy = pltpu.make_async_remote_copy(
        src_ref=queries.at[:, wide : 2 * wide],
        dst_ref=moved_queries,
        send_sem=first_sem.at[1],
        recv_sem=first_recv.at[1],
        device_id={"section": 1 - s},
        device_id_type=MESH,
    )
    residual_send = pltpu.make_async_remote_copy(
        src_ref=residual,
        dst_ref=residuals.at[p],
        send_sem=res_sem.at[0],
        recv_sem=res_sem.at[1],
        device_id={"tp": 1 - p},
        device_id_type=MESH,
    )
    residual_recv = pltpu.make_async_remote_copy(
        src_ref=residual,
        dst_ref=residuals.at[1 - p],
        send_sem=res_sem.at[0],
        recv_sem=res_sem.at[1],
        device_id={"tp": 1 - p},
        device_id_type=MESH,
    )
    residual_copy = pltpu.make_async_copy(residual, residuals.at[p], res_sem.at[2])
    spike_copy = pltpu.make_async_copy(spikes, spike_buf, spike_sem)

    @pl.when(s == 0)
    def _():
        key_copy.start()
        query_copy.start()

    @pl.when(s == 1)
    def _():
        residual_send.start()
        residual_copy.start()
        spike_copy.start()
        key_copy.wait_recv()

    def along(k):
        return pltpu.make_async_remote_copy(
            src_ref=kv.at[2 * k],
            dst_ref=kv.at[2 * k + 2],
            send_sem=kv_send.at[k],
            recv_sem=kv_recv.at[2 * k + 2],
            device_id={"ctx": lax.rem(c + 2, n)},
            device_id_type=MESH,
        )

    def across(k):
        return pltpu.make_async_remote_copy(
            src_ref=kv.at[2 * k],
            dst_ref=kv.at[2 * k + step_to],
            send_sem=kv_forward.at[k],
            recv_sem=kv_recv.at[2 * k + step_to],
            device_id={"ctx": partner},
            device_id_type=MESH,
        )

    def arrival(slot):
        return pltpu.make_async_remote_copy(
            src_ref=kv.at[slot],
            dst_ref=kv.at[slot],
            send_sem=kv_send.at[0],
            recv_sem=kv_recv.at[slot],
            device_id={"ctx": partner},
            device_id_type=MESH,
        )

    before = c // 2
    pairs = n // 2

    @pl.when(c + 2 < n)
    def _():
        along(0).start()

    @pl.when(odd == 0)
    def _():
        across(0).start()

    @pl.when(s == 1)
    def _():
        query_copy.wait_recv()
        for h in range(group):
            stacked[h * rows : (h + 1) * rows, :] = moved_queries[:, h * HEAD : (h + 1) * HEAD]

    def attend(slot, first):
        key_rows = kv[slot, 0:rows]
        value_t = jnp.concatenate(
            [kv[slot, rows : rows + HEAD], kv[slot, rows + HEAD : rows + 2 * HEAD]], axis=1
        )
        key_index = lax.broadcasted_iota(jnp.int32, (rows, rows), 0)
        allowed = key_index < lengths[c - slot]
        if first:
            allowed = allowed & (key_index <= lax.broadcasted_iota(jnp.int32, (rows, rows), 1))
        spans = [slice(h * rows, (h + 1) * rows) for h in range(group)]
        scores = [jnp.where(allowed, nt(key_rows, stacked[at, :]), -1e30) for at in spans]
        best = [jnp.max(x, axis=0, keepdims=True) for x in scores]
        if not first:
            best = [jnp.maximum(x, top[:, at]) for x, at in zip(best, spans)]
        parts = [jnp.exp2((x - b) * factor) for x, b in zip(scores, best)]
        blended = [nn(value_t, x.astype(BF16)) for x in parts]
        sums = [jnp.sum(x, axis=0, keepdims=True) for x in parts]
        for h, at in enumerate(spans):
            if first:
                total[:, at] = sums[h]
                blend[:, at] = blended[h]
            else:
                shrink = jnp.exp2((top[:, at] - best[h]) * factor)
                total[:, at] = total[:, at] * shrink + sums[h]
                blend[:, at] = blend[:, at] * shrink + blended[h]
            top[:, at] = best[h]

    attend(0, True)

    def attend_pair(k, carry):
        arrival(2 * k).wait_recv()

        @pl.when(c + 2 < n)
        def _():
            along(k).start()

        across(k).start()
        attend(2 * k, False)
        behind = 2 * k - 3 + 2 * odd

        @pl.when(behind > 0)
        def _():
            arrival(behind).wait_recv()
            attend(behind, False)

        return carry

    lax.fori_loop(1, before + 1, attend_pair, 0)
    rest_slot = 2 * before - 1 + 2 * odd

    @pl.when(rest_slot > 0)
    def _():
        arrival(rest_slot).wait_recv()
        attend(rest_slot, False)

    row_lane = lax.broadcasted_iota(jnp.int32, (1, rows), 1)
    for h in range(group):
        at = slice(h * rows, (h + 1) * rows)
        scaled = blend[:, at] / jnp.maximum(total[:, at], 1.0)
        scaled = jnp.where(row_lane < own_len, scaled, 0.0)
        attention[s, :, h * HEAD : (h + 1) * HEAD] = jnp.transpose(scaled).astype(BF16)

    att_copy = pltpu.make_async_remote_copy(
        src_ref=attention.at[1],
        dst_ref=attention.at[1],
        send_sem=att_sem.at[0],
        recv_sem=att_sem.at[1],
        device_id={"section": 1 - s},
        device_id_type=MESH,
    )

    def term_own(j):
        return pltpu.make_async_remote_copy(
            src_ref=terms.at[j],
            dst_ref=own_terms.at[j],
            send_sem=term_own_send.at[j],
            recv_sem=term_own_recv.at[j],
            device_id={"section": 1 - s},
            device_id_type=MESH,
        )

    def term_far(j):
        return pltpu.make_async_remote_copy(
            src_ref=terms.at[j],
            dst_ref=far_terms.at[j],
            send_sem=term_far_send.at[j],
            recv_sem=term_far_recv.at[j],
            device_id={"section": 1 - s, "tp": 1 - p},
            device_id_type=MESH,
        )

    def hid(j):
        return pltpu.make_async_remote_copy(
            src_ref=hidden_buf.at[j],
            dst_ref=hidden_out.at[:, pl.ds(pl.multiple_of(j * CHUNK, CHUNK), CHUNK)],
            send_sem=hid_send.at[j],
            recv_sem=hid_recv.at[j],
            device_id={"section": 1 - s},
            device_id_type=MESH,
        )

    def each(count, act):
        def one(j, carry):
            act(j)
            return carry

        lax.fori_loop(0, count, one, 0)

    @pl.when(s == 0)
    def _():
        weights_copy.wait()
        att_copy.wait_recv()

        def project(j, carry):
            at = pl.ds(pl.multiple_of(j * CHUNK, CHUNK), CHUNK)
            both = jnp.concatenate([attention[0], attention[1]], axis=1)
            terms[j] = nn(both, weights[:, at]).astype(BF16)
            term_own(j).start()

            @pl.when(j >= 2)
            def _():
                term_far(j - 2).wait_send()

            term_far(j).start()
            return carry

        lax.fori_loop(0, chunks, project, 0)
        head_out[:, 0:wide] = attention[0]
        head_out[:, wide : 2 * wide] = attention[1]
        term_far(chunks - 2).wait_send()
        term_far(chunks - 1).wait_send()
        each(chunks, lambda j: term_own(j).wait_send())
        key_copy.wait_send()
        query_copy.wait_send()
        each(chunks_half, lambda j: hid(j).wait_recv())

    @pl.when(s == 1)
    def _():
        att_copy.start()
        heads = 2 * group
        row_col = lax.broadcasted_iota(jnp.int32, (rows, 1), 0)
        valid_col = row_col < own_len
        r = lax.broadcasted_iota(jnp.int32, (rows, rows), 0)
        t = lax.broadcasted_iota(jnp.int32, (rows, rows), 1)
        upper = jnp.where(r <= t, 1.0, 0.0)
        decay_wide[...] = jnp.zeros_like(decay_wide)
        decay_wide[0:heads, :] = jnp.where(row_lane < own_len, decay_t[...], 0.0)
        cum_t = jnp.dot(
            decay_wide[...], upper, precision=lax.Precision.HIGHEST, preferred_element_type=F32
        )
        cum = jnp.transpose(cum_t)
        gain_row[...] = gain[...].astype(F32).reshape(1, 2 * half)
        last = cum[rows - 1 : rows, :]
        rest[...] = jnp.exp(last - cum)
        for g in range(2):
            masked = jnp.where(valid_col, keys[:, g * HEAD : (g + 1) * HEAD].astype(F32), 0.0)
            keys_t[g] = jnp.transpose(masked).astype(BF16)
        for h in range(heads):
            at = slice(h * HEAD, (h + 1) * HEAD)
            col = cum[:, h : h + 1]
            row = cum_t[h : h + 1, :]
            query = queries[:, at]
            damping = jnp.where(r >= t, jnp.exp(jnp.minimum(col - row, 0.0)), 0.0)
            damped[h] = (nn(query, keys_t[h // group]) * damping).astype(BF16)
            faded[:, at] = (query.astype(F32) * jnp.exp(col)).astype(BF16)
            sum_row = jnp.broadcast_to(last[:, h : h + 1], (PAD, HEAD))
            high = sum_row.astype(BF16)
            low = sum_row - high.astype(F32)
            in_group = slice((h % group) * HEAD, (h % group + 1) * HEAD)
            states[0, h // group, HEAD : HEAD + PAD, in_group] = jnp.where(
                lax.broadcasted_iota(jnp.int32, (PAD, HEAD), 0) < PAD // 2,
                high.astype(F32),
                low,
            ).astype(BF16)
        values_sum[...] = jnp.zeros_like(values_sum)
        square_sum[...] = jnp.zeros_like(square_sum)
        weights_copy.wait()
        residual_copy.wait()
        residual_recv.wait_recv()

        def collect(j, carry):
            side = j // chunks_half
            col = j - side * chunks_half
            here = pl.ds(pl.multiple_of(col * CHUNK, CHUNK), CHUNK)
            at = pl.ds(pl.multiple_of(j * CHUNK, CHUNK), CHUNK)
            term_own(j).wait_recv()
            term_far(j).wait_recv()
            summed = residuals[side, :, here].astype(F32) + (
                own_terms[j].astype(F32) + far_terms[j].astype(F32)
            )
            narrow = summed.astype(BF16)

            @pl.when(side == p)
            def _():
                hidden_buf[col] = narrow
                hidden_out[:, here] = narrow
                hid(col).start()

            rounded = narrow.astype(F32)
            square_sum[...] += jnp.sum(rounded * rounded, axis=1, keepdims=True)
            ready = (rounded * gain_row[:, at]).astype(BF16)
            values_sum[...] += nt(ready, weights[:, at])
            return carry

        lax.fori_loop(0, chunks, collect, 0)
        scale = lax.rsqrt(square_sum[...] * (1.0 / (2 * half)) + 1e-05)
        values[...] = (values_sum[...] * scale).astype(BF16)
        def swap(g):
            return pltpu.make_async_remote_copy(
                src_ref=states.at[0, g],
                dst_ref=states.at[1, g],
                send_sem=swap_send.at[g],
                recv_sem=swap_recv.at[g],
                device_id={"ctx": partner},
                device_id_type=MESH,
            )

        def onward(k, g):
            return pltpu.make_async_remote_copy(
                src_ref=states.at[2, g],
                dst_ref=states.at[2 + k, g],
                send_sem=state_send.at[k, g],
                recv_sem=state_recv.at[k, g],
                device_id={"ctx": lax.rem(c + 2 * k, n)},
                device_id_type=MESH,
            )

        def sum_of(slot, g):
            rows_of = states[slot, g, HEAD : HEAD + PAD, :].astype(F32)
            return rows_of[0:1, :] + rows_of[PAD // 2 : PAD // 2 + 1, :]

        here_later = pairs - 1 - before
        swap_out = (odd == 0) | (here_later > 0)
        swap_in = (odd == 1) | (here_later > 0)
        for g in range(2):
            for h in range(g * group, (g + 1) * group):
                at = slice(h * HEAD, (h + 1) * HEAD)
                weighted = (values[:, at].astype(F32) * rest[:, h : h + 1]).astype(BF16)
                fresh[:, at] = nn(keys_t[g], weighted)
                in_group = slice((h % group) * HEAD, (h % group + 1) * HEAD)
                states[0, g, 0:HEAD, in_group] = fresh[:, at].astype(BF16)

            @pl.when(swap_out)
            def _():
                swap(g).start()

        for h in range(heads):
            at = slice(h * HEAD, (h + 1) * HEAD)
            mixed[:, at] = nn(damped[h], values[:, at])

        for g in range(2):
            at = slice(g * wide, (g + 1) * wide)

            @pl.when(swap_in)
            def _():
                swap(g).wait_recv()

            @pl.when(here_later > 0)
            def _():
                own_sum = sum_of(0, g)
                other_sum = sum_of(1, g)
                second = jnp.where(odd == 1, own_sum, other_sum)
                own = fresh[:, at]
                other = states[1, g, 0:HEAD, :].astype(F32)
                first_part = jnp.where(odd == 1, other, own)
                second_part = jnp.where(odd == 1, own, other)
                states[2, g, 0:HEAD, :] = (first_part * jnp.exp(second) + second_part).astype(BF16)
                both_sum = jnp.broadcast_to(own_sum + other_sum, (PAD, wide))
                high = both_sum.astype(BF16).astype(F32)
                states[2, g, HEAD : HEAD + PAD, :] = jnp.where(
                    lax.broadcasted_iota(jnp.int32, (PAD, wide), 0) < PAD // 2,
                    high,
                    both_sum - high,
                ).astype(BF16)

                def send_on(k, carry):
                    onward(k, g).start()
                    return carry

                lax.fori_loop(1, here_later + 1, send_on, 0)

        spike_copy.wait()
        for g in range(2):
            at = slice(g * wide, (g + 1) * wide)

            @pl.when(odd == 1)
            def _():
                incoming[:, at] = states[1, g, 0:HEAD, :].astype(F32)
                passed[:, at] = sum_of(1, g)

            @pl.when(odd == 0)
            def _():
                incoming[:, at] = jnp.zeros((HEAD, wide), F32)
                passed[:, at] = jnp.zeros((1, wide), F32)

            def join(k, carry):
                onward(k, g).wait_recv()
                incoming[:, at] += states[2 + k, g, 0:HEAD, :].astype(F32) * jnp.exp(passed[:, at])
                passed[:, at] += sum_of(2 + k, g)
                return carry

            lax.fori_loop(1, before + 1, join, 0)
            for h in range(g * group, (g + 1) * group):
                at = slice(h * HEAD, (h + 1) * HEAD)
                both = mixed[:, at] + nn(faded[:, at], incoming[:, at].astype(BF16))
                scaled = both * lax.rsqrt(jnp.mean(both * both, axis=1, keepdims=True) + 1e-05)
                gated = scaled * (spike_buf[:, at].astype(F32) * thresholds[:, at])
                head_out[:, at] = jnp.where(valid_col, gated, 0.0).astype(BF16)

        for g in range(2):

            @pl.when(swap_out)
            def _():
                swap(g).wait_send()

            def sent_on(k, carry):
                onward(k, g).wait_send()
                return carry

            lax.fori_loop(1, here_later + 1, sent_on, 0)
        each(chunks_half, lambda j: hid(j).wait_send())
        residual_send.wait_send()
        att_copy.wait_send()

    def along_done(k, carry):
        along(k).wait_send()
        return carry

    @pl.when(c + 2 < n)
    def _():
        lax.fori_loop(0, before + 1, along_done, 0)

    @pl.when(odd == 0)
    def _():
        across(0).wait_send()

    def across_done(k, carry):
        across(k).wait_send()
        return carry

    lax.fori_loop(1, before + 1, across_done, 0)


def handed_on(a, b, a_out, b_out, a_buf, b_buf, in_sem, out_sem):
    step = a.shape[0] // PIECES

    def copies(i):
        at = slice(i * step, (i + 1) * step)
        return (
            pltpu.make_async_copy(b.at[at], b_buf.at[at], in_sem.at[0, i]),
            pltpu.make_async_copy(a.at[at], a_buf.at[at], in_sem.at[1, i]),
            pltpu.make_async_copy(b_buf.at[at], b_out.at[at], out_sem.at[0, i]),
            pltpu.make_async_copy(a_buf.at[at], a_out.at[at], out_sem.at[1, i]),
        )

    for i in range(PIECES):
        copies(i)[0].start()
        copies(i)[1].start()
    for i in range(PIECES):
        for k in range(2):
            copies(i)[k].wait()
            copies(i)[k + 2].start()
    for i in range(PIECES):
        copies(i)[2].wait()
        copies(i)[3].wait()


def fused(
    residual,
    queries,
    keys,
    window_values,
    mixing,
    norm_gain,
    log_decay,
    spike_counts,
    thresholds,
    lengths,
):
    n = lax.axis_size("ctx")
    rows, half = residual.shape
    width = queries.shape[2]
    heads = width // HEAD
    chunks = 2 * half // CHUNK
    dma = pltpu.SemaphoreType.DMA
    whole = pl.BlockSpec(memory_space=pltpu.VMEM)
    away = pl.BlockSpec(memory_space=pl.ANY)
    head_outputs, hidden = pl.pallas_call(
        functools.partial(kernel, n),
        out_shape=(
            jax.ShapeDtypeStruct((rows, width), BF16),
            jax.ShapeDtypeStruct((rows, half), BF16),
        ),
        in_specs=[
            away,
            whole,
            whole,
            whole,
            away,
            whole,
            whole,
            away,
            whole,
            pl.BlockSpec(memory_space=pltpu.SMEM),
        ],
        out_specs=(whole, whole),
        scratch_shapes=[
            pltpu.VMEM(mixing.shape[1:], BF16),
            pltpu.VMEM((rows, width), jnp.int32),
            pltpu.VMEM((n, 2 * rows, HEAD), BF16),
            pltpu.VMEM((rows, width // 2), BF16),
            pltpu.VMEM((4 * rows, HEAD), BF16),
            pltpu.VMEM((1, 4 * rows), F32),
            pltpu.VMEM((1, 4 * rows), F32),
            pltpu.VMEM((HEAD, 4 * rows), F32),
            pltpu.VMEM((2, rows, width // 2), BF16),
            pltpu.VMEM((chunks, rows, CHUNK), BF16),
            pltpu.VMEM((chunks, rows, CHUNK), BF16),
            pltpu.VMEM((chunks, rows, CHUNK), BF16),
            pltpu.VMEM((2, rows, half), BF16),
            pltpu.VMEM((chunks // 2, rows, CHUNK), BF16),
            pltpu.VMEM((rows, width), F32),
            pltpu.VMEM((rows, 1), F32),
            pltpu.VMEM((heads, rows, rows), BF16),
            pltpu.VMEM((rows, width), BF16),
            pltpu.VMEM((rows, HEAD), F32),
            pltpu.VMEM((2, HEAD, rows), BF16),
            pltpu.VMEM((rows, width), BF16),
            pltpu.VMEM((n // 2 + 2, 2, HEAD + PAD, width // 2), BF16),
            pltpu.VMEM((HEAD, width), F32),
            pltpu.VMEM((HEAD, width), F32),
            pltpu.VMEM((1, width), F32),
            pltpu.VMEM((rows, width), F32),
            pltpu.VMEM((1, 2 * half), F32),
            pltpu.VMEM((HEAD, rows), F32),
            dma,
            dma,
            dma((3,)),
            dma((2,)),
            dma((2,)),
            dma((n // 2,)),
            dma((n,)),
            dma((n // 2,)),
            dma((2,)),
            dma((chunks,)),
            dma((chunks,)),
            dma((chunks,)),
            dma((chunks,)),
            dma((chunks // 2,)),
            dma((chunks // 2,)),
            dma((2,)),
            dma((2,)),
            dma((n // 2, 2)),
            dma((n // 2, 2)),
        ],
        compiler_params=pltpu.CompilerParams(
            collective_id=0, has_side_effects=True, vmem_limit_bytes=56 * 1024 * 1024
        ),
    )(
        residual,
        queries[0],
        keys[0],
        window_values,
        mixing[0],
        norm_gain,
        log_decay.T,
        spike_counts,
        thresholds.reshape(1, -1),
        lengths,
    )
    head_outputs, hidden = pl.pallas_call(
        handed_on,
        out_shape=(
            jax.ShapeDtypeStruct((rows, width), BF16),
            jax.ShapeDtypeStruct((rows, half), BF16),
        ),
        in_specs=[away, away],
        out_specs=(away, away),
        scratch_shapes=[
            pltpu.VMEM((rows, width), BF16),
            pltpu.VMEM((rows, half), BF16),
            dma((2, PIECES)),
            dma((2, PIECES)),
        ],
        compiler_params=pltpu.CompilerParams(vmem_limit_bytes=60 * 1024 * 1024),
    )(head_outputs, hidden)
    return (head_outputs[None], hidden)


def chosen(*arrays):
    residual, queries, keys = arrays[:3]
    shards = lax.axis_size("ctx")
    rows = residual.shape[0]
    fits = (
        lax.axis_size("tp") == 2
        and lax.axis_size("section") == 2
        and keys.shape[2] == 2 * HEAD
        and queries.shape[2] == 8 * HEAD
        and rows == 2 * HEAD
        and residual.shape[1] % CHUNK == 0
        and shards % 2 == 0
        and shards * rows <= WINDOW
    )
    return fused(*arrays) if fits else body(*arrays)


def solution(mesh):
    return jax.shard_map(
        chosen,
        mesh=mesh,
        in_specs=(
            P("ctx", "tp"),
            P("section", "ctx", "tp"),
            P("section", "ctx", "tp"),
            P("ctx", "tp"),
            P("section", "tp", None),
            P(),
            P("ctx", "tp"),
            P("ctx", "tp"),
            P("tp"),
            P(),
        ),
        out_specs=(P("section", "ctx", "tp"), P("ctx", "tp")),
        check_vma=False,
    )
```

```python
import functools
import math

import jax
import jax.numpy as jnp
from jax import lax
from jax.experimental import pallas as pl
from jax.experimental.pallas import tpu as pltpu
from jax.sharding import PartitionSpec as P

HEAD = 128
WINDOW = 4096


def passed_along(x, axis, by):
    devices = lax.axis_size(axis)
    pairs = [(i, i + by) for i in range(devices) if 0 <= i + by < devices]
    return lax.ppermute(x, axis, pairs)


def entering(x, axis, join, neutral):
    place = lax.axis_index(axis)
    gathered = jax.tree.map(
        lambda a, kind: lax.all_gather(a.astype(kind), axis), x, (jnp.bfloat16, jnp.bfloat16)
    )
    state = jax.tree.map(lambda a, e: jnp.zeros_like(a) + jnp.asarray(e, a.dtype), x, neutral)

    def one(step, state):
        return join(
            state,
            jax.tree.map(
                lambda a, own: lax.dynamic_index_in_dim(a, step, 0, False).astype(own.dtype),
                gathered,
                x,
            ),
        )

    return lax.fori_loop(0, place, one, state)


def body(
    residual,
    queries,
    keys,
    window_values,
    mixing,
    norm_gain,
    log_decay,
    spike_counts,
    thresholds,
    lengths,
):
    section_index = lax.axis_index("section")
    shard_index = lax.axis_index("ctx")
    row_count = keys.shape[1]
    head_size = HEAD
    key_heads = keys.shape[2] // head_size
    query_head_rows = queries.shape[2] // head_size
    group_size = query_head_rows // key_heads
    span_blocks = WINDOW // row_count
    feature_count = mixing.shape[2]
    scale = 1.0 / math.sqrt(head_size)
    positions = jnp.arange(row_count, dtype=jnp.int32)
    valid_rows = positions < lengths[shard_index]
    own_keys = keys[0]
    earlier = [
        passed_along((own_keys, window_values), "ctx", distance + 1)
        for distance in range(span_blocks)
    ]
    key_blocks = jnp.stack([pair[0] for pair in earlier[::-1]] + [own_keys], 0)
    value_blocks = jnp.stack([pair[1] for pair in earlier[::-1]] + [window_values], 0)

    def window_layer(dummy_arg):
        query_rows = queries[0].reshape(row_count, key_heads, group_size, head_size)
        sources = shard_index - span_blocks + jnp.arange(span_blocks + 1, dtype=jnp.int32)
        block_valid = (sources[:, None] >= 0) & (
            positions[None, :] < lengths[jnp.clip(sources, 0, None)][:, None]
        )
        offsets = (span_blocks - jnp.arange(span_blocks + 1, dtype=jnp.int32)) * row_count
        base_distance = positions[:, None] - positions[None, :]

        def weight_step(carry, items):
            running, totals, best = carry
            scores = (
                jnp.einsum(
                    "rgjd,kgd->gjrk",
                    query_rows,
                    items[0].reshape(row_count, key_heads, head_size),
                    preferred_element_type=jnp.float32,
                )
                * scale
            )
            distance = base_distance + items[3]
            allowed = items[2][None, :] & (distance >= 0) & (distance < WINDOW)
            scores = jnp.where(allowed, scores, -1e30)
            new_best = jnp.maximum(best, jnp.max(scores, axis=-1))
            factor = jnp.exp(best - new_best)
            weights = jnp.where(allowed, jnp.exp(scores - new_best[..., None]), 0.0)
            blended = jnp.einsum(
                "gjrk,kgd->gjrd",
                weights.astype(jnp.bfloat16),
                items[1].reshape(row_count, key_heads, head_size),
                preferred_element_type=jnp.float32,
            )
            return (
                (
                    running * factor[..., None] + blended,
                    totals * factor + jnp.sum(weights, axis=-1),
                    new_best,
                ),
                None,
            )

        start_sums = (
            jnp.zeros((key_heads, group_size, row_count, head_size), jnp.float32),
            jnp.zeros((key_heads, group_size, row_count), jnp.float32),
            jnp.full((key_heads, group_size, row_count), -1e30, jnp.float32),
        )
        (blended, totals, unused_best), unused_sum = lax.scan(
            weight_step, start_sums, (key_blocks, value_blocks, block_valid, offsets)
        )
        attention = blended / jnp.maximum(totals, 1.0)[..., None]
        attention = attention.transpose(2, 0, 1, 3).reshape(row_count, query_head_rows * head_size)
        attention = jnp.where(valid_rows[:, None], attention, 0.0).astype(jnp.bfloat16)
        projected = jnp.dot(attention, mixing[0], preferred_element_type=jnp.float32)
        return (attention, projected)

    def window_skip(dummy_arg):
        return (
            jnp.zeros((row_count, query_head_rows * head_size), jnp.bfloat16),
            jnp.zeros((row_count, feature_count), jnp.float32),
        )

    attention, projected = lax.cond(section_index == 0, window_layer, window_skip, 0)
    share = lax.psum_scatter(
        projected.astype(jnp.bfloat16), "tp", scatter_dimension=1, tiled=True
    ).astype(jnp.float32)
    own_hidden = (share + residual.astype(jnp.float32)).astype(jnp.bfloat16)
    moved_share = passed_along(own_hidden, "section", 1)
    local_activations = jnp.where(section_index == 0, own_hidden, moved_share)
    complete_hidden_matrix = lax.all_gather(local_activations, "tp", axis=1, tiled=True)
    masked_keys = jnp.where(valid_rows[:, None], own_keys, jnp.zeros_like(own_keys)).reshape(
        row_count, key_heads, head_size
    )
    wide_keys = masked_keys.astype(jnp.float32)
    decays = log_decay * valid_rows[:, None].astype(jnp.float32)

    def linear_prepare(dummy_arg):
        wide = complete_hidden_matrix.astype(jnp.float32)
        normed = (
            wide
            * lax.rsqrt(jnp.mean(wide * wide, axis=-1, keepdims=True) + 1e-05)
            * norm_gain.astype(jnp.float32)
        ).astype(jnp.bfloat16)
        payload_vectors = lax.dot_general(
            normed, mixing[0], (((1,), (1,)), ((), ())), preferred_element_type=jnp.float32
        ).astype(jnp.bfloat16)
        cumulated = jnp.cumsum(decays, axis=0).reshape(row_count, key_heads, group_size)
        value_rows = payload_vectors.astype(jnp.float32).reshape(
            row_count, key_heads, group_size, head_size
        )
        fresh_state = jnp.einsum(
            "sgd,sgje->gdje",
            wide_keys,
            value_rows * jnp.exp(cumulated[-1] - cumulated)[..., None],
            precision=lax.Precision.HIGHEST,
        )
        return (payload_vectors, cumulated, fresh_state)

    def linear_skip(dummy_arg):
        return (
            jnp.zeros((row_count, query_head_rows * head_size), jnp.bfloat16),
            jnp.zeros((row_count, key_heads, group_size), jnp.float32),
            jnp.zeros((key_heads, head_size, group_size, head_size), jnp.float32),
        )

    payload_vectors, cumulated, fresh_state = lax.cond(
        section_index == 1, linear_prepare, linear_skip, 0
    )

    def chain(previous_entry, latter):
        return (
            previous_entry[0] + latter[0],
            previous_entry[1] * jnp.exp(latter[0])[:, None, :, None] + latter[1],
        )

    identity = (jnp.zeros((key_heads, group_size), jnp.float32), jnp.zeros_like(fresh_state))
    unused_total, incoming = entering((cumulated[-1], fresh_state), "ctx", chain, identity)

    def linear_finish(dummy_arg):
        query_narrow = queries[0].reshape(row_count, key_heads, group_size, head_size)
        query_rows = query_narrow.astype(jnp.float32)
        value_rows = payload_vectors.astype(jnp.float32).reshape(
            row_count, key_heads, group_size, head_size
        )
        inter = (
            jnp.einsum("rgjd,gdje->rgje", query_rows, incoming, precision=lax.Precision.HIGHEST)
            * jnp.exp(cumulated)[..., None]
        )
        products = jnp.einsum(
            "rgjd,sgd->gjrs", query_narrow, masked_keys, preferred_element_type=jnp.float32
        )
        ordered = cumulated.transpose(1, 2, 0)
        spread = ordered[..., :, None] - ordered[..., None, :]
        triangle = positions[:, None] >= positions[None, :]
        damping = jnp.where(triangle, jnp.exp(jnp.minimum(spread, 0.0)), 0.0)
        intra = jnp.einsum(
            "gjrs,sgje->rgje", products * damping, value_rows, precision=lax.Precision.HIGHEST
        )
        mixed = (inter + intra).reshape(row_count, query_head_rows, head_size)
        scaled = mixed * lax.rsqrt(jnp.mean(mixed * mixed, axis=-1, keepdims=True) + 1e-05)
        gating = spike_counts.astype(jnp.float32).reshape(
            row_count, query_head_rows, head_size
        ) * thresholds.reshape(query_head_rows, head_size)
        return jnp.where(
            valid_rows[:, None],
            (scaled * gating).reshape(row_count, query_head_rows * head_size),
            0.0,
        ).astype(jnp.bfloat16)

    def finish_skip(dummy_arg):
        return jnp.zeros((row_count, query_head_rows * head_size), jnp.bfloat16)

    gated = lax.cond(section_index == 1, linear_finish, finish_skip, 0)
    head_outputs = jnp.where(section_index == 0, attention, gated)[None]
    return (head_outputs, local_activations)


MESH = pl.DeviceIdType.MESH
F32 = jnp.float32
BF16 = jnp.bfloat16
CHUNK = 256
PAD = 16
PIECES = 4


def nt(a, b):
    return lax.dot_general(a, b, (((1,), (1,)), ((), ())), preferred_element_type=F32)


def nn(a, b):
    return jnp.dot(a, b, preferred_element_type=F32)


def turned(x):
    return jnp.transpose(x.astype(F32)).astype(BF16)


def kernel(
    n,
    residual,
    queries,
    keys,
    window_values,
    mixing,
    gain,
    decay_t,
    spikes,
    thresholds,
    lengths,
    head_out,
    hidden_out,
    weights,
    spike_buf,
    kv,
    moved_queries,
    stacked,
    top,
    total,
    blend,
    attention,
    terms,
    own_terms,
    far_terms,
    residuals,
    hidden_buf,
    values_sum,
    square_sum,
    damped,
    faded,
    rest,
    keys_t,
    values,
    states,
    fresh,
    incoming,
    mixed,
    gate,
    gain_row,
    decay_wide,
    weights_sem,
    spike_sem,
    res_sem,
    first_sem,
    first_recv,
    kv_send,
    kv_recv,
    kv_forward,
    att_sem,
    term_own_send,
    term_far_send,
    term_own_recv,
    term_far_recv,
    hid_send,
    hid_recv,
    swap_send,
    swap_recv,
    state_send,
    state_recv,
):
    c = lax.axis_index("ctx")
    s = lax.axis_index("section")
    p = lax.axis_index("tp")
    odd = c % 2
    step_to = 1 - 2 * odd
    partner = c + step_to
    rows = keys.shape[0]
    half = residual.shape[1]
    chunks_half = half // CHUNK
    chunks = 2 * chunks_half
    group = 4
    wide = group * HEAD
    factor = math.log2(math.e) / math.sqrt(HEAD)

    barrier = pltpu.get_barrier_semaphore()
    pl.semaphore_signal(barrier, inc=1, device_id={"section": 1 - s}, device_id_type=MESH)
    pl.semaphore_signal(barrier, inc=1, device_id={"tp": 1 - p}, device_id_type=MESH)
    pl.semaphore_signal(
        barrier, inc=1, device_id={"section": 1 - s, "tp": 1 - p}, device_id_type=MESH
    )
    pl.semaphore_signal(barrier, inc=1, device_id={"ctx": partner}, device_id_type=MESH)
    for shift in (2, n - 2):
        pl.semaphore_signal(
            barrier, inc=1, device_id={"ctx": lax.rem(c + shift, n)}, device_id_type=MESH
        )

    weights_copy = pltpu.make_async_copy(mixing, weights, weights_sem)
    weights_copy.start()

    own_len = lengths[c]

    @pl.when(s == 0)
    def _():
        kv[0, 0:rows] = keys[:, 0:HEAD]
        value_t = turned(window_values[:, 0:HEAD])
        kv[0, rows : rows + HEAD] = value_t[:, 0:HEAD]
        kv[0, rows + HEAD : rows + 2 * HEAD] = value_t[:, HEAD : 2 * HEAD]
        for h in range(group):
            stacked[h * rows : (h + 1) * rows, :] = queries[:, h * HEAD : (h + 1) * HEAD]

    @pl.when(s == 1)
    def _():
        value_t = turned(window_values[:, HEAD : 2 * HEAD])
        kv[0, rows : rows + HEAD] = value_t[:, 0:HEAD]
        kv[0, rows + HEAD : rows + 2 * HEAD] = value_t[:, HEAD : 2 * HEAD]

    pl.semaphore_wait(barrier, 6)

    key_copy = pltpu.make_async_remote_copy(
        src_ref=keys.at[:, HEAD : 2 * HEAD],
        dst_ref=kv.at[0, 0:rows],
        send_sem=first_sem.at[0],
        recv_sem=first_recv.at[0],
        device_id={"section": 1 - s},
        device_id_type=MESH,
    )
    query_copy = pltpu.make_async_remote_copy(
        src_ref=queries.at[:, wide : 2 * wide],
        dst_ref=moved_queries,
        send_sem=first_sem.at[1],
        recv_sem=first_recv.at[1],
        device_id={"section": 1 - s},
        device_id_type=MESH,
    )
    residual_send = pltpu.make_async_remote_copy(
        src_ref=residual,
        dst_ref=residuals.at[p],
        send_sem=res_sem.at[0],
        recv_sem=res_sem.at[1],
        device_id={"tp": 1 - p},
        device_id_type=MESH,
    )
    residual_recv = pltpu.make_async_remote_copy(
        src_ref=residual,
        dst_ref=residuals.at[1 - p],
        send_sem=res_sem.at[0],
        recv_sem=res_sem.at[1],
        device_id={"tp": 1 - p},
        device_id_type=MESH,
    )
    residual_copy = pltpu.make_async_copy(residual, residuals.at[p], res_sem.at[2])
    spike_copy = pltpu.make_async_copy(spikes, spike_buf, spike_sem)

    @pl.when(s == 0)
    def _():
        key_copy.start()
        query_copy.start()

    @pl.when(s == 1)
    def _():
        residual_send.start()
        residual_copy.start()
        spike_copy.start()
        key_copy.wait_recv()

    def along(k):
        return pltpu.make_async_remote_copy(
            src_ref=kv.at[2 * k],
            dst_ref=kv.at[2 * k + 2],
            send_sem=kv_send.at[k],
            recv_sem=kv_recv.at[2 * k + 2],
            device_id={"ctx": lax.rem(c + 2, n)},
            device_id_type=MESH,
        )

    def across(k):
        return pltpu.make_async_remote_copy(
            src_ref=kv.at[2 * k],
            dst_ref=kv.at[2 * k + step_to],
            send_sem=kv_forward.at[k],
            recv_sem=kv_recv.at[2 * k + step_to],
            device_id={"ctx": partner},
            device_id_type=MESH,
        )

    def arrival(slot):
        return pltpu.make_async_remote_copy(
            src_ref=kv.at[slot],
            dst_ref=kv.at[slot],
            send_sem=kv_send.at[0],
            recv_sem=kv_recv.at[slot],
            device_id={"ctx": partner},
            device_id_type=MESH,
        )

    before = c // 2
    pairs = n // 2

    @pl.when(c + 2 < n)
    def _():
        along(0).start()

    @pl.when(odd == 0)
    def _():
        across(0).start()

    @pl.when(s == 1)
    def _():
        query_copy.wait_recv()
        for h in range(group):
            stacked[h * rows : (h + 1) * rows, :] = moved_queries[:, h * HEAD : (h + 1) * HEAD]

    def attend(slot, first):
        key_rows = kv[slot, 0:rows]
        value_t = jnp.concatenate(
            [kv[slot, rows : rows + HEAD], kv[slot, rows + HEAD : rows + 2 * HEAD]], axis=1
        )
        key_index = lax.broadcasted_iota(jnp.int32, (rows, rows), 0)
        allowed = key_index < lengths[c - slot]
        if first:
            allowed = allowed & (key_index <= lax.broadcasted_iota(jnp.int32, (rows, rows), 1))
        spans = [slice(h * rows, (h + 1) * rows) for h in range(group)]
        scores = [jnp.where(allowed, nt(key_rows, stacked[at, :]), -1e30) for at in spans]
        best = [jnp.max(x, axis=0, keepdims=True) for x in scores]
        if not first:
            best = [jnp.maximum(x, top[:, at]) for x, at in zip(best, spans)]
        parts = [jnp.exp2((x - b) * factor) for x, b in zip(scores, best)]
        blended = [nn(value_t, x.astype(BF16)) for x in parts]
        sums = [jnp.sum(x, axis=0, keepdims=True) for x in parts]
        for h, at in enumerate(spans):
            if first:
                total[:, at] = sums[h]
                blend[:, at] = blended[h]
            else:
                shrink = jnp.exp2((top[:, at] - best[h]) * factor)
                total[:, at] = total[:, at] * shrink + sums[h]
                blend[:, at] = blend[:, at] * shrink + blended[h]
            top[:, at] = best[h]

    attend(0, True)

    def attend_pair(k, carry):
        arrival(2 * k).wait_recv()

        @pl.when(c + 2 < n)
        def _():
            along(k).start()

        across(k).start()
        attend(2 * k, False)
        behind = 2 * k - 3 + 2 * odd

        @pl.when(behind > 0)
        def _():
            arrival(behind).wait_recv()
            attend(behind, False)

        return carry

    lax.fori_loop(1, before + 1, attend_pair, 0)
    rest_slot = 2 * before - 1 + 2 * odd

    @pl.when(rest_slot > 0)
    def _():
        arrival(rest_slot).wait_recv()
        attend(rest_slot, False)

    row_lane = lax.broadcasted_iota(jnp.int32, (1, rows), 1)
    for h in range(group):
        at = slice(h * rows, (h + 1) * rows)
        scaled = blend[:, at] / jnp.maximum(total[:, at], 1.0)
        scaled = jnp.where(row_lane < own_len, scaled, 0.0)
        attention[s, :, h * HEAD : (h + 1) * HEAD] = jnp.transpose(scaled).astype(BF16)

    att_copy = pltpu.make_async_remote_copy(
        src_ref=attention.at[1],
        dst_ref=attention.at[1],
        send_sem=att_sem.at[0],
        recv_sem=att_sem.at[1],
        device_id={"section": 1 - s},
        device_id_type=MESH,
    )

    def term_own(j):
        return pltpu.make_async_remote_copy(
            src_ref=terms.at[j],
            dst_ref=own_terms.at[j],
            send_sem=term_own_send.at[j],
            recv_sem=term_own_recv.at[j],
            device_id={"section": 1 - s},
            device_id_type=MESH,
        )

    def term_far(j):
        return pltpu.make_async_remote_copy(
            src_ref=terms.at[j],
            dst_ref=far_terms.at[j],
            send_sem=term_far_send.at[j],
            recv_sem=term_far_recv.at[j],
            device_id={"section": 1 - s, "tp": 1 - p},
            device_id_type=MESH,
        )

    def hid(j):
        return pltpu.make_async_remote_copy(
            src_ref=hidden_buf.at[j],
            dst_ref=hidden_out.at[:, pl.ds(pl.multiple_of(j * CHUNK, CHUNK), CHUNK)],
            send_sem=hid_send.at[j],
            recv_sem=hid_recv.at[j],
            device_id={"section": 1 - s},
            device_id_type=MESH,
        )

    def each(count, act):
        def one(j, carry):
            act(j)
            return carry

        lax.fori_loop(0, count, one, 0)

    @pl.when(s == 0)
    def _():
        weights_copy.wait()
        att_copy.wait_recv()

        def project(j, carry):
            at = pl.ds(pl.multiple_of(j * CHUNK, CHUNK), CHUNK)
            both = jnp.concatenate([attention[0], attention[1]], axis=1)
            terms[j] = nn(both, weights[:, at]).astype(BF16)
            term_own(j).start()

            @pl.when(j >= 2)
            def _():
                term_far(j - 2).wait_send()

            term_far(j).start()
            return carry

        lax.fori_loop(0, chunks, project, 0)
        head_out[:, 0:wide] = attention[0]
        head_out[:, wide : 2 * wide] = attention[1]
        term_far(chunks - 2).wait_send()
        term_far(chunks - 1).wait_send()
        each(chunks, lambda j: term_own(j).wait_send())
        key_copy.wait_send()
        query_copy.wait_send()
        each(chunks_half, lambda j: hid(j).wait_recv())

    @pl.when(s == 1)
    def _():
        att_copy.start()
        heads = 2 * group
        row_col = lax.broadcasted_iota(jnp.int32, (rows, 1), 0)
        valid_col = row_col < own_len
        r = lax.broadcasted_iota(jnp.int32, (rows, rows), 0)
        t = lax.broadcasted_iota(jnp.int32, (rows, rows), 1)
        upper = jnp.where(r <= t, 1.0, 0.0)
        decay_wide[...] = jnp.zeros_like(decay_wide)
        decay_wide[0:heads, :] = jnp.where(row_lane < own_len, decay_t[...], 0.0)
        cum_t = jnp.dot(
            decay_wide[...], upper, precision=lax.Precision.HIGHEST, preferred_element_type=F32
        )
        cum = jnp.transpose(cum_t)
        gain_row[...] = gain[...].astype(F32).reshape(1, 2 * half)
        last = cum[rows - 1 : rows, :]
        left = jnp.exp(last - cum)
        for g in range(2):
            masked = jnp.where(valid_col, keys[:, g * HEAD : (g + 1) * HEAD].astype(F32), 0.0)
            keys_t[g] = jnp.transpose(masked).astype(BF16)
        for h in range(heads):
            at = slice(h * HEAD, (h + 1) * HEAD)
            col = cum[:, h : h + 1]
            row = cum_t[h : h + 1, :]
            query = queries[:, at]
            damping = jnp.where(r >= t, jnp.exp(jnp.minimum(col - row, 0.0)), 0.0)
            rest[:, at] = jnp.broadcast_to(left[:, h : h + 1], (rows, HEAD))
            damped[h] = (nn(query, keys_t[h // group]) * damping).astype(BF16)
            faded[:, at] = (query.astype(F32) * jnp.exp(col)).astype(BF16)
            sum_row = jnp.broadcast_to(last[:, h : h + 1], (PAD, HEAD))
            high = sum_row.astype(BF16)
            low = sum_row - high.astype(F32)
            in_group = slice((h % group) * HEAD, (h % group + 1) * HEAD)
            states[0, h // group, HEAD : HEAD + PAD, in_group] = jnp.where(
                lax.broadcasted_iota(jnp.int32, (PAD, HEAD), 0) < PAD // 2,
                high.astype(F32),
                low,
            ).astype(BF16)
        spike_copy.wait()
        for h in range(heads):
            at = slice(h * HEAD, (h + 1) * HEAD)
            gated = spike_buf[:, at].astype(F32) * thresholds[:, at]
            gate[:, at] = jnp.where(valid_col, gated, 0.0)
        values_sum[...] = jnp.zeros_like(values_sum)
        square_sum[...] = jnp.zeros_like(square_sum)
        weights_copy.wait()
        residual_copy.wait()
        residual_recv.wait_recv()

        def collect(j, carry):
            side = j // chunks_half
            col = j - side * chunks_half
            here = pl.ds(pl.multiple_of(col * CHUNK, CHUNK), CHUNK)
            at = pl.ds(pl.multiple_of(j * CHUNK, CHUNK), CHUNK)
            term_own(j).wait_recv()
            term_far(j).wait_recv()
            summed = residuals[side, :, here].astype(F32) + (
                own_terms[j].astype(F32) + far_terms[j].astype(F32)
            )
            narrow = summed.astype(BF16)

            @pl.when(side == p)
            def _():
                hidden_buf[col] = narrow
                hidden_out[:, here] = narrow
                hid(col).start()

            rounded = narrow.astype(F32)
            square_sum[...] += jnp.sum(rounded * rounded, axis=1, keepdims=True)
            ready = (rounded * gain_row[:, at]).astype(BF16)
            values_sum[...] += nt(ready, weights[:, at])
            return carry

        lax.fori_loop(0, chunks, collect, 0)
        scale = lax.rsqrt(square_sum[...] * (1.0 / (2 * half)) + 1e-05)
        values[...] = (values_sum[...] * scale).astype(BF16)
        def swap(g):
            return pltpu.make_async_remote_copy(
                src_ref=states.at[0, g],
                dst_ref=states.at[1, g],
                send_sem=swap_send.at[g],
                recv_sem=swap_recv.at[g],
                device_id={"ctx": partner},
                device_id_type=MESH,
            )

        def onward(g):
            return pltpu.make_async_remote_copy(
                src_ref=states.at[2, g, 0:HEAD],
                dst_ref=states.at[3, g, 0:HEAD],
                send_sem=state_send.at[g],
                recv_sem=state_recv.at[g],
                device_id={"ctx": lax.rem(c + 2, n)},
                device_id_type=MESH,
            )

        def sum_of(slot, g):
            rows_of = states[slot, g, HEAD : HEAD + PAD, :].astype(F32)
            return rows_of[0:1, :] + rows_of[PAD // 2 : PAD // 2 + 1, :]

        here_later = pairs - 1 - before
        swap_out = (odd == 0) | (here_later > 0)
        swap_in = (odd == 1) | (here_later > 0)
        for g in range(2):
            for h in range(g * group, (g + 1) * group):
                at = slice(h * HEAD, (h + 1) * HEAD)
                weighted = (values[:, at].astype(F32) * rest[:, at]).astype(BF16)
                fresh[:, at] = nn(keys_t[g], weighted)
                in_group = slice((h % group) * HEAD, (h % group + 1) * HEAD)
                states[0, g, 0:HEAD, in_group] = fresh[:, at].astype(BF16)

            @pl.when(swap_out)
            def _():
                swap(g).start()

        for h in range(heads):
            at = slice(h * HEAD, (h + 1) * HEAD)
            mixed[:, at] = nn(damped[h], values[:, at])

        for g in range(2):
            at = slice(g * wide, (g + 1) * wide)

            @pl.when(swap_in)
            def _():
                swap(g).wait_recv()

            @pl.when(here_later > 0)
            def _():
                own = fresh[:, at]
                other = states[1, g, 0:HEAD, :].astype(F32)
                second = jnp.where(odd == 1, sum_of(0, g), sum_of(1, g))
                first_part = jnp.where(odd == 1, other, own)
                second_part = jnp.where(odd == 1, own, other)
                fresh[:, at] = first_part * jnp.exp(second) + second_part

            @pl.when(before > 0)
            def _():
                onward(g).wait_recv()
                incoming[:, at] = states[3, g, 0:HEAD, :].astype(F32)

            @pl.when(before == 0)
            def _():
                incoming[:, at] = jnp.zeros((HEAD, wide), F32)

            @pl.when(here_later > 0)
            def _():
                faded_in = incoming[:, at] * jnp.exp(sum_of(0, g) + sum_of(1, g))
                states[2, g, 0:HEAD, :] = (faded_in + fresh[:, at]).astype(BF16)
                onward(g).start()

            @pl.when(odd == 1)
            def _():
                incoming[:, at] = incoming[:, at] * jnp.exp(sum_of(1, g)) + states[
                    1, g, 0:HEAD, :
                ].astype(F32)

            for h in range(g * group, (g + 1) * group):
                at = slice(h * HEAD, (h + 1) * HEAD)
                both = mixed[:, at] + nn(faded[:, at], incoming[:, at].astype(BF16))
                scaled = both * lax.rsqrt(jnp.mean(both * both, axis=1, keepdims=True) + 1e-05)
                head_out[:, at] = (scaled * gate[:, at]).astype(BF16)

        for g in range(2):

            @pl.when(swap_out)
            def _():
                swap(g).wait_send()

            @pl.when(here_later > 0)
            def _():
                onward(g).wait_send()

        each(chunks_half, lambda j: hid(j).wait_send())
        residual_send.wait_send()
        att_copy.wait_send()

    def along_done(k, carry):
        along(k).wait_send()
        return carry

    @pl.when(c + 2 < n)
    def _():
        lax.fori_loop(0, before + 1, along_done, 0)

    @pl.when(odd == 0)
    def _():
        across(0).wait_send()

    def across_done(k, carry):
        across(k).wait_send()
        return carry

    lax.fori_loop(1, before + 1, across_done, 0)


def handed_on(a, b, a_out, b_out, a_buf, b_buf, in_sem, out_sem):
    step = a.shape[0] // PIECES

    def copies(i):
        at = slice(i * step, (i + 1) * step)
        return (
            pltpu.make_async_copy(b.at[at], b_buf.at[at], in_sem.at[0, i]),
            pltpu.make_async_copy(a.at[at], a_buf.at[at], in_sem.at[1, i]),
            pltpu.make_async_copy(b_buf.at[at], b_out.at[at], out_sem.at[0, i]),
            pltpu.make_async_copy(a_buf.at[at], a_out.at[at], out_sem.at[1, i]),
        )

    for i in range(PIECES):
        copies(i)[0].start()
        copies(i)[1].start()
    for i in range(PIECES):
        for k in range(2):
            copies(i)[k].wait()
            copies(i)[k + 2].start()
    for i in range(PIECES):
        copies(i)[2].wait()
        copies(i)[3].wait()


def fused(
    residual,
    queries,
    keys,
    window_values,
    mixing,
    norm_gain,
    log_decay,
    spike_counts,
    thresholds,
    lengths,
):
    n = lax.axis_size("ctx")
    rows, half = residual.shape
    width = queries.shape[2]
    heads = width // HEAD
    chunks = 2 * half // CHUNK
    dma = pltpu.SemaphoreType.DMA
    whole = pl.BlockSpec(memory_space=pltpu.VMEM)
    away = pl.BlockSpec(memory_space=pl.ANY)
    head_outputs, hidden = pl.pallas_call(
        functools.partial(kernel, n),
        out_shape=(
            jax.ShapeDtypeStruct((rows, width), BF16),
            jax.ShapeDtypeStruct((rows, half), BF16),
        ),
        in_specs=[
            away,
            whole,
            whole,
            whole,
            away,
            whole,
            whole,
            away,
            whole,
            pl.BlockSpec(memory_space=pltpu.SMEM),
        ],
        out_specs=(whole, whole),
        scratch_shapes=[
            pltpu.VMEM(mixing.shape[1:], BF16),
            pltpu.VMEM((rows, width), jnp.int32),
            pltpu.VMEM((n, 2 * rows, HEAD), BF16),
            pltpu.VMEM((rows, width // 2), BF16),
            pltpu.VMEM((4 * rows, HEAD), BF16),
            pltpu.VMEM((1, 4 * rows), F32),
            pltpu.VMEM((1, 4 * rows), F32),
            pltpu.VMEM((HEAD, 4 * rows), F32),
            pltpu.VMEM((2, rows, width // 2), BF16),
            pltpu.VMEM((chunks, rows, CHUNK), BF16),
            pltpu.VMEM((chunks, rows, CHUNK), BF16),
            pltpu.VMEM((chunks, rows, CHUNK), BF16),
            pltpu.VMEM((2, rows, half), BF16),
            pltpu.VMEM((chunks // 2, rows, CHUNK), BF16),
            pltpu.VMEM((rows, width), F32),
            pltpu.VMEM((rows, 1), F32),
            pltpu.VMEM((heads, rows, rows), BF16),
            pltpu.VMEM((rows, width), BF16),
            pltpu.VMEM((rows, width), F32),
            pltpu.VMEM((2, HEAD, rows), BF16),
            pltpu.VMEM((rows, width), BF16),
            pltpu.VMEM((4, 2, HEAD + PAD, width // 2), BF16),
            pltpu.VMEM((HEAD, width), F32),
            pltpu.VMEM((HEAD, width), F32),
            pltpu.VMEM((rows, width), F32),
            pltpu.VMEM((rows, width), F32),
            pltpu.VMEM((1, 2 * half), F32),
            pltpu.VMEM((HEAD, rows), F32),
            dma,
            dma,
            dma((3,)),
            dma((2,)),
            dma((2,)),
            dma((n // 2,)),
            dma((n,)),
            dma((n // 2,)),
            dma((2,)),
            dma((chunks,)),
            dma((chunks,)),
            dma((chunks,)),
            dma((chunks,)),
            dma((chunks // 2,)),
            dma((chunks // 2,)),
            dma((2,)),
            dma((2,)),
            dma((2,)),
            dma((2,)),
        ],
        compiler_params=pltpu.CompilerParams(
            collective_id=0, has_side_effects=True, vmem_limit_bytes=56 * 1024 * 1024
        ),
    )(
        residual,
        queries[0],
        keys[0],
        window_values,
        mixing[0],
        norm_gain,
        log_decay.T,
        spike_counts,
        thresholds.reshape(1, -1),
        lengths,
    )
    head_outputs, hidden = pl.pallas_call(
        handed_on,
        out_shape=(
            jax.ShapeDtypeStruct((rows, width), BF16),
            jax.ShapeDtypeStruct((rows, half), BF16),
        ),
        in_specs=[away, away],
        out_specs=(away, away),
        scratch_shapes=[
            pltpu.VMEM((rows, width), BF16),
            pltpu.VMEM((rows, half), BF16),
            dma((2, PIECES)),
            dma((2, PIECES)),
        ],
        compiler_params=pltpu.CompilerParams(vmem_limit_bytes=60 * 1024 * 1024),
    )(head_outputs, hidden)
    return (head_outputs[None], hidden)


def chosen(*arrays):
    residual, queries, keys = arrays[:3]
    shards = lax.axis_size("ctx")
    rows = residual.shape[0]
    fits = (
        lax.axis_size("tp") == 2
        and lax.axis_size("section") == 2
        and keys.shape[2] == 2 * HEAD
        and queries.shape[2] == 8 * HEAD
        and rows == 2 * HEAD
        and residual.shape[1] % CHUNK == 0
        and shards % 2 == 0
        and shards >= 4
        and shards * rows <= WINDOW
    )
    return fused(*arrays) if fits else body(*arrays)


def solution(mesh):
    return jax.shard_map(
        chosen,
        mesh=mesh,
        in_specs=(
            P("ctx", "tp"),
            P("section", "ctx", "tp"),
            P("section", "ctx", "tp"),
            P("ctx", "tp"),
            P("section", "tp", None),
            P(),
            P("ctx", "tp"),
            P("ctx", "tp"),
            P("tp"),
            P(),
        ),
        out_specs=(P("section", "ctx", "tp"), P("ctx", "tp")),
        check_vma=False,
    )
```

```python
import functools
import math

import jax
import jax.numpy as jnp
from jax import lax
from jax.experimental import pallas as pl
from jax.experimental.pallas import tpu as pltpu
from jax.sharding import PartitionSpec as P

HEAD = 128
WINDOW = 4096


def passed_along(x, axis, by):
    devices = lax.axis_size(axis)
    pairs = [(i, i + by) for i in range(devices) if 0 <= i + by < devices]
    return lax.ppermute(x, axis, pairs)


def entering(x, axis, join, neutral):
    place = lax.axis_index(axis)
    gathered = jax.tree.map(
        lambda a, kind: lax.all_gather(a.astype(kind), axis), x, (jnp.bfloat16, jnp.bfloat16)
    )
    state = jax.tree.map(lambda a, e: jnp.zeros_like(a) + jnp.asarray(e, a.dtype), x, neutral)

    def one(step, state):
        return join(
            state,
            jax.tree.map(
                lambda a, own: lax.dynamic_index_in_dim(a, step, 0, False).astype(own.dtype),
                gathered,
                x,
            ),
        )

    return lax.fori_loop(0, place, one, state)


def body(
    residual,
    queries,
    keys,
    window_values,
    mixing,
    norm_gain,
    log_decay,
    spike_counts,
    thresholds,
    lengths,
):
    section_index = lax.axis_index("section")
    shard_index = lax.axis_index("ctx")
    row_count = keys.shape[1]
    head_size = HEAD
    key_heads = keys.shape[2] // head_size
    query_head_rows = queries.shape[2] // head_size
    group_size = query_head_rows // key_heads
    span_blocks = WINDOW // row_count
    feature_count = mixing.shape[2]
    scale = 1.0 / math.sqrt(head_size)
    positions = jnp.arange(row_count, dtype=jnp.int32)
    valid_rows = positions < lengths[shard_index]
    own_keys = keys[0]
    earlier = [
        passed_along((own_keys, window_values), "ctx", distance + 1)
        for distance in range(span_blocks)
    ]
    key_blocks = jnp.stack([pair[0] for pair in earlier[::-1]] + [own_keys], 0)
    value_blocks = jnp.stack([pair[1] for pair in earlier[::-1]] + [window_values], 0)

    def window_layer(dummy_arg):
        query_rows = queries[0].reshape(row_count, key_heads, group_size, head_size)
        sources = shard_index - span_blocks + jnp.arange(span_blocks + 1, dtype=jnp.int32)
        block_valid = (sources[:, None] >= 0) & (
            positions[None, :] < lengths[jnp.clip(sources, 0, None)][:, None]
        )
        offsets = (span_blocks - jnp.arange(span_blocks + 1, dtype=jnp.int32)) * row_count
        base_distance = positions[:, None] - positions[None, :]

        def weight_step(carry, items):
            running, totals, best = carry
            scores = (
                jnp.einsum(
                    "rgjd,kgd->gjrk",
                    query_rows,
                    items[0].reshape(row_count, key_heads, head_size),
                    preferred_element_type=jnp.float32,
                )
                * scale
            )
            distance = base_distance + items[3]
            allowed = items[2][None, :] & (distance >= 0) & (distance < WINDOW)
            scores = jnp.where(allowed, scores, -1e30)
            new_best = jnp.maximum(best, jnp.max(scores, axis=-1))
            factor = jnp.exp(best - new_best)
            weights = jnp.where(allowed, jnp.exp(scores - new_best[..., None]), 0.0)
            blended = jnp.einsum(
                "gjrk,kgd->gjrd",
                weights.astype(jnp.bfloat16),
                items[1].reshape(row_count, key_heads, head_size),
                preferred_element_type=jnp.float32,
            )
            return (
                (
                    running * factor[..., None] + blended,
                    totals * factor + jnp.sum(weights, axis=-1),
                    new_best,
                ),
                None,
            )

        start_sums = (
            jnp.zeros((key_heads, group_size, row_count, head_size), jnp.float32),
            jnp.zeros((key_heads, group_size, row_count), jnp.float32),
            jnp.full((key_heads, group_size, row_count), -1e30, jnp.float32),
        )
        (blended, totals, unused_best), unused_sum = lax.scan(
            weight_step, start_sums, (key_blocks, value_blocks, block_valid, offsets)
        )
        attention = blended / jnp.maximum(totals, 1.0)[..., None]
        attention = attention.transpose(2, 0, 1, 3).reshape(row_count, query_head_rows * head_size)
        attention = jnp.where(valid_rows[:, None], attention, 0.0).astype(jnp.bfloat16)
        projected = jnp.dot(attention, mixing[0], preferred_element_type=jnp.float32)
        return (attention, projected)

    def window_skip(dummy_arg):
        return (
            jnp.zeros((row_count, query_head_rows * head_size), jnp.bfloat16),
            jnp.zeros((row_count, feature_count), jnp.float32),
        )

    attention, projected = lax.cond(section_index == 0, window_layer, window_skip, 0)
    share = lax.psum_scatter(
        projected.astype(jnp.bfloat16), "tp", scatter_dimension=1, tiled=True
    ).astype(jnp.float32)
    own_hidden = (share + residual.astype(jnp.float32)).astype(jnp.bfloat16)
    moved_share = passed_along(own_hidden, "section", 1)
    local_activations = jnp.where(section_index == 0, own_hidden, moved_share)
    complete_hidden_matrix = lax.all_gather(local_activations, "tp", axis=1, tiled=True)
    masked_keys = jnp.where(valid_rows[:, None], own_keys, jnp.zeros_like(own_keys)).reshape(
        row_count, key_heads, head_size
    )
    wide_keys = masked_keys.astype(jnp.float32)
    decays = log_decay * valid_rows[:, None].astype(jnp.float32)

    def linear_prepare(dummy_arg):
        wide = complete_hidden_matrix.astype(jnp.float32)
        normed = (
            wide
            * lax.rsqrt(jnp.mean(wide * wide, axis=-1, keepdims=True) + 1e-05)
            * norm_gain.astype(jnp.float32)
        ).astype(jnp.bfloat16)
        payload_vectors = lax.dot_general(
            normed, mixing[0], (((1,), (1,)), ((), ())), preferred_element_type=jnp.float32
        ).astype(jnp.bfloat16)
        cumulated = jnp.cumsum(decays, axis=0).reshape(row_count, key_heads, group_size)
        value_rows = payload_vectors.astype(jnp.float32).reshape(
            row_count, key_heads, group_size, head_size
        )
        fresh_state = jnp.einsum(
            "sgd,sgje->gdje",
            wide_keys,
            value_rows * jnp.exp(cumulated[-1] - cumulated)[..., None],
            precision=lax.Precision.HIGHEST,
        )
        return (payload_vectors, cumulated, fresh_state)

    def linear_skip(dummy_arg):
        return (
            jnp.zeros((row_count, query_head_rows * head_size), jnp.bfloat16),
            jnp.zeros((row_count, key_heads, group_size), jnp.float32),
            jnp.zeros((key_heads, head_size, group_size, head_size), jnp.float32),
        )

    payload_vectors, cumulated, fresh_state = lax.cond(
        section_index == 1, linear_prepare, linear_skip, 0
    )

    def chain(previous_entry, latter):
        return (
            previous_entry[0] + latter[0],
            previous_entry[1] * jnp.exp(latter[0])[:, None, :, None] + latter[1],
        )

    identity = (jnp.zeros((key_heads, group_size), jnp.float32), jnp.zeros_like(fresh_state))
    unused_total, incoming = entering((cumulated[-1], fresh_state), "ctx", chain, identity)

    def linear_finish(dummy_arg):
        query_narrow = queries[0].reshape(row_count, key_heads, group_size, head_size)
        query_rows = query_narrow.astype(jnp.float32)
        value_rows = payload_vectors.astype(jnp.float32).reshape(
            row_count, key_heads, group_size, head_size
        )
        inter = (
            jnp.einsum("rgjd,gdje->rgje", query_rows, incoming, precision=lax.Precision.HIGHEST)
            * jnp.exp(cumulated)[..., None]
        )
        products = jnp.einsum(
            "rgjd,sgd->gjrs", query_narrow, masked_keys, preferred_element_type=jnp.float32
        )
        ordered = cumulated.transpose(1, 2, 0)
        spread = ordered[..., :, None] - ordered[..., None, :]
        triangle = positions[:, None] >= positions[None, :]
        damping = jnp.where(triangle, jnp.exp(jnp.minimum(spread, 0.0)), 0.0)
        intra = jnp.einsum(
            "gjrs,sgje->rgje", products * damping, value_rows, precision=lax.Precision.HIGHEST
        )
        mixed = (inter + intra).reshape(row_count, query_head_rows, head_size)
        scaled = mixed * lax.rsqrt(jnp.mean(mixed * mixed, axis=-1, keepdims=True) + 1e-05)
        gating = spike_counts.astype(jnp.float32).reshape(
            row_count, query_head_rows, head_size
        ) * thresholds.reshape(query_head_rows, head_size)
        return jnp.where(
            valid_rows[:, None],
            (scaled * gating).reshape(row_count, query_head_rows * head_size),
            0.0,
        ).astype(jnp.bfloat16)

    def finish_skip(dummy_arg):
        return jnp.zeros((row_count, query_head_rows * head_size), jnp.bfloat16)

    gated = lax.cond(section_index == 1, linear_finish, finish_skip, 0)
    head_outputs = jnp.where(section_index == 0, attention, gated)[None]
    return (head_outputs, local_activations)


MESH = pl.DeviceIdType.MESH
F32 = jnp.float32
BF16 = jnp.bfloat16
CHUNK = 256
PAD = 8
PIECES = 4


def nt(a, b):
    return lax.dot_general(a, b, (((1,), (1,)), ((), ())), preferred_element_type=F32)


def nn(a, b):
    return jnp.dot(a, b, preferred_element_type=F32)


def turned(x):
    return jnp.transpose(x.astype(F32)).astype(BF16)


def kernel(
    n,
    residual,
    queries,
    keys,
    window_values,
    mixing,
    gain,
    decay_t,
    spikes,
    thresholds,
    lengths,
    head_out,
    hidden_out,
    weights,
    spike_buf,
    kv,
    moved_queries,
    stacked,
    top,
    total,
    blend,
    attention,
    terms,
    own_terms,
    far_terms,
    residuals,
    hidden_buf,
    values_sum,
    square_sum,
    damped,
    faded,
    rest,
    keys_t,
    values,
    states,
    fresh,
    incoming,
    mixed,
    gate,
    totals,
    gain_row,
    decay_wide,
    weights_sem,
    spike_sem,
    res_sem,
    first_sem,
    first_recv,
    kv_send,
    kv_recv,
    kv_forward,
    att_sem,
    term_own_send,
    term_far_send,
    term_own_recv,
    term_far_recv,
    hid_send,
    hid_recv,
    totals_sem,
    swap_send,
    swap_recv,
    state_send,
    state_recv,
):
    c = lax.axis_index("ctx")
    s = lax.axis_index("section")
    p = lax.axis_index("tp")
    odd = c % 2
    step_to = 1 - 2 * odd
    partner = c + step_to
    rows = keys.shape[0]
    half = residual.shape[1]
    chunks_half = half // CHUNK
    chunks = 2 * chunks_half
    group = 4
    wide = group * HEAD
    factor = math.log2(math.e) / math.sqrt(HEAD)

    barrier = pltpu.get_barrier_semaphore()
    pl.semaphore_signal(barrier, inc=1, device_id={"section": 1 - s}, device_id_type=MESH)
    pl.semaphore_signal(barrier, inc=1, device_id={"tp": 1 - p}, device_id_type=MESH)
    pl.semaphore_signal(
        barrier, inc=1, device_id={"section": 1 - s, "tp": 1 - p}, device_id_type=MESH
    )
    pl.semaphore_signal(barrier, inc=1, device_id={"ctx": partner}, device_id_type=MESH)
    for shift in (2, n - 2):
        pl.semaphore_signal(
            barrier, inc=1, device_id={"ctx": lax.rem(c + shift, n)}, device_id_type=MESH
        )

    weights_copy = pltpu.make_async_copy(mixing, weights, weights_sem)
    weights_copy.start()

    own_len = lengths[c]

    @pl.when(s == 0)
    def _():
        kv[0, 0:rows] = keys[:, 0:HEAD]
        value_t = turned(window_values[:, 0:HEAD])
        kv[0, rows : rows + HEAD] = value_t[:, 0:HEAD]
        kv[0, rows + HEAD : rows + 2 * HEAD] = value_t[:, HEAD : 2 * HEAD]
        for h in range(group):
            stacked[h * rows : (h + 1) * rows, :] = queries[:, h * HEAD : (h + 1) * HEAD]

    @pl.when(s == 1)
    def _():
        value_t = turned(window_values[:, HEAD : 2 * HEAD])
        kv[0, rows : rows + HEAD] = value_t[:, 0:HEAD]
        kv[0, rows + HEAD : rows + 2 * HEAD] = value_t[:, HEAD : 2 * HEAD]

    pl.semaphore_wait(barrier, 6)

    key_copy = pltpu.make_async_remote_copy(
        src_ref=keys.at[:, HEAD : 2 * HEAD],
        dst_ref=kv.at[0, 0:rows],
        send_sem=first_sem.at[0],
        recv_sem=first_recv.at[0],
        device_id={"section": 1 - s},
        device_id_type=MESH,
    )
    query_copy = pltpu.make_async_remote_copy(
        src_ref=queries.at[:, wide : 2 * wide],
        dst_ref=moved_queries,
        send_sem=first_sem.at[1],
        recv_sem=first_recv.at[1],
        device_id={"section": 1 - s},
        device_id_type=MESH,
    )
    residual_send = pltpu.make_async_remote_copy(
        src_ref=residual,
        dst_ref=residuals.at[p],
        send_sem=res_sem.at[0],
        recv_sem=res_sem.at[1],
        device_id={"tp": 1 - p},
        device_id_type=MESH,
    )
    residual_recv = pltpu.make_async_remote_copy(
        src_ref=residual,
        dst_ref=residuals.at[1 - p],
        send_sem=res_sem.at[0],
        recv_sem=res_sem.at[1],
        device_id={"tp": 1 - p},
        device_id_type=MESH,
    )
    residual_copy = pltpu.make_async_copy(residual, residuals.at[p], res_sem.at[2])
    spike_copy = pltpu.make_async_copy(spikes, spike_buf, spike_sem)

    def along(k, part):
        at = slice(part * rows, (part + 1) * rows)
        return pltpu.make_async_remote_copy(
            src_ref=kv.at[2 * k, at],
            dst_ref=kv.at[2 * k + 2, at],
            send_sem=kv_send.at[k, part],
            recv_sem=kv_recv.at[2 * k + 2, part],
            device_id={"ctx": lax.rem(c + 2, n)},
            device_id_type=MESH,
        )

    def across(k, part):
        at = slice(part * rows, (part + 1) * rows)
        return pltpu.make_async_remote_copy(
            src_ref=kv.at[2 * k, at],
            dst_ref=kv.at[2 * k + step_to, at],
            send_sem=kv_forward.at[k, part],
            recv_sem=kv_recv.at[2 * k + step_to, part],
            device_id={"ctx": partner},
            device_id_type=MESH,
        )

    def arrival(slot, part):
        at = slice(part * rows, (part + 1) * rows)
        return pltpu.make_async_remote_copy(
            src_ref=kv.at[slot, at],
            dst_ref=kv.at[slot, at],
            send_sem=kv_send.at[0, part],
            recv_sem=kv_recv.at[slot, part],
            device_id={"ctx": partner},
            device_id_type=MESH,
        )

    before = c // 2
    pairs = n // 2

    def send_own(part):
        @pl.when(c + 2 < n)
        def _():
            along(0, part).start()

        @pl.when(odd == 0)
        def _():
            across(0, part).start()

    @pl.when(s == 0)
    def _():
        key_copy.start()
        query_copy.start()

    send_own(1)

    @pl.when(s == 1)
    def _():
        residual_send.start()
        residual_copy.start()
        spike_copy.start()
        key_copy.wait_recv()

    send_own(0)

    @pl.when(s == 1)
    def _():
        query_copy.wait_recv()
        for h in range(group):
            stacked[h * rows : (h + 1) * rows, :] = moved_queries[:, h * HEAD : (h + 1) * HEAD]

    def attend(slot, first):
        key_rows = kv[slot, 0:rows]
        value_t = jnp.concatenate(
            [kv[slot, rows : rows + HEAD], kv[slot, rows + HEAD : rows + 2 * HEAD]], axis=1
        )
        key_index = lax.broadcasted_iota(jnp.int32, (rows, rows), 0)
        allowed = key_index < lengths[c - slot]
        if first:
            allowed = allowed & (key_index <= lax.broadcasted_iota(jnp.int32, (rows, rows), 1))
        spans = [slice(h * rows, (h + 1) * rows) for h in range(group)]
        scores = [jnp.where(allowed, nt(key_rows, stacked[at, :]), -1e30) for at in spans]
        best = [jnp.max(x, axis=0, keepdims=True) for x in scores]
        if not first:
            best = [jnp.maximum(x, top[:, at]) for x, at in zip(best, spans)]
        parts = [jnp.exp2((x - b) * factor) for x, b in zip(scores, best)]
        blended = [nn(value_t, x.astype(BF16)) for x in parts]
        sums = [jnp.sum(x, axis=0, keepdims=True) for x in parts]
        for h, at in enumerate(spans):
            if first:
                total[:, at] = sums[h]
                blend[:, at] = blended[h]
            else:
                shrink = jnp.exp2((top[:, at] - best[h]) * factor)
                total[:, at] = total[:, at] * shrink + sums[h]
                blend[:, at] = blend[:, at] * shrink + blended[h]
            top[:, at] = best[h]

    attend(0, True)

    def attend_pair(k, carry):
        for part in (1, 0):
            arrival(2 * k, part).wait_recv()

            @pl.when(c + 2 < n)
            def _():
                along(k, part).start()

            across(k, part).start()
        attend(2 * k, False)
        behind = 2 * k - 3 + 2 * odd

        @pl.when(behind > 0)
        def _():
            arrival(behind, 1).wait_recv()
            arrival(behind, 0).wait_recv()
            attend(behind, False)

        return carry

    lax.fori_loop(1, before + 1, attend_pair, 0)
    rest_slot = 2 * before - 1 + 2 * odd

    @pl.when(rest_slot > 0)
    def _():
        arrival(rest_slot, 1).wait_recv()
        arrival(rest_slot, 0).wait_recv()
        attend(rest_slot, False)

    row_lane = lax.broadcasted_iota(jnp.int32, (1, rows), 1)
    for h in range(group):
        at = slice(h * rows, (h + 1) * rows)
        scaled = blend[:, at] / jnp.maximum(total[:, at], 1.0)
        scaled = jnp.where(row_lane < own_len, scaled, 0.0)
        attention[s, :, h * HEAD : (h + 1) * HEAD] = jnp.transpose(scaled).astype(BF16)

    att_copy = pltpu.make_async_remote_copy(
        src_ref=attention.at[1],
        dst_ref=attention.at[1],
        send_sem=att_sem.at[0],
        recv_sem=att_sem.at[1],
        device_id={"section": 1 - s},
        device_id_type=MESH,
    )

    def term_own(j):
        return pltpu.make_async_remote_copy(
            src_ref=terms.at[j],
            dst_ref=own_terms.at[j],
            send_sem=term_own_send.at[j],
            recv_sem=term_own_recv.at[j],
            device_id={"section": 1 - s},
            device_id_type=MESH,
        )

    def term_far(j):
        return pltpu.make_async_remote_copy(
            src_ref=terms.at[j],
            dst_ref=far_terms.at[j],
            send_sem=term_far_send.at[j],
            recv_sem=term_far_recv.at[j],
            device_id={"section": 1 - s, "tp": 1 - p},
            device_id_type=MESH,
        )

    def hid(j):
        return pltpu.make_async_remote_copy(
            src_ref=hidden_buf.at[j],
            dst_ref=hidden_out.at[:, pl.ds(pl.multiple_of(j * CHUNK, CHUNK), CHUNK)],
            send_sem=hid_send.at[j],
            recv_sem=hid_recv.at[j],
            device_id={"section": 1 - s},
            device_id_type=MESH,
        )

    def each(count, act):
        def one(j, carry):
            act(j)
            return carry

        lax.fori_loop(0, count, one, 0)

    @pl.when(s == 0)
    def _():
        weights_copy.wait()
        att_copy.wait_recv()

        def project(j, carry):
            at = pl.ds(pl.multiple_of(j * CHUNK, CHUNK), CHUNK)
            both = jnp.concatenate([attention[0], attention[1]], axis=1)
            terms[j] = nn(both, weights[:, at]).astype(BF16)

            @pl.when(j >= 2)
            def _():
                term_far(j - 2).wait_send()

            term_far(j).start()
            term_own(j).start()
            return carry

        lax.fori_loop(0, chunks, project, 0)
        head_out[:, 0:wide] = attention[0]
        head_out[:, wide : 2 * wide] = attention[1]
        term_far(chunks - 2).wait_send()
        term_far(chunks - 1).wait_send()
        each(chunks, lambda j: term_own(j).wait_send())
        key_copy.wait_send()
        query_copy.wait_send()
        each(chunks_half, lambda j: hid(j).wait_recv())

    @pl.when(s == 1)
    def _():
        att_copy.start()
        heads = 2 * group
        row_col = lax.broadcasted_iota(jnp.int32, (rows, 1), 0)
        valid_col = row_col < own_len
        r = lax.broadcasted_iota(jnp.int32, (rows, rows), 0)
        t = lax.broadcasted_iota(jnp.int32, (rows, rows), 1)
        upper = jnp.where(r <= t, 1.0, 0.0)
        decay_wide[...] = jnp.zeros_like(decay_wide)
        decay_wide[0:heads, :] = jnp.where(row_lane < own_len, decay_t[...], 0.0)
        cum_t = jnp.dot(
            decay_wide[...], upper, precision=lax.Precision.HIGHEST, preferred_element_type=F32
        )
        cum = jnp.transpose(cum_t)
        gain_row[...] = gain[...].astype(F32).reshape(1, 2 * half)
        last = cum[rows - 1 : rows, :]
        left = jnp.exp(last - cum)
        for g in range(2):
            masked = jnp.where(valid_col, keys[:, g * HEAD : (g + 1) * HEAD].astype(F32), 0.0)
            keys_t[g] = jnp.transpose(masked).astype(BF16)
        for h in range(heads):
            at = slice(h * HEAD, (h + 1) * HEAD)
            col = cum[:, h : h + 1]
            row = cum_t[h : h + 1, :]
            query = queries[:, at]
            damping = jnp.where(r >= t, jnp.exp(jnp.minimum(col - row, 0.0)), 0.0)
            rest[:, at] = jnp.broadcast_to(left[:, h : h + 1], (rows, HEAD))
            damped[h] = (nn(query, keys_t[h // group]) * damping).astype(BF16)
            faded[:, at] = (query.astype(F32) * jnp.exp(col)).astype(BF16)
            totals[0, :, at] = jnp.broadcast_to(last[:, h : h + 1], (PAD, HEAD))
        totals_copy = pltpu.make_async_remote_copy(
            src_ref=totals.at[0],
            dst_ref=totals.at[1],
            send_sem=totals_sem.at[0],
            recv_sem=totals_sem.at[1],
            device_id={"ctx": partner},
            device_id_type=MESH,
        )
        totals_copy.start()
        spike_copy.wait()
        for h in range(heads):
            at = slice(h * HEAD, (h + 1) * HEAD)
            gated = spike_buf[:, at].astype(F32) * thresholds[:, at]
            gate[:, at] = jnp.where(valid_col, gated, 0.0)
        values_sum[...] = jnp.zeros_like(values_sum)
        square_sum[...] = jnp.zeros_like(square_sum)
        weights_copy.wait()
        residual_copy.wait()
        residual_recv.wait_recv()

        def collect(j, carry):
            side = j // chunks_half
            col = j - side * chunks_half
            here = pl.ds(pl.multiple_of(col * CHUNK, CHUNK), CHUNK)
            at = pl.ds(pl.multiple_of(j * CHUNK, CHUNK), CHUNK)
            term_own(j).wait_recv()
            term_far(j).wait_recv()
            summed = residuals[side, :, here].astype(F32) + (
                own_terms[j].astype(F32) + far_terms[j].astype(F32)
            )
            narrow = summed.astype(BF16)

            @pl.when(side == p)
            def _():
                hidden_buf[col] = narrow
                hidden_out[:, here] = narrow
                hid(col).start()

            rounded = narrow.astype(F32)
            square_sum[...] += jnp.sum(rounded * rounded, axis=1, keepdims=True)
            ready = (rounded * gain_row[:, at]).astype(BF16)
            values_sum[...] += nt(ready, weights[:, at])
            return carry

        lax.fori_loop(0, chunks, collect, 0)
        scale = lax.rsqrt(square_sum[...] * (1.0 / (2 * half)) + 1e-05)
        values[...] = (values_sum[...] * scale).astype(BF16)
        def swap(g):
            return pltpu.make_async_remote_copy(
                src_ref=states.at[0, g],
                dst_ref=states.at[1, g],
                send_sem=swap_send.at[g],
                recv_sem=swap_recv.at[g],
                device_id={"ctx": partner},
                device_id_type=MESH,
            )

        def onward(g):
            return pltpu.make_async_remote_copy(
                src_ref=states.at[2, g],
                dst_ref=states.at[3, g],
                send_sem=state_send.at[g],
                recv_sem=state_recv.at[g],
                device_id={"ctx": lax.rem(c + 2, n)},
                device_id_type=MESH,
            )

        def sum_of(slot, g):
            return totals[slot, 0:1, g * wide : (g + 1) * wide]

        here_later = pairs - 1 - before
        swap_out = (odd == 0) | (here_later > 0)
        swap_in = (odd == 1) | (here_later > 0)
        for g in range(2):
            for h in range(g * group, (g + 1) * group):
                at = slice(h * HEAD, (h + 1) * HEAD)
                weighted = (values[:, at].astype(F32) * rest[:, at]).astype(BF16)
                fresh[:, at] = nn(keys_t[g], weighted)
                in_group = slice((h % group) * HEAD, (h % group + 1) * HEAD)
                states[0, g, 0:HEAD, in_group] = fresh[:, at].astype(BF16)

            @pl.when(swap_out)
            def _():
                swap(g).start()

        for h in range(heads):
            at = slice(h * HEAD, (h + 1) * HEAD)
            mixed[:, at] = nn(damped[h], values[:, at])

        totals_copy.wait_recv()

        for g in range(2):
            at = slice(g * wide, (g + 1) * wide)

            @pl.when(swap_in)
            def _():
                swap(g).wait_recv()

            @pl.when(here_later > 0)
            def _():
                own = fresh[:, at]
                other = states[1, g, 0:HEAD, :].astype(F32)
                second = jnp.where(odd == 1, sum_of(0, g), sum_of(1, g))
                first_part = jnp.where(odd == 1, other, own)
                second_part = jnp.where(odd == 1, own, other)
                fresh[:, at] = first_part * jnp.exp(second) + second_part

            @pl.when(before > 0)
            def _():
                onward(g).wait_recv()
                incoming[:, at] = states[3, g, 0:HEAD, :].astype(F32)

            @pl.when(before == 0)
            def _():
                incoming[:, at] = jnp.zeros((HEAD, wide), F32)

            @pl.when(here_later > 0)
            def _():
                faded_in = incoming[:, at] * jnp.exp(sum_of(0, g) + sum_of(1, g))
                states[2, g, 0:HEAD, :] = (faded_in + fresh[:, at]).astype(BF16)
                onward(g).start()

            @pl.when(odd == 1)
            def _():
                incoming[:, at] = incoming[:, at] * jnp.exp(sum_of(1, g)) + states[
                    1, g, 0:HEAD, :
                ].astype(F32)

            for h in range(g * group, (g + 1) * group):
                at = slice(h * HEAD, (h + 1) * HEAD)
                both = mixed[:, at] + nn(faded[:, at], incoming[:, at].astype(BF16))
                scaled = both * lax.rsqrt(jnp.mean(both * both, axis=1, keepdims=True) + 1e-05)
                head_out[:, at] = (scaled * gate[:, at]).astype(BF16)

        for g in range(2):

            @pl.when(swap_out)
            def _():
                swap(g).wait_send()

            @pl.when(here_later > 0)
            def _():
                onward(g).wait_send()

        each(chunks_half, lambda j: hid(j).wait_send())
        residual_send.wait_send()
        totals_copy.wait_send()
        att_copy.wait_send()

    def along_done(k, carry):
        along(k, 0).wait_send()
        along(k, 1).wait_send()
        return carry

    @pl.when(c + 2 < n)
    def _():
        lax.fori_loop(0, before + 1, along_done, 0)

    @pl.when(odd == 0)
    def _():
        across(0, 0).wait_send()
        across(0, 1).wait_send()

    def across_done(k, carry):
        across(k, 0).wait_send()
        across(k, 1).wait_send()
        return carry

    lax.fori_loop(1, before + 1, across_done, 0)


def handed_on(a, b, a_out, b_out, a_buf, b_buf, in_sem, out_sem):
    step = a.shape[0] // PIECES

    def copies(i):
        at = slice(i * step, (i + 1) * step)
        return (
            pltpu.make_async_copy(b.at[at], b_buf.at[at], in_sem.at[0, i]),
            pltpu.make_async_copy(a.at[at], a_buf.at[at], in_sem.at[1, i]),
            pltpu.make_async_copy(b_buf.at[at], b_out.at[at], out_sem.at[0, i]),
            pltpu.make_async_copy(a_buf.at[at], a_out.at[at], out_sem.at[1, i]),
        )

    for i in range(PIECES):
        copies(i)[0].start()
        copies(i)[1].start()
    for i in range(PIECES):
        for k in range(2):
            copies(i)[k].wait()
            copies(i)[k + 2].start()
    for i in range(PIECES):
        copies(i)[2].wait()
        copies(i)[3].wait()


def fused(
    residual,
    queries,
    keys,
    window_values,
    mixing,
    norm_gain,
    log_decay,
    spike_counts,
    thresholds,
    lengths,
):
    n = lax.axis_size("ctx")
    rows, half = residual.shape
    width = queries.shape[2]
    heads = width // HEAD
    chunks = 2 * half // CHUNK
    dma = pltpu.SemaphoreType.DMA
    whole = pl.BlockSpec(memory_space=pltpu.VMEM)
    away = pl.BlockSpec(memory_space=pl.ANY)
    head_outputs, hidden = pl.pallas_call(
        functools.partial(kernel, n),
        out_shape=(
            jax.ShapeDtypeStruct((rows, width), BF16),
            jax.ShapeDtypeStruct((rows, half), BF16),
        ),
        in_specs=[
            away,
            whole,
            whole,
            whole,
            away,
            whole,
            whole,
            away,
            whole,
            pl.BlockSpec(memory_space=pltpu.SMEM),
        ],
        out_specs=(whole, whole),
        scratch_shapes=[
            pltpu.VMEM(mixing.shape[1:], BF16),
            pltpu.VMEM((rows, width), jnp.int32),
            pltpu.VMEM((n, 2 * rows, HEAD), BF16),
            pltpu.VMEM((rows, width // 2), BF16),
            pltpu.VMEM((4 * rows, HEAD), BF16),
            pltpu.VMEM((1, 4 * rows), F32),
            pltpu.VMEM((1, 4 * rows), F32),
            pltpu.VMEM((HEAD, 4 * rows), F32),
            pltpu.VMEM((2, rows, width // 2), BF16),
            pltpu.VMEM((chunks, rows, CHUNK), BF16),
            pltpu.VMEM((chunks, rows, CHUNK), BF16),
            pltpu.VMEM((chunks, rows, CHUNK), BF16),
            pltpu.VMEM((2, rows, half), BF16),
            pltpu.VMEM((chunks // 2, rows, CHUNK), BF16),
            pltpu.VMEM((rows, width), F32),
            pltpu.VMEM((rows, 1), F32),
            pltpu.VMEM((heads, rows, rows), BF16),
            pltpu.VMEM((rows, width), BF16),
            pltpu.VMEM((rows, width), F32),
            pltpu.VMEM((2, HEAD, rows), BF16),
            pltpu.VMEM((rows, width), BF16),
            pltpu.VMEM((4, 2, HEAD, width // 2), BF16),
            pltpu.VMEM((HEAD, width), F32),
            pltpu.VMEM((HEAD, width), F32),
            pltpu.VMEM((rows, width), F32),
            pltpu.VMEM((rows, width), F32),
            pltpu.VMEM((2, PAD, width), F32),
            pltpu.VMEM((1, 2 * half), F32),
            pltpu.VMEM((HEAD, rows), F32),
            dma,
            dma,
            dma((3,)),
            dma((2,)),
            dma((2,)),
            dma((n // 2, 2)),
            dma((n, 2)),
            dma((n // 2, 2)),
            dma((2,)),
            dma((chunks,)),
            dma((chunks,)),
            dma((chunks,)),
            dma((chunks,)),
            dma((chunks // 2,)),
            dma((chunks // 2,)),
            dma((2,)),
            dma((2,)),
            dma((2,)),
            dma((2,)),
            dma((2,)),
        ],
        compiler_params=pltpu.CompilerParams(
            collective_id=0, has_side_effects=True, vmem_limit_bytes=56 * 1024 * 1024
        ),
    )(
        residual,
        queries[0],
        keys[0],
        window_values,
        mixing[0],
        norm_gain,
        log_decay.T,
        spike_counts,
        thresholds.reshape(1, -1),
        lengths,
    )
    head_outputs, hidden = pl.pallas_call(
        handed_on,
        out_shape=(
            jax.ShapeDtypeStruct((rows, width), BF16),
            jax.ShapeDtypeStruct((rows, half), BF16),
        ),
        in_specs=[away, away],
        out_specs=(away, away),
        scratch_shapes=[
            pltpu.VMEM((rows, width), BF16),
            pltpu.VMEM((rows, half), BF16),
            dma((2, PIECES)),
            dma((2, PIECES)),
        ],
        compiler_params=pltpu.CompilerParams(vmem_limit_bytes=60 * 1024 * 1024),
    )(head_outputs, hidden)
    return (head_outputs[None], hidden)


def chosen(*arrays):
    residual, queries, keys = arrays[:3]
    shards = lax.axis_size("ctx")
    rows = residual.shape[0]
    fits = (
        lax.axis_size("tp") == 2
        and lax.axis_size("section") == 2
        and keys.shape[2] == 2 * HEAD
        and queries.shape[2] == 8 * HEAD
        and rows == 2 * HEAD
        and residual.shape[1] % CHUNK == 0
        and shards % 2 == 0
        and shards >= 4
        and shards * rows <= WINDOW
    )
    return fused(*arrays) if fits else body(*arrays)


def solution(mesh):
    return jax.shard_map(
        chosen,
        mesh=mesh,
        in_specs=(
            P("ctx", "tp"),
            P("section", "ctx", "tp"),
            P("section", "ctx", "tp"),
            P("ctx", "tp"),
            P("section", "tp", None),
            P(),
            P("ctx", "tp"),
            P("ctx", "tp"),
            P("tp"),
            P(),
        ),
        out_specs=(P("section", "ctx", "tp"), P("ctx", "tp")),
        check_vma=False,
    )
```

```python
import functools
import math

import jax
import jax.numpy as jnp
from jax import lax
from jax.experimental import pallas as pl
from jax.experimental.pallas import tpu as pltpu
from jax.sharding import PartitionSpec as P

HEAD = 128
WINDOW = 4096


def passed_along(x, axis, by):
    devices = lax.axis_size(axis)
    pairs = [(i, i + by) for i in range(devices) if 0 <= i + by < devices]
    return lax.ppermute(x, axis, pairs)


def entering(x, axis, join, neutral):
    place = lax.axis_index(axis)
    gathered = jax.tree.map(
        lambda a, kind: lax.all_gather(a.astype(kind), axis), x, (jnp.bfloat16, jnp.bfloat16)
    )
    state = jax.tree.map(lambda a, e: jnp.zeros_like(a) + jnp.asarray(e, a.dtype), x, neutral)

    def one(step, state):
        return join(
            state,
            jax.tree.map(
                lambda a, own: lax.dynamic_index_in_dim(a, step, 0, False).astype(own.dtype),
                gathered,
                x,
            ),
        )

    return lax.fori_loop(0, place, one, state)


def body(
    residual,
    queries,
    keys,
    window_values,
    mixing,
    norm_gain,
    log_decay,
    spike_counts,
    thresholds,
    lengths,
):
    section_index = lax.axis_index("section")
    shard_index = lax.axis_index("ctx")
    row_count = keys.shape[1]
    head_size = HEAD
    key_heads = keys.shape[2] // head_size
    query_head_rows = queries.shape[2] // head_size
    group_size = query_head_rows // key_heads
    span_blocks = WINDOW // row_count
    feature_count = mixing.shape[2]
    scale = 1.0 / math.sqrt(head_size)
    positions = jnp.arange(row_count, dtype=jnp.int32)
    valid_rows = positions < lengths[shard_index]
    own_keys = keys[0]
    earlier = [
        passed_along((own_keys, window_values), "ctx", distance + 1)
        for distance in range(span_blocks)
    ]
    key_blocks = jnp.stack([pair[0] for pair in earlier[::-1]] + [own_keys], 0)
    value_blocks = jnp.stack([pair[1] for pair in earlier[::-1]] + [window_values], 0)

    def window_layer(dummy_arg):
        query_rows = queries[0].reshape(row_count, key_heads, group_size, head_size)
        sources = shard_index - span_blocks + jnp.arange(span_blocks + 1, dtype=jnp.int32)
        block_valid = (sources[:, None] >= 0) & (
            positions[None, :] < lengths[jnp.clip(sources, 0, None)][:, None]
        )
        offsets = (span_blocks - jnp.arange(span_blocks + 1, dtype=jnp.int32)) * row_count
        base_distance = positions[:, None] - positions[None, :]

        def weight_step(carry, items):
            running, totals, best = carry
            scores = (
                jnp.einsum(
                    "rgjd,kgd->gjrk",
                    query_rows,
                    items[0].reshape(row_count, key_heads, head_size),
                    preferred_element_type=jnp.float32,
                )
                * scale
            )
            distance = base_distance + items[3]
            allowed = items[2][None, :] & (distance >= 0) & (distance < WINDOW)
            scores = jnp.where(allowed, scores, -1e30)
            new_best = jnp.maximum(best, jnp.max(scores, axis=-1))
            factor = jnp.exp(best - new_best)
            weights = jnp.where(allowed, jnp.exp(scores - new_best[..., None]), 0.0)
            blended = jnp.einsum(
                "gjrk,kgd->gjrd",
                weights.astype(jnp.bfloat16),
                items[1].reshape(row_count, key_heads, head_size),
                preferred_element_type=jnp.float32,
            )
            return (
                (
                    running * factor[..., None] + blended,
                    totals * factor + jnp.sum(weights, axis=-1),
                    new_best,
                ),
                None,
            )

        start_sums = (
            jnp.zeros((key_heads, group_size, row_count, head_size), jnp.float32),
            jnp.zeros((key_heads, group_size, row_count), jnp.float32),
            jnp.full((key_heads, group_size, row_count), -1e30, jnp.float32),
        )
        (blended, totals, unused_best), unused_sum = lax.scan(
            weight_step, start_sums, (key_blocks, value_blocks, block_valid, offsets)
        )
        attention = blended / jnp.maximum(totals, 1.0)[..., None]
        attention = attention.transpose(2, 0, 1, 3).reshape(row_count, query_head_rows * head_size)
        attention = jnp.where(valid_rows[:, None], attention, 0.0).astype(jnp.bfloat16)
        projected = jnp.dot(attention, mixing[0], preferred_element_type=jnp.float32)
        return (attention, projected)

    def window_skip(dummy_arg):
        return (
            jnp.zeros((row_count, query_head_rows * head_size), jnp.bfloat16),
            jnp.zeros((row_count, feature_count), jnp.float32),
        )

    attention, projected = lax.cond(section_index == 0, window_layer, window_skip, 0)
    share = lax.psum_scatter(
        projected.astype(jnp.bfloat16), "tp", scatter_dimension=1, tiled=True
    ).astype(jnp.float32)
    own_hidden = (share + residual.astype(jnp.float32)).astype(jnp.bfloat16)
    moved_share = passed_along(own_hidden, "section", 1)
    local_activations = jnp.where(section_index == 0, own_hidden, moved_share)
    complete_hidden_matrix = lax.all_gather(local_activations, "tp", axis=1, tiled=True)
    masked_keys = jnp.where(valid_rows[:, None], own_keys, jnp.zeros_like(own_keys)).reshape(
        row_count, key_heads, head_size
    )
    wide_keys = masked_keys.astype(jnp.float32)
    decays = log_decay * valid_rows[:, None].astype(jnp.float32)

    def linear_prepare(dummy_arg):
        wide = complete_hidden_matrix.astype(jnp.float32)
        normed = (
            wide
            * lax.rsqrt(jnp.mean(wide * wide, axis=-1, keepdims=True) + 1e-05)
            * norm_gain.astype(jnp.float32)
        ).astype(jnp.bfloat16)
        payload_vectors = lax.dot_general(
            normed, mixing[0], (((1,), (1,)), ((), ())), preferred_element_type=jnp.float32
        ).astype(jnp.bfloat16)
        cumulated = jnp.cumsum(decays, axis=0).reshape(row_count, key_heads, group_size)
        value_rows = payload_vectors.astype(jnp.float32).reshape(
            row_count, key_heads, group_size, head_size
        )
        fresh_state = jnp.einsum(
            "sgd,sgje->gdje",
            wide_keys,
            value_rows * jnp.exp(cumulated[-1] - cumulated)[..., None],
            precision=lax.Precision.HIGHEST,
        )
        return (payload_vectors, cumulated, fresh_state)

    def linear_skip(dummy_arg):
        return (
            jnp.zeros((row_count, query_head_rows * head_size), jnp.bfloat16),
            jnp.zeros((row_count, key_heads, group_size), jnp.float32),
            jnp.zeros((key_heads, head_size, group_size, head_size), jnp.float32),
        )

    payload_vectors, cumulated, fresh_state = lax.cond(
        section_index == 1, linear_prepare, linear_skip, 0
    )

    def chain(previous_entry, latter):
        return (
            previous_entry[0] + latter[0],
            previous_entry[1] * jnp.exp(latter[0])[:, None, :, None] + latter[1],
        )

    identity = (jnp.zeros((key_heads, group_size), jnp.float32), jnp.zeros_like(fresh_state))
    unused_total, incoming = entering((cumulated[-1], fresh_state), "ctx", chain, identity)

    def linear_finish(dummy_arg):
        query_narrow = queries[0].reshape(row_count, key_heads, group_size, head_size)
        query_rows = query_narrow.astype(jnp.float32)
        value_rows = payload_vectors.astype(jnp.float32).reshape(
            row_count, key_heads, group_size, head_size
        )
        inter = (
            jnp.einsum("rgjd,gdje->rgje", query_rows, incoming, precision=lax.Precision.HIGHEST)
            * jnp.exp(cumulated)[..., None]
        )
        products = jnp.einsum(
            "rgjd,sgd->gjrs", query_narrow, masked_keys, preferred_element_type=jnp.float32
        )
        ordered = cumulated.transpose(1, 2, 0)
        spread = ordered[..., :, None] - ordered[..., None, :]
        triangle = positions[:, None] >= positions[None, :]
        damping = jnp.where(triangle, jnp.exp(jnp.minimum(spread, 0.0)), 0.0)
        intra = jnp.einsum(
            "gjrs,sgje->rgje", products * damping, value_rows, precision=lax.Precision.HIGHEST
        )
        mixed = (inter + intra).reshape(row_count, query_head_rows, head_size)
        scaled = mixed * lax.rsqrt(jnp.mean(mixed * mixed, axis=-1, keepdims=True) + 1e-05)
        gating = spike_counts.astype(jnp.float32).reshape(
            row_count, query_head_rows, head_size
        ) * thresholds.reshape(query_head_rows, head_size)
        return jnp.where(
            valid_rows[:, None],
            (scaled * gating).reshape(row_count, query_head_rows * head_size),
            0.0,
        ).astype(jnp.bfloat16)

    def finish_skip(dummy_arg):
        return jnp.zeros((row_count, query_head_rows * head_size), jnp.bfloat16)

    gated = lax.cond(section_index == 1, linear_finish, finish_skip, 0)
    head_outputs = jnp.where(section_index == 0, attention, gated)[None]
    return (head_outputs, local_activations)


MESH = pl.DeviceIdType.MESH
F32 = jnp.float32
BF16 = jnp.bfloat16
CHUNK = 256
PAD = 8
PIECES = 4


def nt(a, b):
    return lax.dot_general(a, b, (((1,), (1,)), ((), ())), preferred_element_type=F32)


def nn(a, b):
    return jnp.dot(a, b, preferred_element_type=F32)


def turned(x):
    return jnp.transpose(x.astype(F32)).astype(BF16)


def kernel(
    n,
    residual,
    queries,
    keys,
    window_values,
    mixing,
    gain,
    decay_t,
    spikes,
    thresholds,
    lengths,
    head_out,
    hidden_out,
    weights,
    spike_buf,
    kv,
    moved_queries,
    stacked,
    top,
    total,
    blend,
    attention,
    terms,
    own_terms,
    far_terms,
    residuals,
    hidden_buf,
    current,
    values_sum,
    square_sum,
    damped,
    faded,
    rest,
    keys_t,
    values,
    states,
    fresh,
    incoming,
    mixed,
    gate,
    totals,
    gain_row,
    decay_wide,
    weights_sem,
    spike_sem,
    res_sem,
    first_sem,
    first_recv,
    kv_send,
    kv_recv,
    kv_forward,
    att_sem,
    term_own_send,
    term_far_send,
    term_own_recv,
    term_far_recv,
    hid_send,
    hid_recv,
    totals_sem,
    swap_send,
    swap_recv,
    state_send,
    state_recv,
):
    c = lax.axis_index("ctx")
    s = lax.axis_index("section")
    p = lax.axis_index("tp")
    odd = c % 2
    step_to = 1 - 2 * odd
    partner = c + step_to
    rows = keys.shape[0]
    half = residual.shape[1]
    chunks_half = half // CHUNK
    chunks = 2 * chunks_half
    group = 4
    wide = group * HEAD
    factor = math.log2(math.e) / math.sqrt(HEAD)

    barrier = pltpu.get_barrier_semaphore()
    pl.semaphore_signal(barrier, inc=1, device_id={"section": 1 - s}, device_id_type=MESH)
    pl.semaphore_signal(barrier, inc=1, device_id={"tp": 1 - p}, device_id_type=MESH)
    pl.semaphore_signal(
        barrier, inc=1, device_id={"section": 1 - s, "tp": 1 - p}, device_id_type=MESH
    )
    pl.semaphore_signal(barrier, inc=1, device_id={"ctx": partner}, device_id_type=MESH)
    for shift in (2, n - 2):
        pl.semaphore_signal(
            barrier, inc=1, device_id={"ctx": lax.rem(c + shift, n)}, device_id_type=MESH
        )

    weights_copy = pltpu.make_async_copy(mixing, weights, weights_sem)
    weights_copy.start()

    own_len = lengths[c]

    @pl.when(s == 0)
    def _():
        kv[0, 0:rows] = keys[:, 0:HEAD]
        value_t = turned(window_values[:, 0:HEAD])
        kv[0, rows : rows + HEAD] = value_t[:, 0:HEAD]
        kv[0, rows + HEAD : rows + 2 * HEAD] = value_t[:, HEAD : 2 * HEAD]
        for h in range(group):
            stacked[h * rows : (h + 1) * rows, :] = queries[:, h * HEAD : (h + 1) * HEAD]

    @pl.when(s == 1)
    def _():
        value_t = turned(window_values[:, HEAD : 2 * HEAD])
        kv[0, rows : rows + HEAD] = value_t[:, 0:HEAD]
        kv[0, rows + HEAD : rows + 2 * HEAD] = value_t[:, HEAD : 2 * HEAD]

    pl.semaphore_wait(barrier, 6)

    key_copy = pltpu.make_async_remote_copy(
        src_ref=keys.at[:, HEAD : 2 * HEAD],
        dst_ref=kv.at[0, 0:rows],
        send_sem=first_sem.at[0],
        recv_sem=first_recv.at[0],
        device_id={"section": 1 - s},
        device_id_type=MESH,
    )
    query_copy = pltpu.make_async_remote_copy(
        src_ref=queries.at[:, wide : 2 * wide],
        dst_ref=moved_queries,
        send_sem=first_sem.at[1],
        recv_sem=first_recv.at[1],
        device_id={"section": 1 - s},
        device_id_type=MESH,
    )
    residual_send = pltpu.make_async_remote_copy(
        src_ref=residual,
        dst_ref=residuals.at[p],
        send_sem=res_sem.at[0],
        recv_sem=res_sem.at[1],
        device_id={"tp": 1 - p},
        device_id_type=MESH,
    )
    residual_recv = pltpu.make_async_remote_copy(
        src_ref=residual,
        dst_ref=residuals.at[1 - p],
        send_sem=res_sem.at[0],
        recv_sem=res_sem.at[1],
        device_id={"tp": 1 - p},
        device_id_type=MESH,
    )
    residual_copy = pltpu.make_async_copy(residual, residuals.at[p], res_sem.at[2])
    spike_copy = pltpu.make_async_copy(spikes, spike_buf, spike_sem)

    def along(k, part):
        at = slice(part * rows, (part + 1) * rows)
        return pltpu.make_async_remote_copy(
            src_ref=kv.at[2 * k, at],
            dst_ref=kv.at[2 * k + 2, at],
            send_sem=kv_send.at[k, part],
            recv_sem=kv_recv.at[2 * k + 2, part],
            device_id={"ctx": lax.rem(c + 2, n)},
            device_id_type=MESH,
        )

    def across(k, part):
        at = slice(part * rows, (part + 1) * rows)
        return pltpu.make_async_remote_copy(
            src_ref=kv.at[2 * k, at],
            dst_ref=kv.at[2 * k + step_to, at],
            send_sem=kv_forward.at[k, part],
            recv_sem=kv_recv.at[2 * k + step_to, part],
            device_id={"ctx": partner},
            device_id_type=MESH,
        )

    def arrival(slot, part):
        at = slice(part * rows, (part + 1) * rows)
        return pltpu.make_async_remote_copy(
            src_ref=kv.at[slot, at],
            dst_ref=kv.at[slot, at],
            send_sem=kv_send.at[0, part],
            recv_sem=kv_recv.at[slot, part],
            device_id={"ctx": partner},
            device_id_type=MESH,
        )

    late_one = c // (n // 2)
    late = late_one == 1
    before = c // 2
    pairs = n // 2

    def send_own(part):
        @pl.when(c + 2 < n)
        def _():
            along(0, part).start()

        @pl.when(odd == 0)
        def _():
            across(0, part).start()

    @pl.when(s == 0)
    def _():
        key_copy.start()
        query_copy.start()

    send_own(1)

    @pl.when(s == 1)
    def _():

        @pl.when(late)
        def _():
            residual_send.start()

        residual_copy.start()
        spike_copy.start()
        key_copy.wait_recv()

    send_own(0)

    @pl.when(s == 1)
    def _():
        query_copy.wait_recv()
        for h in range(group):
            stacked[h * rows : (h + 1) * rows, :] = moved_queries[:, h * HEAD : (h + 1) * HEAD]

    def attend(slot, first):
        key_rows = kv[slot, 0:rows]
        value_t = jnp.concatenate(
            [kv[slot, rows : rows + HEAD], kv[slot, rows + HEAD : rows + 2 * HEAD]], axis=1
        )
        key_index = lax.broadcasted_iota(jnp.int32, (rows, rows), 0)
        allowed = key_index < lengths[c - slot]
        if first:
            allowed = allowed & (key_index <= lax.broadcasted_iota(jnp.int32, (rows, rows), 1))
        spans = [slice(h * rows, (h + 1) * rows) for h in range(group)]
        scores = [jnp.where(allowed, nt(key_rows, stacked[at, :]), -1e30) for at in spans]
        best = [jnp.max(x, axis=0, keepdims=True) for x in scores]
        if not first:
            best = [jnp.maximum(x, top[:, at]) for x, at in zip(best, spans)]
        parts = [jnp.exp2((x - b) * factor) for x, b in zip(scores, best)]
        blended = [nn(value_t, x.astype(BF16)) for x in parts]
        sums = [jnp.sum(x, axis=0, keepdims=True) for x in parts]
        for h, at in enumerate(spans):
            if first:
                total[:, at] = sums[h]
                blend[:, at] = blended[h]
            else:
                shrink = jnp.exp2((top[:, at] - best[h]) * factor)
                total[:, at] = total[:, at] * shrink + sums[h]
                blend[:, at] = blend[:, at] * shrink + blended[h]
            top[:, at] = best[h]

    attend(0, True)

    def attend_pair(k, carry):
        for part in (1, 0):
            arrival(2 * k, part).wait_recv()

            @pl.when(c + 2 < n)
            def _():
                along(k, part).start()

            across(k, part).start()
        attend(2 * k, False)
        behind = 2 * k - 3 + 2 * odd

        @pl.when(behind > 0)
        def _():
            arrival(behind, 1).wait_recv()
            arrival(behind, 0).wait_recv()
            attend(behind, False)

        return carry

    lax.fori_loop(1, before + 1, attend_pair, 0)
    rest_slot = 2 * before - 1 + 2 * odd

    @pl.when(rest_slot > 0)
    def _():
        arrival(rest_slot, 1).wait_recv()
        arrival(rest_slot, 0).wait_recv()
        attend(rest_slot, False)

    row_lane = lax.broadcasted_iota(jnp.int32, (1, rows), 1)
    for h in range(group):
        at = slice(h * rows, (h + 1) * rows)
        scaled = blend[:, at] / jnp.maximum(total[:, at], 1.0)
        scaled = jnp.where(row_lane < own_len, scaled, 0.0)
        attention[s, :, h * HEAD : (h + 1) * HEAD] = jnp.transpose(scaled).astype(BF16)

    att_copy = pltpu.make_async_remote_copy(
        src_ref=attention.at[1],
        dst_ref=attention.at[1],
        send_sem=att_sem.at[0],
        recv_sem=att_sem.at[1],
        device_id={"section": 1 - s},
        device_id_type=MESH,
    )

    def term_own(j):
        return pltpu.make_async_remote_copy(
            src_ref=terms.at[j],
            dst_ref=own_terms.at[j],
            send_sem=term_own_send.at[j],
            recv_sem=term_own_recv.at[j],
            device_id={"section": 1 - s},
            device_id_type=MESH,
        )

    def term_far(j):
        return pltpu.make_async_remote_copy(
            src_ref=terms.at[j],
            dst_ref=far_terms.at[j],
            send_sem=term_far_send.at[j],
            recv_sem=term_far_recv.at[j],
            device_id={"section": 1 - s, "tp": 1 - p},
            device_id_type=MESH,
        )

    def hid(j):
        return pltpu.make_async_remote_copy(
            src_ref=hidden_buf.at[j],
            dst_ref=hidden_out.at[:, pl.ds(pl.multiple_of(j * CHUNK, CHUNK), CHUNK)],
            send_sem=hid_send.at[j],
            recv_sem=hid_recv.at[j],
            device_id={"section": 1 - s},
            device_id_type=MESH,
        )

    def hid_across(j):
        return pltpu.make_async_remote_copy(
            src_ref=hidden_buf.at[j],
            dst_ref=far_terms.at[p * chunks_half + j],
            send_sem=term_far_send.at[p * chunks_half + j],
            recv_sem=term_far_recv.at[p * chunks_half + j],
            device_id={"tp": 1 - p},
            device_id_type=MESH,
        )

    def each(count, act):
        def one(j, carry):
            act(j)
            return carry

        lax.fori_loop(0, count, one, 0)

    @pl.when(s == 0)
    def _():
        weights_copy.wait()
        att_copy.wait_recv()

        def project(i, carry):
            flip = 1 - i % 2
            side = p + flip - 2 * p * flip
            j = side * chunks_half + i // 2
            at = pl.ds(pl.multiple_of(j * CHUNK, CHUNK), CHUNK)
            both = jnp.concatenate([attention[0], attention[1]], axis=1)
            terms[j] = nn(both, weights[:, at]).astype(BF16)

            @pl.when((flip == 1) | late)
            def _():
                term_far(j).start()

            @pl.when((flip == 0) | late)
            def _():
                term_own(j).start()

            return carry

        def sent(j, carry):
            @pl.when((j // chunks_half != p) | late)
            def _():
                term_far(j).wait_send()

            @pl.when((j // chunks_half == p) | late)
            def _():
                term_own(j).wait_send()

            return carry

        lax.fori_loop(0, chunks, project, 0)
        head_out[:, 0:wide] = attention[0]
        head_out[:, wide : 2 * wide] = attention[1]
        lax.fori_loop(0, chunks, sent, 0)
        key_copy.wait_send()
        query_copy.wait_send()
        each(chunks_half, lambda j: hid(j).wait_recv())

    @pl.when(s == 1)
    def _():
        att_copy.start()
        heads = 2 * group
        row_col = lax.broadcasted_iota(jnp.int32, (rows, 1), 0)
        valid_col = row_col < own_len
        r = lax.broadcasted_iota(jnp.int32, (rows, rows), 0)
        t = lax.broadcasted_iota(jnp.int32, (rows, rows), 1)
        upper = jnp.where(r <= t, 1.0, 0.0)
        decay_wide[...] = jnp.zeros_like(decay_wide)
        decay_wide[0:heads, :] = jnp.where(row_lane < own_len, decay_t[...], 0.0)
        cum_t = jnp.dot(
            decay_wide[...], upper, precision=lax.Precision.HIGHEST, preferred_element_type=F32
        )
        cum = jnp.transpose(cum_t)
        gain_row[...] = gain[...].astype(F32).reshape(1, 2 * half)
        last = cum[rows - 1 : rows, :]
        left = jnp.exp(last - cum)
        for g in range(2):
            masked = jnp.where(valid_col, keys[:, g * HEAD : (g + 1) * HEAD].astype(F32), 0.0)
            keys_t[g] = jnp.transpose(masked).astype(BF16)
        for h in range(heads):
            at = slice(h * HEAD, (h + 1) * HEAD)
            col = cum[:, h : h + 1]
            row = cum_t[h : h + 1, :]
            query = queries[:, at]
            damping = jnp.where(r >= t, jnp.exp(jnp.minimum(col - row, 0.0)), 0.0)
            rest[:, at] = jnp.broadcast_to(left[:, h : h + 1], (rows, HEAD))
            damped[h] = (nn(query, keys_t[h // group]) * damping).astype(BF16)
            faded[:, at] = (query.astype(F32) * jnp.exp(col)).astype(BF16)
            totals[0, :, at] = jnp.broadcast_to(last[:, h : h + 1], (PAD, HEAD))
        totals_copy = pltpu.make_async_remote_copy(
            src_ref=totals.at[0],
            dst_ref=totals.at[1],
            send_sem=totals_sem.at[0],
            recv_sem=totals_sem.at[1],
            device_id={"ctx": partner},
            device_id_type=MESH,
        )
        totals_copy.start()
        spike_copy.wait()
        for h in range(heads):
            at = slice(h * HEAD, (h + 1) * HEAD)
            gated = spike_buf[:, at].astype(F32) * thresholds[:, at]
            gate[:, at] = jnp.where(valid_col, gated, 0.0)
        values_sum[...] = jnp.zeros_like(values_sum)
        square_sum[...] = jnp.zeros_like(square_sum)
        weights_copy.wait()
        residual_copy.wait()

        @pl.when(late)
        def _():
            residual_recv.wait_recv()

        def collect(i, carry):
            col = late_one * (i // 2) + (1 - late_one) * (i % chunks_half)
            flip = late_one * (i % 2) + (1 - late_one) * (i // chunks_half)
            side = p + flip - 2 * p * flip
            j = side * chunks_half + col
            here = pl.ds(pl.multiple_of(col * CHUNK, CHUNK), CHUNK)
            at = pl.ds(pl.multiple_of(j * CHUNK, CHUNK), CHUNK)
            term_far(j).wait_recv()

            @pl.when((flip == 0) | late)
            def _():
                term_own(j).wait_recv()
                summed = residuals[side, :, here].astype(F32) + (
                    own_terms[j].astype(F32) + far_terms[j].astype(F32)
                )
                current[...] = summed.astype(BF16)

            @pl.when((flip == 1) & (late_one == 0))
            def _():
                current[...] = far_terms[j]

            narrow = current[...]

            @pl.when(flip == 0)
            def _():
                hidden_buf[col] = narrow
                hidden_out[:, here] = narrow

                @pl.when(late_one == 0)
                def _():
                    hid_across(col).start()

                hid(col).start()

            rounded = narrow.astype(F32)
            square_sum[...] += jnp.sum(rounded * rounded, axis=1, keepdims=True)
            ready = (rounded * gain_row[:, at]).astype(BF16)
            values_sum[...] += nt(ready, weights[:, at])
            return carry

        lax.fori_loop(0, chunks, collect, 0)
        scale = lax.rsqrt(square_sum[...] * (1.0 / (2 * half)) + 1e-05)
        values[...] = (values_sum[...] * scale).astype(BF16)
        def swap(g):
            return pltpu.make_async_remote_copy(
                src_ref=states.at[0, g],
                dst_ref=states.at[1, g],
                send_sem=swap_send.at[g],
                recv_sem=swap_recv.at[g],
                device_id={"ctx": partner},
                device_id_type=MESH,
            )

        def onward(g):
            return pltpu.make_async_remote_copy(
                src_ref=states.at[2, g],
                dst_ref=states.at[3, g],
                send_sem=state_send.at[g],
                recv_sem=state_recv.at[g],
                device_id={"ctx": lax.rem(c + 2, n)},
                device_id_type=MESH,
            )

        def sum_of(slot, g):
            return totals[slot, 0:1, g * wide : (g + 1) * wide]

        here_later = pairs - 1 - before
        swap_out = (odd == 0) | (here_later > 0)
        swap_in = (odd == 1) | (here_later > 0)
        for g in range(2):
            for h in range(g * group, (g + 1) * group):
                at = slice(h * HEAD, (h + 1) * HEAD)
                weighted = (values[:, at].astype(F32) * rest[:, at]).astype(BF16)
                fresh[:, at] = nn(keys_t[g], weighted)
                in_group = slice((h % group) * HEAD, (h % group + 1) * HEAD)
                states[0, g, 0:HEAD, in_group] = fresh[:, at].astype(BF16)

            @pl.when(swap_out)
            def _():
                swap(g).start()

        for h in range(heads):
            at = slice(h * HEAD, (h + 1) * HEAD)
            mixed[:, at] = nn(damped[h], values[:, at])

        totals_copy.wait_recv()

        for g in range(2):
            at = slice(g * wide, (g + 1) * wide)

            @pl.when(swap_in)
            def _():
                swap(g).wait_recv()

            @pl.when(here_later > 0)
            def _():
                own = fresh[:, at]
                other = states[1, g, 0:HEAD, :].astype(F32)
                second = jnp.where(odd == 1, sum_of(0, g), sum_of(1, g))
                first_part = jnp.where(odd == 1, other, own)
                second_part = jnp.where(odd == 1, own, other)
                fresh[:, at] = first_part * jnp.exp(second) + second_part

            @pl.when(before > 0)
            def _():
                onward(g).wait_recv()
                incoming[:, at] = states[3, g, 0:HEAD, :].astype(F32)

            @pl.when(before == 0)
            def _():
                incoming[:, at] = jnp.zeros((HEAD, wide), F32)

            @pl.when(here_later > 0)
            def _():
                faded_in = incoming[:, at] * jnp.exp(sum_of(0, g) + sum_of(1, g))
                states[2, g, 0:HEAD, :] = (faded_in + fresh[:, at]).astype(BF16)
                onward(g).start()

            @pl.when(odd == 1)
            def _():
                incoming[:, at] = incoming[:, at] * jnp.exp(sum_of(1, g)) + states[
                    1, g, 0:HEAD, :
                ].astype(F32)

            for h in range(g * group, (g + 1) * group):
                at = slice(h * HEAD, (h + 1) * HEAD)
                both = mixed[:, at] + nn(faded[:, at], incoming[:, at].astype(BF16))
                scaled = both * lax.rsqrt(jnp.mean(both * both, axis=1, keepdims=True) + 1e-05)
                head_out[:, at] = (scaled * gate[:, at]).astype(BF16)

        for g in range(2):

            @pl.when(swap_out)
            def _():
                swap(g).wait_send()

            @pl.when(here_later > 0)
            def _():
                onward(g).wait_send()

        each(chunks_half, lambda j: hid(j).wait_send())

        @pl.when(late)
        def _():
            residual_send.wait_send()

        @pl.when(late_one == 0)
        def _():
            each(chunks_half, lambda j: hid_across(j).wait_send())

        totals_copy.wait_send()
        att_copy.wait_send()

    def along_done(k, carry):
        along(k, 0).wait_send()
        along(k, 1).wait_send()
        return carry

    @pl.when(c + 2 < n)
    def _():
        lax.fori_loop(0, before + 1, along_done, 0)

    @pl.when(odd == 0)
    def _():
        across(0, 0).wait_send()
        across(0, 1).wait_send()

    def across_done(k, carry):
        across(k, 0).wait_send()
        across(k, 1).wait_send()
        return carry

    lax.fori_loop(1, before + 1, across_done, 0)


def handed_on(a, b, a_out, b_out, a_buf, b_buf, in_sem, out_sem):
    step = a.shape[0] // PIECES

    def copies(i):
        at = slice(i * step, (i + 1) * step)
        return (
            pltpu.make_async_copy(b.at[at], b_buf.at[at], in_sem.at[0, i]),
            pltpu.make_async_copy(a.at[at], a_buf.at[at], in_sem.at[1, i]),
            pltpu.make_async_copy(b_buf.at[at], b_out.at[at], out_sem.at[0, i]),
            pltpu.make_async_copy(a_buf.at[at], a_out.at[at], out_sem.at[1, i]),
        )

    for i in range(PIECES):
        copies(i)[0].start()
        copies(i)[1].start()
    for i in range(PIECES):
        for k in range(2):
            copies(i)[k].wait()
            copies(i)[k + 2].start()
    for i in range(PIECES):
        copies(i)[2].wait()
        copies(i)[3].wait()


def fused(
    residual,
    queries,
    keys,
    window_values,
    mixing,
    norm_gain,
    log_decay,
    spike_counts,
    thresholds,
    lengths,
):
    n = lax.axis_size("ctx")
    rows, half = residual.shape
    width = queries.shape[2]
    heads = width // HEAD
    chunks = 2 * half // CHUNK
    dma = pltpu.SemaphoreType.DMA
    whole = pl.BlockSpec(memory_space=pltpu.VMEM)
    away = pl.BlockSpec(memory_space=pl.ANY)
    head_outputs, hidden = pl.pallas_call(
        functools.partial(kernel, n),
        out_shape=(
            jax.ShapeDtypeStruct((rows, width), BF16),
            jax.ShapeDtypeStruct((rows, half), BF16),
        ),
        in_specs=[
            away,
            whole,
            whole,
            whole,
            away,
            whole,
            whole,
            away,
            whole,
            pl.BlockSpec(memory_space=pltpu.SMEM),
        ],
        out_specs=(whole, whole),
        scratch_shapes=[
            pltpu.VMEM(mixing.shape[1:], BF16),
            pltpu.VMEM((rows, width), jnp.int32),
            pltpu.VMEM((n, 2 * rows, HEAD), BF16),
            pltpu.VMEM((rows, width // 2), BF16),
            pltpu.VMEM((4 * rows, HEAD), BF16),
            pltpu.VMEM((1, 4 * rows), F32),
            pltpu.VMEM((1, 4 * rows), F32),
            pltpu.VMEM((HEAD, 4 * rows), F32),
            pltpu.VMEM((2, rows, width // 2), BF16),
            pltpu.VMEM((chunks, rows, CHUNK), BF16),
            pltpu.VMEM((chunks, rows, CHUNK), BF16),
            pltpu.VMEM((chunks, rows, CHUNK), BF16),
            pltpu.VMEM((2, rows, half), BF16),
            pltpu.VMEM((chunks // 2, rows, CHUNK), BF16),
            pltpu.VMEM((rows, CHUNK), BF16),
            pltpu.VMEM((rows, width), F32),
            pltpu.VMEM((rows, 1), F32),
            pltpu.VMEM((heads, rows, rows), BF16),
            pltpu.VMEM((rows, width), BF16),
            pltpu.VMEM((rows, width), F32),
            pltpu.VMEM((2, HEAD, rows), BF16),
            pltpu.VMEM((rows, width), BF16),
            pltpu.VMEM((4, 2, HEAD, width // 2), BF16),
            pltpu.VMEM((HEAD, width), F32),
            pltpu.VMEM((HEAD, width), F32),
            pltpu.VMEM((rows, width), F32),
            pltpu.VMEM((rows, width), F32),
            pltpu.VMEM((2, PAD, width), F32),
            pltpu.VMEM((1, 2 * half), F32),
            pltpu.VMEM((HEAD, rows), F32),
            dma,
            dma,
            dma((3,)),
            dma((2,)),
            dma((2,)),
            dma((n // 2, 2)),
            dma((n, 2)),
            dma((n // 2, 2)),
            dma((2,)),
            dma((chunks,)),
            dma((chunks,)),
            dma((chunks,)),
            dma((chunks,)),
            dma((chunks // 2,)),
            dma((chunks // 2,)),
            dma((2,)),
            dma((2,)),
            dma((2,)),
            dma((2,)),
            dma((2,)),
        ],
        compiler_params=pltpu.CompilerParams(
            collective_id=0, has_side_effects=True, vmem_limit_bytes=56 * 1024 * 1024
        ),
    )(
        residual,
        queries[0],
        keys[0],
        window_values,
        mixing[0],
        norm_gain,
        log_decay.T,
        spike_counts,
        thresholds.reshape(1, -1),
        lengths,
    )
    head_outputs, hidden = pl.pallas_call(
        handed_on,
        out_shape=(
            jax.ShapeDtypeStruct((rows, width), BF16),
            jax.ShapeDtypeStruct((rows, half), BF16),
        ),
        in_specs=[away, away],
        out_specs=(away, away),
        scratch_shapes=[
            pltpu.VMEM((rows, width), BF16),
            pltpu.VMEM((rows, half), BF16),
            dma((2, PIECES)),
            dma((2, PIECES)),
        ],
        compiler_params=pltpu.CompilerParams(vmem_limit_bytes=60 * 1024 * 1024),
    )(head_outputs, hidden)
    return (head_outputs[None], hidden)


def chosen(*arrays):
    residual, queries, keys = arrays[:3]
    shards = lax.axis_size("ctx")
    rows = residual.shape[0]
    fits = (
        lax.axis_size("tp") == 2
        and lax.axis_size("section") == 2
        and keys.shape[2] == 2 * HEAD
        and queries.shape[2] == 8 * HEAD
        and rows == 2 * HEAD
        and residual.shape[1] % CHUNK == 0
        and shards % 2 == 0
        and shards >= 4
        and shards * rows <= WINDOW
    )
    return fused(*arrays) if fits else body(*arrays)


def solution(mesh):
    return jax.shard_map(
        chosen,
        mesh=mesh,
        in_specs=(
            P("ctx", "tp"),
            P("section", "ctx", "tp"),
            P("section", "ctx", "tp"),
            P("ctx", "tp"),
            P("section", "tp", None),
            P(),
            P("ctx", "tp"),
            P("ctx", "tp"),
            P("tp"),
            P(),
        ),
        out_specs=(P("section", "ctx", "tp"), P("ctx", "tp")),
        check_vma=False,
    )
```
